32 devices in a mesh: seq: 8 (over z, y), ctx: 4 (over x, core).
Axes of the slice: x: 2, y: 2, z: 4, core: 2. Of those that a mesh axis runs over, the one named last changes fastest.
Arguments:
- tokens: bfloat16 [64, 512, 1024], P('seq', 'ctx'), may hold values from -6 to 6
- segment_ids: int32 [64, 512], P('seq'), may hold values from 0 to 2, as said below
- project_weight: bfloat16 [1024, 3072], P(('seq', 'ctx')), may hold values from -0.25 to 0.25
- query_bias: bfloat16 [1024], P(('seq', 'ctx')), may hold values from -3 to 3
- value_bias: bfloat16 [1024], P(('seq', 'ctx')), may hold values from -3 to 3
- output_weight: bfloat16 [1024, 1024], P(('seq', 'ctx')), may hold values from -0.5 to 0.5
- output_bias: bfloat16 [1024], P(('seq', 'ctx')), may hold values from -2 to 2
- first_gain: bfloat16 [1024], P(('seq', 'ctx')), may hold values from 0.5 to 1.5
- first_shift: bfloat16 [1024], P(('seq', 'ctx')), may hold values from -2 to 2
- expand_weight: bfloat16 [1024, 4096], P(('seq', 'ctx')), may hold values from -0.1875 to 0.1875
- expand_bias: bfloat16 [4096], P(('seq', 'ctx')), may hold values from -3 to 3
- reduce_weight: bfloat16 [4096, 1024], P(('seq', 'ctx')), may hold values from -0.09375 to 0.09375
- reduce_bias: bfloat16 [1024], P(('seq', 'ctx')), may hold values from -2 to 2
- second_gain: bfloat16 [1024], P(('seq', 'ctx')), may hold values from 0.5 to 1.5
- second_shift: bfloat16 [1024], P(('seq', 'ctx')), may hold values from -2 to 2
- grad_out: bfloat16 [64, 512, 1024], P('seq', 'ctx'), may hold values from -6 to 6
Outputs:
- layer_out: bfloat16 [64, 512, 1024], P('seq', 'ctx')
- grad_tokens: float32 [64, 512, 1024], P('seq', 'ctx')
- project_grad: float32 [1024, 3072], P(('seq', 'ctx'))
- query_bias_grad: float32 [1024], P(('seq', 'ctx'))
- value_bias_grad: float32 [1024], P(('seq', 'ctx'))
- output_grad: float32 [1024, 1024], P(('seq', 'ctx'))
- output_bias_grad: float32 [1024], P(('seq', 'ctx'))
- first_gain_grad: float32 [1024], P(('seq', 'ctx'))
- first_shift_grad: float32 [1024], P(('seq', 'ctx'))
- expand_grad: float32 [1024, 4096], P(('seq', 'ctx'))
- expand_bias_grad: float32 [4096], P(('seq', 'ctx'))
- reduce_grad: float32 [4096, 1024], P(('seq', 'ctx'))
- reduce_bias_grad: float32 [1024], P(('seq', 'ctx'))
- second_gain_grad: float32 [1024], P(('seq', 'ctx'))
- second_shift_grad: float32 [1024], P(('seq', 'ctx'))
The draws below stay inside these ranges and needn't reach their ends.
Inputs may be any that keep to these rules, and one draw needn't show every extreme that they name: `segment_ids`: within each sequence the ids start at 0 and never fall; equal ids mark one document's piece, and every piece has 64 tokens or more. In each aligned block of 8 sequences one holds a single document; the others hold three.
All inputs are finite; a program needn't handle non-finite values.
Results may differ from the reference program's by a relative error of at most 0.014.
The reference program's roundings to bfloat16 on the way count: a program that leaves them out, or rounds other values in their place, can miss the bound.
Values may be sent and summed in bfloat16 or wider, within the bound.
No kernel may reach another device: no remote copies, remote signals or barrier semaphores. Data moves between devices by JAX's collectives and lax.ppermute only.
A program may use at most 320 MiB of HBM per device.

```python
import math
import jax
import jax.numpy as jnp
from jax import lax

D = 1024
HEADS = 16
HEAD_DIM = 64
FF = 4096
LEN = 512
SEQ_DEV = 8
SEQS = 64


def draw_segment_ids(key, part):
    key = jax.random.fold_in(key, 7)
    first_key, second_key, whole_key = jax.random.split(key, 3)
    least = LEN // 8
    first_cut = jax.random.randint(first_key, (SEQS, 1), least, LEN // 2)
    second_cut = first_cut + jax.random.randint(second_key, (SEQS, 1), least, LEN // 2 - least + 1)
    chosen = jax.random.randint(whole_key, (SEQS // SEQ_DEV,), 0, SEQ_DEV)
    sequence = jnp.arange(SEQS, dtype=jnp.int32)
    single = (sequence % SEQ_DEV == chosen[sequence // SEQ_DEV])[:, None]
    first_cut = jnp.where(single, LEN, first_cut)
    second_cut = jnp.where(single, LEN, second_cut)
    places = jnp.arange(LEN, dtype=jnp.int32)[None, :]
    return (places >= first_cut).astype(jnp.int32) + (places >= second_cut).astype(jnp.int32)


def levels(key, shape, shards, low, top_value):
    loudness = 1.0
    for position, shards_of in shards:
        steps = jax.random.uniform(jax.random.fold_in(jax.random.fold_in(key, 6), position), (shards_of,), jnp.float32, low / len(shards), top_value / len(shards))
        loudness = loudness * jnp.repeat(jnp.exp(steps), shape[position] // shards_of).reshape((-1,) + (1,) * (len(shape) - 1 - position))
    return loudness


def normal_values(stream_key, dims, deviation, bound, pieces=(), held_as=jnp.bfloat16):
    entries = deviation * jax.random.normal(stream_key, dims, jnp.float32)
    if pieces:
        entries = entries * levels(stream_key, dims, pieces, -0.22, 0.18)
    return jnp.clip(entries, -bound, bound).astype(held_as)


def setup_inputs(seed: int = 0) -> dict:
    arg_keys = jax.random.split(jax.random.key(seed), 17)
    return {
        "tokens": normal_values(arg_keys[0], (SEQS, LEN, D), 1.0, 6.0, ((0, 8), (1, 4))),
        "segment_ids": draw_segment_ids(jax.random.fold_in(arg_keys[16], 71), 0),
        "project_weight": normal_values(arg_keys[2], (D, 3 * D), (D // 2) ** -0.5, 0.25, ((0, 32),)),
        "query_bias": normal_values(arg_keys[3], (D,), 0.5, 3.0, ((0, 32),)),
        "value_bias": normal_values(arg_keys[4], (D,), 0.5, 3.0, ((0, 32),)),
        "output_weight": normal_values(arg_keys[5], (D, D), (D // 8) ** -0.5, 0.5, ((0, 32),)),
        "output_bias": normal_values(arg_keys[6], (D,), 0.3, 2.0, ((0, 32),)),
        "first_gain": jnp.clip(1.0 + 0.1 * jax.random.normal(arg_keys[7], (D,), jnp.float32), 0.5, 1.5).astype(jnp.bfloat16),
        "first_shift": normal_values(arg_keys[8], (D,), 0.3, 2.0, ((0, 32),)),
        "expand_weight": normal_values(arg_keys[9], (D, FF), D ** -0.5, 0.1875, ((0, 32),)),
        "expand_bias": normal_values(arg_keys[10], (FF,), 0.5, 3.0, ((0, 32),)),
        "reduce_weight": normal_values(arg_keys[11], (FF, D), FF ** -0.5, 0.09375, ((0, 32),)),
        "reduce_bias": normal_values(arg_keys[12], (D,), 0.3, 2.0, ((0, 32),)),
        "second_gain": jnp.clip(1.0 + 0.1 * jax.random.normal(arg_keys[13], (D,), jnp.float32), 0.5, 1.5).astype(jnp.bfloat16),
        "second_shift": normal_values(arg_keys[14], (D,), 0.3, 2.0, ((0, 32),)),
        "grad_out": normal_values(arg_keys[15], (SEQS, LEN, D), 1.0, 6.0, ((0, 8), (1, 4))),
    }


@jax.custom_vjp
def low(v):
    return lax.optimization_barrier(v.astype(jnp.bfloat16)).astype(jnp.float32)

@jax.custom_vjp
def low_back(v):
    return v

def low_keep(v):
    return (low(v), None)

def low_pass(kept, grad):
    return (grad,)

def back_keep(v):
    return (v, None)

def back_low(kept, grad):
    return (low(grad),)
low.defvjp(low_keep, low_pass)
low_back.defvjp(back_keep, back_low)

def matmul(left, right):
    return jnp.dot(left, right, precision=lax.Precision.HIGHEST, preferred_element_type=jnp.float32)

def normalize(values, gain, shift):
    center = values - lax.optimization_barrier(jnp.mean(values, axis=-1, keepdims=True))
    spread = lax.optimization_barrier(jnp.mean(center * center, axis=-1, keepdims=True))
    return center * lax.rsqrt(spread + 1e-05) * gain + shift

def layer(inputs, allowed, params):
    project_weight, query_bias, value_bias, output_weight, output_bias, first_gain, first_shift, expand_weight, expand_bias, reduce_weight, reduce_bias, second_gain, second_shift = params
    groups = inputs.shape[0]
    rows = inputs.reshape(groups * LEN, D)
    bias_all = jnp.concatenate([query_bias, jnp.zeros((D,), jnp.float32), value_bias])
    project = low(low_back(matmul(rows, project_weight) + bias_all))
    project = project.reshape(groups, LEN, 3, HEADS, HEAD_DIM)
    queries = project[:, :, 0]
    keys_all = project[:, :, 1]
    values_all = project[:, :, 2]
    scores = jnp.einsum('gqhd,gkhd->ghqk', queries, keys_all, precision=lax.Precision.HIGHEST) * HEAD_DIM ** (-0.5)
    scores = low_back(scores)
    scores = jnp.where(allowed[:, None], scores, -1e+30)
    top = lax.optimization_barrier(jnp.max(scores, axis=-1, keepdims=True))
    expo = jnp.exp(scores - top)
    weights = low(expo / lax.optimization_barrier(jnp.sum(expo, axis=-1, keepdims=True)))
    mixed = jnp.einsum('ghqk,gkhd->gqhd', weights, values_all, precision=lax.Precision.HIGHEST)
    mixed = low(low_back(mixed.reshape(groups * LEN, D)))
    attended = low_back(matmul(mixed, output_weight) + output_bias)
    first = normalize(rows + attended, first_gain, first_shift)
    expanded = low_back(matmul(low(first), expand_weight) + expand_bias)
    activated = low(jax.nn.gelu(expanded, approximate=True))
    reduced = low_back(matmul(activated, reduce_weight) + reduce_bias)
    return normalize(first + reduced, second_gain, second_shift).reshape(groups, LEN, D)

def reference(tokens, segment_ids, project_weight, query_bias, value_bias, output_weight, output_bias, first_gain, first_shift, expand_weight, expand_bias, reduce_weight, reduce_bias, second_gain, second_shift, grad_out):
    params = tuple((entry.astype(jnp.float32) for entry in (project_weight, query_bias, value_bias, output_weight, output_bias, first_gain, first_shift, expand_weight, expand_bias, reduce_weight, reduce_bias, second_gain, second_shift)))
    per_block = math.gcd(SEQS, max(1, 4096 // LEN))
    blocks = SEQS // per_block
    inputs = tokens.reshape(blocks, per_block, LEN, D)
    segments = segment_ids.reshape(blocks, per_block, LEN)
    cotangent = grad_out.reshape(blocks, per_block, LEN, D)
    starting = jax.tree.map(jnp.zeros_like, params)

    def advance(totals, batch_item):
        block_in, block_seg, block_cot = batch_item
        allowed = block_seg[:, :, None] == block_seg[:, None, :]

        def forward(values, weights):
            return layer(values, allowed, weights)
        result, pullback = jax.vjp(forward, block_in.astype(jnp.float32), params)
        grad_in, grad_params = pullback(block_cot.astype(jnp.float32))
        return (jax.tree.map(jnp.add, totals, grad_params), (result, grad_in))
    totals, (results, grad_inputs) = lax.scan(advance, starting, (inputs, segments, cotangent))
    grad_project, grad_query, grad_value, grad_output, grad_outbias, grad_gain_one, grad_shift_one, grad_expand, grad_expbias, grad_reduce, grad_redbias, grad_gain_two, grad_shift_two = totals
    layer_out = results.reshape(SEQS, LEN, D).astype(jnp.bfloat16)
    grad_tokens = grad_inputs.reshape(SEQS, LEN, D).astype(jnp.float32)
    return (layer_out, grad_tokens, grad_project, grad_query, grad_value, grad_output, grad_outbias, grad_gain_one, grad_shift_one, grad_expand, grad_expbias, grad_reduce, grad_redbias, grad_gain_two, grad_shift_two)
```

```python
import functools

import jax
import jax.numpy as jnp
from jax import lax
from jax.experimental import pallas as pl
from jax.experimental.pallas import tpu as pltpu
from jax.sharding import Mesh
from jax.sharding import PartitionSpec as P

HEADS = 16
HEAD_DIM = 64
CHUNKS = 4
MIB = 1 << 20
CHIPS = ("z", "y", "x")
SEQ = ("z", "y")
CTX = ("x", "c")
ALL = ("z", "y", "x", "c")
F32 = jnp.float32
BF16 = jnp.bfloat16


def dot(left, right, contract=(1, 0)):
    return lax.dot_general(
        left, right, (((contract[0],), (contract[1],)), ((), ())), preferred_element_type=F32
    )


def resident(shape):
    return pl.BlockSpec(shape, lambda i: (0,) * len(shape), pipeline_mode=pl.Buffered(1))


def by_row(shape):
    return pl.BlockSpec(shape, lambda i: (i,) + (0,) * (len(shape) - 1))


def softmax_down(scores, allowed):
    scores = jnp.where(allowed, scores, -1e30)
    top = jnp.max(scores, axis=0, keepdims=True)
    expo = jnp.exp(scores - top)
    total = jnp.sum(expo, axis=0, keepdims=True)
    return expo * (1.0 / total)


def head_lanes(width, head):
    lane = lax.broadcasted_iota(jnp.int32, (1, width), 1)
    return (lane // HEAD_DIM == head).astype(F32)


def attend_kernel(t0, t1, t2, t3, weight, bias, seg_key, seg_query, m0, m1, m2, m3, kept, saved):
    part = t0.shape[1]
    rows = jnp.concatenate([t[0] for t in (t0, t1, t2, t3)], axis=0)
    kept[0] = rows
    project = dot(rows, weight[...]) + bias[...]
    saved[0] = project.astype(BF16)
    width = project.shape[1] // 3
    queries = (project[:, :width].astype(BF16).astype(F32) * HEAD_DIM**-0.5).astype(BF16)
    keys = project[:, width : 2 * width].astype(BF16).astype(F32)
    values_t = jnp.transpose(project[:, 2 * width :]).astype(BF16)
    allowed = seg_key[0] == seg_query[0]
    mixed = []
    for head in range(width // HEAD_DIM):
        own_keys = (keys * head_lanes(width, head)).astype(BF16)
        chances = softmax_down(dot(own_keys, queries, (1, 1)), allowed)
        own_values = values_t[head * HEAD_DIM : (head + 1) * HEAD_DIM]
        mixed.append(dot(own_values, chances.astype(BF16)))
    mixed = jnp.transpose(jnp.concatenate(mixed, axis=0)).astype(BF16)
    for index, out in enumerate((m0, m1, m2, m3)):
        out[0] = mixed[index * part : (index + 1) * part]


def attend(tokens, weight, bias, seg_key, seg_query):
    count, part, depth = tokens[0].shape
    wide = weight.shape[1]
    length = 4 * part
    return pl.pallas_call(
        attend_kernel,
        grid=(count,),
        in_specs=[by_row((1, part, depth))] * 4
        + [
            resident((depth, wide)),
            resident((1, wide)),
            by_row((1, length, 1)),
            by_row((1, 1, length)),
        ],
        out_specs=[by_row((1, part, wide // 3))] * 4
        + [by_row((1, length, depth)), by_row((1, length, wide))],
        out_shape=[jax.ShapeDtypeStruct((count, part, wide // 3), BF16)] * 4
        + [
            jax.ShapeDtypeStruct((count, length, depth), BF16),
            jax.ShapeDtypeStruct((count, length, wide), BF16),
        ],
        compiler_params=pltpu.CompilerParams(vmem_limit_bytes=40 * MIB),
        cost_estimate=pl.CostEstimate(
            flops=count * length * wide * (2 * depth + 16 * length // 3),
            bytes_accessed=count * length * (depth + 2 * wide) * 2,
            transcendentals=count * length * length * wide // (3 * HEAD_DIM),
        ),
        name="attend_forward",
    )(*tokens, weight, bias, seg_key, seg_query)


def attend_back_kernel(
    saved, g0, g1, g2, g3, weight, seg_key, seg_query, grad_project, r0, r1, r2, r3, sums
):
    part = g0.shape[1]
    width = saved.shape[2] // 3
    factor = HEAD_DIM**-0.5
    queries = (saved[0, :, :width].astype(F32) * factor).astype(BF16)
    keys = saved[0, :, width : 2 * width].astype(F32)
    values = saved[0, :, 2 * width :].astype(F32)
    keys_t = jnp.transpose(keys * factor).astype(BF16)
    grad_mixed = jnp.concatenate([g[0] for g in (g0, g1, g2, g3)], axis=0)
    allowed = seg_key[0] == seg_query[0]
    grad_queries = []
    grad_keys = None
    grad_values = None
    for head in range(width // HEAD_DIM):
        lanes = head_lanes(width, head)
        chances = softmax_down(
            dot((keys * lanes).astype(BF16), queries, (1, 1)), allowed
        )
        grad_weights = dot((values * lanes).astype(BF16), grad_mixed, (1, 1))
        inner = jnp.sum(chances * grad_weights, axis=0, keepdims=True)
        grad_scores = (chances * (grad_weights - inner)).astype(BF16)
        grad_queries.append(dot(keys_t[head * HEAD_DIM : (head + 1) * HEAD_DIM], grad_scores))
        keys_term = dot(grad_scores, queries)
        values_term = dot(chances.astype(BF16), grad_mixed)
        if head == 0:
            grad_keys, grad_values = keys_term, values_term
        else:
            here = lanes > 0.5
            grad_keys = jnp.where(here, keys_term, grad_keys)
            grad_values = jnp.where(here, values_term, grad_values)
    grad_queries = jnp.transpose(jnp.concatenate(grad_queries, axis=0))
    whole = jnp.concatenate(
        [grad_queries.astype(BF16), grad_keys.astype(BF16), grad_values.astype(BF16)], axis=1
    )
    grad_project[0] = whole
    sums[0] = jnp.sum(whole.astype(F32), axis=0, keepdims=True)
    for index, out in enumerate((r0, r1, r2, r3)):
        out[0] = dot(whole[index * part : (index + 1) * part], weight[...], (1, 1)).astype(
            out.dtype
        )


def attend_back(saved, grads, weight, seg_key, seg_query):
    count, part, width = grads[0].shape
    depth, wide = weight.shape
    length = 4 * part
    return pl.pallas_call(
        attend_back_kernel,
        grid=(count,),
        in_specs=[by_row((1, length, wide))]
        + [by_row((1, part, width))] * 4
        + [
            resident((depth, wide)),
            by_row((1, length, 1)),
            by_row((1, 1, length)),
        ],
        out_specs=[by_row((1, length, wide))]
        + [by_row((1, part, depth))] * 4
        + [by_row((1, 1, wide))],
        out_shape=[jax.ShapeDtypeStruct((count, length, wide), BF16)]
        + [jax.ShapeDtypeStruct((count, part, depth), t) for t in (F32, BF16, F32, BF16)]
        + [jax.ShapeDtypeStruct((count, 1, wide), F32)],
        compiler_params=pltpu.CompilerParams(vmem_limit_bytes=48 * MIB),
        cost_estimate=pl.CostEstimate(
            flops=count * length * wide * (2 * depth + 40 * length // 3),
            bytes_accessed=count * length * (3 * depth + 3 * wide) * 2,
            transcendentals=count * length * length * wide // (3 * HEAD_DIM),
        ),
        name="attend_backward",
    )(saved, *grads, weight, seg_key, seg_query)


def pick(first_half, own, other):
    return jnp.where(first_half, own, other)


def feed_kernel(steps, own, other, expand, bias, reduce, act, slope, own_out, other_out):
    step = pl.program_id(0)
    rows = pick(step < steps, own[...], other[...])
    hidden = expand.shape[1]
    piece = hidden // 4
    for index in range(4):
        at = slice(index * piece, (index + 1) * piece)
        inside = dot(rows, expand[:, at]) + bias[:, at]
        square = inside * inside
        curve = jnp.tanh(0.7978845608028654 * inside * (1.0 + 0.044715 * square))
        half = 0.5 * (1.0 + curve)
        act[:, at] = (inside * half).astype(BF16)
        slope[:, at] = (
            half
            + 0.5
            * inside
            * (1.0 - curve * curve)
            * (0.7978845608028654 * (1.0 + 3 * 0.044715 * square))
        ).astype(BF16)
    total = dot(act[...], reduce[...])

    @pl.when(step < steps)
    def _():
        own_out[...] = total

    @pl.when(step >= steps)
    def _():
        other_out[...] = total.astype(BF16)


def halves(steps, shape):
    return [
        pl.BlockSpec(shape, lambda i: (jnp.minimum(i, steps - 1), 0)),
        pl.BlockSpec(shape, lambda i: (jnp.maximum(i - steps, 0), 0)),
    ]


def feed(own, other, expand, bias, reduce):
    rows, depth = own.shape
    hidden = expand.shape[1]
    block = 256
    steps = rows // block
    return pl.pallas_call(
        functools.partial(feed_kernel, steps),
        grid=(2 * steps,),
        in_specs=halves(steps, (block, depth))
        + [resident((depth, hidden)), resident((1, hidden)), resident((hidden, depth))],
        out_specs=[by_row((block, hidden))] * 2 + halves(steps, (block, depth)),
        out_shape=[jax.ShapeDtypeStruct((2 * rows, hidden), BF16)] * 2
        + [
            jax.ShapeDtypeStruct((rows, depth), F32),
            jax.ShapeDtypeStruct((rows, depth), BF16),
        ],
        compiler_params=pltpu.CompilerParams(vmem_limit_bytes=48 * MIB),
        cost_estimate=pl.CostEstimate(
            flops=8 * rows * depth * hidden,
            bytes_accessed=4 * rows * (2 * hidden + 3 * depth),
            transcendentals=2 * rows * hidden,
        ),
        name="feed_forward",
    )(own, other, expand, bias, reduce)


def feed_back_kernel(
    steps,
    own_grad,
    other_grad,
    own_rows,
    other_rows,
    act,
    slope,
    expand,
    reduce,
    expand_grad,
    reduce_grad,
    bias_grad,
    own_out,
    other_out,
    expand_sum,
    reduce_sum,
):
    step = pl.program_id(0)
    grad = pick(step < steps, own_grad[...], other_grad[...])
    rows = pick(step < steps, own_rows[...], other_rows[...])
    grad_act = dot(grad, reduce[...], (1, 1))
    grad_inside = (grad_act * slope[...].astype(F32)).astype(BF16)
    bias_part = jnp.sum(grad_inside.astype(F32), axis=0, keepdims=True)
    expand_part = dot(rows, grad_inside, (0, 0))
    reduce_part = dot(act[...], grad, (0, 0))

    @pl.when(step == 0)
    def _():
        bias_grad[...] = bias_part
        expand_sum[...] = expand_part
        reduce_sum[...] = reduce_part

    @pl.when(step > 0)
    def _():
        bias_grad[...] += bias_part
        expand_sum[...] += expand_part
        reduce_sum[...] += reduce_part

    total = dot(grad_inside, expand[...], (1, 1))

    @pl.when(step < steps)
    def _():
        own_out[...] = total

    @pl.when(step >= steps)
    def _():
        other_out[...] = total.astype(BF16)

    @pl.when(step == 2 * steps - 1)
    def _():
        expand_grad[...] = expand_sum[...].astype(BF16)
        reduce_grad[...] = reduce_sum[...].astype(BF16)


def feed_back(own_grad, other_grad, own_rows, other_rows, act, slope, expand, reduce):
    rows, depth = own_grad.shape
    hidden = expand.shape[1]
    block = 256
    steps = rows // block
    return pl.pallas_call(
        functools.partial(feed_back_kernel, steps),
        grid=(2 * steps,),
        in_specs=halves(steps, (block, depth))
        + halves(steps, (block, depth))
        + [by_row((block, hidden))] * 2
        + [resident((depth, hidden)), resident((hidden, depth))],
        out_specs=[
            resident((depth, hidden)),
            resident((hidden, depth)),
            resident((1, hidden)),
        ]
        + halves(steps, (block, depth)),
        out_shape=[
            jax.ShapeDtypeStruct((depth, hidden), BF16),
            jax.ShapeDtypeStruct((hidden, depth), BF16),
            jax.ShapeDtypeStruct((1, hidden), F32),
            jax.ShapeDtypeStruct((rows, depth), F32),
            jax.ShapeDtypeStruct((rows, depth), BF16),
        ],
        scratch_shapes=[
            pltpu.VMEM((depth, hidden), F32),
            pltpu.VMEM((hidden, depth), F32),
        ],
        compiler_params=pltpu.CompilerParams(vmem_limit_bytes=60 * MIB),
        cost_estimate=pl.CostEstimate(
            flops=16 * rows * depth * hidden,
            bytes_accessed=4 * rows * (2 * hidden + 5 * depth) + 8 * depth * hidden,
            transcendentals=0,
        ),
        name="feed_backward",
    )(own_grad, other_grad, own_rows, other_rows, act, slope, expand, reduce)


def normalize(values):
    center = values - jnp.mean(values, axis=-1, keepdims=True)
    inverse = lax.rsqrt(jnp.mean(center * center, axis=-1, keepdims=True) + 1e-05)
    return (center * inverse, inverse)


def normalize_back(incoming, scaled, inverse, gain):
    grad_scaled = incoming * gain
    mean_one = jnp.mean(grad_scaled, axis=-1, keepdims=True)
    mean_two = jnp.mean(grad_scaled * scaled, axis=-1, keepdims=True)
    outgoing = inverse * (grad_scaled - mean_one - scaled * mean_two)
    return (outgoing, jnp.sum(incoming * scaled, axis=0), jnp.sum(incoming, axis=0))


def on_device(
    sizes,
    tokens,
    segment_ids,
    project_weight,
    query_bias,
    value_bias,
    output_weight,
    output_bias,
    first_gain,
    first_shift,
    expand_weight,
    expand_bias,
    reduce_weight,
    reduce_bias,
    second_gain,
    second_shift,
    grad_out,
):
    chips = sizes["z"] * sizes["y"] * sizes["x"]
    ctx_size = sizes["x"] * sizes["c"]
    everyone = chips * sizes["c"]
    seq_count, part, width = tokens.shape
    rows_count = seq_count * part
    hidden = expand_weight.shape[1]
    share = width // everyone
    own_hidden = hidden // 2
    lanes = width // ctx_size
    place = lax.axis_index(CTX)
    core = lax.axis_index("c")
    low_core = core == 0

    def hop(array, step):
        return lax.ppermute(array, CTX, [(i, i ^ step) for i in range(ctx_size)])

    def swap(array):
        return lax.ppermute(array, "c", [(0, 1), (1, 0)])

    def chosen(array, index, axis):
        return lax.dynamic_index_in_dim(array, index, axis, keepdims=False)

    def by_core(own, other, axis):
        return jnp.where(
            low_core, jnp.stack([own, other], axis=axis), jnp.stack([other, own], axis=axis)
        )

    pieces = [tokens[i * seq_count // CHUNKS : (i + 1) * seq_count // CHUNKS] for i in range(CHUNKS)]
    gathered = []
    for piece in pieces:
        across = hop(piece, 2)
        gathered.append((piece, swap(piece), across, swap(across)))
    seg_parts = segment_ids.reshape(seq_count, ctx_size, part)
    seg = jnp.concatenate([chosen(seg_parts, place ^ r, 1) for r in range(ctx_size)], axis=1)
    seg_key = seg[:, :, None]
    seg_query = seg[:, None, :]

    mine = lax.all_to_all(
        project_weight.reshape(share, 3, ctx_size, lanes), CTX, 2, 0, tiled=False
    ).reshape(ctx_size * share, 3 * lanes)
    full_project = lax.all_gather(mine, SEQ, axis=0, tiled=True)

    vectors = (
        query_bias,
        value_bias,
        output_bias,
        first_gain,
        first_shift,
        reduce_bias,
        second_gain,
        second_shift,
    )
    packed = lax.all_gather(
        jnp.concatenate(vectors + (expand_bias,))[None], ALL, axis=0, tiled=True
    ).astype(F32)
    full_query, full_value, out_bias, gain_one, shift_one, red_bias, gain_two, shift_two = [
        packed[:, i * share : (i + 1) * share].reshape(width) for i in range(8)
    ]
    exp_bias = chosen(packed[:, 8 * share :].reshape(chips, 2, -1), core, 1).reshape(1, own_hidden)
    bias_all = jnp.concatenate(
        [
            lax.dynamic_slice_in_dim(full_query, place * lanes, lanes),
            jnp.zeros((lanes,), F32),
            lax.dynamic_slice_in_dim(full_value, place * lanes, lanes),
        ]
    )[None]

    out_half = lax.all_gather(output_weight, CHIPS, axis=0, tiled=True).reshape(
        chips, share, width
    )
    full_output = by_core(out_half, swap(out_half), 1).reshape(ctx_size, lanes, width)
    full_output = jnp.concatenate(
        [chosen(full_output, place ^ r, 0) for r in range(ctx_size)], axis=0
    )

    columns = expand_weight.reshape(share, chips, 2, own_hidden // chips)
    own_columns = chosen(columns, core, 2).reshape(share, own_hidden)
    far_columns = chosen(columns, 1 - core, 2).reshape(share, own_hidden)
    both = by_core(own_columns, swap(far_columns), 0).reshape(2 * share, own_hidden)
    full_expand = lax.all_gather(both, CHIPS, axis=0, tiled=True)
    full_reduce = lax.all_gather(reduce_weight, CHIPS, axis=0, tiled=True)

    saved = []
    kept_rows = []
    mixed_parts = []
    for index in range(CHUNKS):
        at = slice(index * seq_count // CHUNKS, (index + 1) * seq_count // CHUNKS)
        *mixed, all_rows, kept = attend(
            gathered[index], full_project, bias_all, seg_key[at], seg_query[at]
        )
        kept_rows.append(all_rows.reshape(-1, width))
        saved.append(kept)
        mixed_parts.append(
            jnp.concatenate([mixed[0]] + [hop(mixed[r], r) for r in (1, 2, 3)], axis=2)
        )
    mixed_low = jnp.concatenate(mixed_parts, axis=0).reshape(rows_count, width)

    rows = tokens.reshape(rows_count, width)
    attended = dot(mixed_low, full_output) + out_bias
    scaled_one, inverse_one = normalize(rows.astype(F32) + attended)
    first = scaled_one * gain_one + shift_one
    first_low = first.astype(BF16)
    first_far = swap(first_low)
    act, slope, own_sum, far_sum = feed(first_low, first_far, full_expand, exp_bias, full_reduce)
    reduced = own_sum + swap(far_sum).astype(F32) + red_bias
    scaled_two, inverse_two = normalize(first + reduced)
    layer_work = (scaled_two * gain_two + shift_two).astype(BF16).reshape(tokens.shape)

    grad_rows = grad_out.reshape(rows_count, width).astype(F32)
    grad_second, grad_gain_two, grad_shift_two = normalize_back(
        grad_rows, scaled_two, inverse_two, gain_two
    )
    grad_reduced = grad_second.astype(BF16)
    reduce_bias_grad = jnp.sum(grad_reduced.astype(F32), axis=0)
    expand_grad, reduce_grad, expand_bias_grad, own_back, far_back = feed_back(
        grad_reduced,
        swap(grad_reduced),
        first_low,
        first_far,
        act,
        slope,
        full_expand,
        full_reduce,
    )
    reduce_owned = lax.psum_scatter(reduce_grad, CHIPS, scatter_dimension=0, tiled=True)
    expand_owned = lax.psum_scatter(expand_grad, CHIPS, scatter_dimension=0, tiled=True)
    grad_first = grad_second + own_back + swap(far_back).astype(F32)
    grad_hidden, grad_gain_one, grad_shift_one = normalize_back(
        grad_first, scaled_one, inverse_one, gain_one
    )
    grad_attended = grad_hidden.astype(BF16)
    output_bias_grad = jnp.sum(grad_attended.astype(F32), axis=0)
    grad_mixed = dot(grad_attended, full_output, (1, 1)).astype(BF16)
    grad_mixed = grad_mixed.reshape(seq_count, part, ctx_size, lanes)

    output_grad = dot(mixed_low, grad_attended, (0, 0)).astype(BF16)
    output_grad = output_grad.reshape(ctx_size, lanes, width)
    output_grad = jnp.concatenate(
        [chosen(output_grad, place ^ r, 0) for r in range(ctx_size)], axis=0
    ).reshape(chips, 2, share, width)
    output_grad = chosen(output_grad, core, 1).astype(F32) + swap(
        chosen(output_grad, 1 - core, 1)
    ).astype(F32)
    output_owned = lax.psum_scatter(
        output_grad.astype(BF16).reshape(chips * share, width),
        CHIPS,
        scatter_dimension=0,
        tiled=True,
    )

    project_parts = []
    work_parts = []
    sum_parts = []
    for index in range(CHUNKS):
        at = slice(index * seq_count // CHUNKS, (index + 1) * seq_count // CHUNKS)
        grads = [grad_mixed[at, :, 0]] + [hop(grad_mixed[at, :, r], r) for r in (1, 2, 3)]
        grad_part, r0, r1, r2, r3, sums = attend_back(
            saved[index], grads, full_project, seg_key[at], seg_query[at]
        )
        across = r2 + swap(r3).astype(F32)
        work_parts.append(r0 + swap(r1).astype(F32) + hop(across.astype(BF16), 2).astype(F32))
        project_parts.append(grad_part)
        sum_parts.append(sums)
    project_grad = sum(
        dot(all_rows, grad_part.reshape(-1, 3 * lanes), (0, 0))
        for all_rows, grad_part in zip(kept_rows, project_parts)
    )
    grad_work = grad_hidden.reshape(tokens.shape) + jnp.concatenate(work_parts, axis=0)
    project_owned = lax.psum_scatter(
        project_grad.astype(BF16), SEQ, scatter_dimension=0, tiled=True
    )
    project_owned = lax.all_to_all(
        project_owned.reshape(ctx_size, share, 3, lanes), CTX, 0, 2, tiled=False
    ).reshape(share, 3 * width)

    far_rows = expand_owned.reshape(2, share, own_hidden)
    expand_owned = by_core(
        chosen(far_rows, core, 0).reshape(share, chips, -1),
        swap(chosen(far_rows, 1 - core, 0)).reshape(share, chips, -1),
        2,
    ).reshape(share, hidden)

    column_sums = jnp.sum(jnp.concatenate(sum_parts, axis=0), axis=(0, 1))
    zeros = jnp.zeros((width,), F32)
    grad_vectors = (
        lax.dynamic_update_slice_in_dim(zeros, column_sums[:lanes], place * lanes, 0),
        lax.dynamic_update_slice_in_dim(zeros, column_sums[2 * lanes :], place * lanes, 0),
        output_bias_grad,
        grad_gain_one,
        grad_shift_one,
        reduce_bias_grad,
        grad_gain_two,
        grad_shift_two,
    )
    hidden_sums = expand_bias_grad.reshape(chips, 1, own_hidden // chips)
    hidden_sums = jnp.where(
        low_core,
        jnp.concatenate([hidden_sums, jnp.zeros_like(hidden_sums)], axis=1),
        jnp.concatenate([jnp.zeros_like(hidden_sums), hidden_sums], axis=1),
    )
    packed_grads = jnp.concatenate(
        [vector.reshape(everyone, share) for vector in grad_vectors]
        + [hidden_sums.reshape(everyone, -1)],
        axis=1,
    )
    owned = lax.psum_scatter(packed_grads, ALL, scatter_dimension=0, tiled=True)[0]
    small = [owned[i * share : (i + 1) * share] for i in range(8)]
    return (
        layer_work,
        grad_work,
        project_owned.astype(F32),
        small[0],
        small[1],
        output_owned.astype(F32),
        small[2],
        small[3],
        small[4],
        expand_owned.astype(F32),
        owned[8 * share :],
        reduce_owned.astype(F32),
        small[5],
        small[6],
        small[7],
    )


def solution(mesh):
    seq_size, ctx_size = mesh.shape["seq"], mesh.shape["ctx"]
    sizes = {"z": seq_size // 2, "y": 2, "x": ctx_size // 2, "c": 2}
    fine = Mesh(mesh.devices.reshape(tuple(sizes.values())), tuple(sizes))
    rows = P(SEQ, CTX, None)
    matrix = P(ALL, None)
    vector = P(ALL)
    return jax.shard_map(
        functools.partial(on_device, sizes),
        mesh=fine,
        in_specs=(
            rows,
            P(SEQ, None),
            matrix,
            vector,
            vector,
            matrix,
            vector,
            vector,
            vector,
            matrix,
            vector,
            matrix,
            vector,
            vector,
            vector,
            rows,
        ),
        out_specs=(
            rows,
            rows,
            matrix,
            vector,
            vector,
            matrix,
            vector,
            vector,
            vector,
            matrix,
            vector,
            matrix,
            vector,
            vector,
            vector,
        ),
        check_vma=False,
    )
```

```python
import functools

import jax
import jax.numpy as jnp
from jax import lax
from jax.experimental import pallas as pl
from jax.experimental.pallas import tpu as pltpu
from jax.sharding import Mesh
from jax.sharding import PartitionSpec as P

HEADS = 16
HEAD_DIM = 64
CHUNKS = 4
MIB = 1 << 20
CHIPS = ("z", "y", "x")
SEQ = ("z", "y")
CTX = ("x", "c")
ALL = ("z", "y", "x", "c")
F32 = jnp.float32
BF16 = jnp.bfloat16
ELSEWHERE = pl.BlockSpec(memory_space=pl.ANY)


def dot(left, right, contract=(1, 0)):
    return lax.dot_general(
        left, right, (((contract[0],), (contract[1],)), ((), ())), preferred_element_type=F32
    )


def resident(shape):
    return pl.BlockSpec(shape, lambda i: (0,) * len(shape), pipeline_mode=pl.Buffered(1))


def by_row(shape):
    return pl.BlockSpec(shape, lambda i: (i,) + (0,) * (len(shape) - 1))


def softmax_down(scores, allowed):
    scores = jnp.where(allowed, scores, -1e30)
    top = jnp.max(scores, axis=0, keepdims=True)
    expo = jnp.exp(scores - top)
    total = jnp.sum(expo, axis=0, keepdims=True)
    return expo * (1.0 / total)


def head_lanes(width, head):
    lane = lax.broadcasted_iota(jnp.int32, (1, width), 1)
    return (lane // HEAD_DIM == head).astype(F32)


def attend_kernel(late, t0, t1, t2, t3, weight, bias, seg_key, seg_query, *refs):
    m0, m1, m2, m3, kept, saved = refs[late:]
    part = t0.shape[1]
    rows = jnp.concatenate([t[0] for t in (t0, t1, t2, t3)], axis=0)
    kept[0] = rows
    project = dot(rows, weight[...]) + bias[...]
    saved[0] = project.astype(BF16)
    width = project.shape[1] // 3
    queries = (project[:, :width].astype(BF16).astype(F32) * HEAD_DIM**-0.5).astype(BF16)
    keys = project[:, width : 2 * width].astype(BF16).astype(F32)
    values_t = jnp.transpose(project[:, 2 * width :]).astype(BF16)
    allowed = seg_key[0] == seg_query[0]
    mixed = []
    for head in range(width // HEAD_DIM):
        own_keys = (keys * head_lanes(width, head)).astype(BF16)
        chances = softmax_down(dot(own_keys, queries, (1, 1)), allowed)
        own_values = values_t[head * HEAD_DIM : (head + 1) * HEAD_DIM]
        mixed.append(dot(own_values, chances.astype(BF16)))
    mixed = jnp.transpose(jnp.concatenate(mixed, axis=0)).astype(BF16)
    for index, out in enumerate((m0, m1, m2, m3)):
        out[0] = mixed[index * part : (index + 1) * part]


def attend(tokens, weight, bias, seg_key, seg_query, after):
    count, part, depth = tokens[0].shape
    wide = weight.shape[1]
    length = 4 * part
    return pl.pallas_call(
        functools.partial(attend_kernel, len(after)),
        grid=(count,),
        in_specs=[by_row((1, part, depth))] * 4
        + [
            resident((depth, wide)),
            resident((1, wide)),
            by_row((1, length, 1)),
            by_row((1, 1, length)),
        ]
        + [ELSEWHERE] * len(after),
        out_specs=[by_row((1, part, wide // 3))] * 4
        + [by_row((1, length, depth)), by_row((1, length, wide))],
        out_shape=[jax.ShapeDtypeStruct((count, part, wide // 3), BF16)] * 4
        + [
            jax.ShapeDtypeStruct((count, length, depth), BF16),
            jax.ShapeDtypeStruct((count, length, wide), BF16),
        ],
        compiler_params=pltpu.CompilerParams(vmem_limit_bytes=40 * MIB),
        cost_estimate=pl.CostEstimate(
            flops=count * length * wide * (2 * depth + 16 * length // 3),
            bytes_accessed=count * length * (depth + 2 * wide) * 2,
            transcendentals=count * length * length * wide // (3 * HEAD_DIM),
        ),
        name="attend_forward",
    )(*tokens, weight, bias, seg_key, seg_query, *after)


def attend_back_kernel(late, saved, g0, g1, g2, g3, weight, seg_key, seg_query, *refs):
    grad_project, r0, r1, r2, r3, sums = refs[late:]
    part = g0.shape[1]
    width = saved.shape[2] // 3
    factor = HEAD_DIM**-0.5
    queries = (saved[0, :, :width].astype(F32) * factor).astype(BF16)
    keys = saved[0, :, width : 2 * width].astype(F32)
    values = saved[0, :, 2 * width :].astype(F32)
    keys_t = jnp.transpose(keys * factor).astype(BF16)
    grad_mixed = jnp.concatenate([g[0] for g in (g0, g1, g2, g3)], axis=0)
    allowed = seg_key[0] == seg_query[0]
    grad_queries = []
    grad_keys = None
    grad_values = None
    for head in range(width // HEAD_DIM):
        lanes = head_lanes(width, head)
        chances = softmax_down(
            dot((keys * lanes).astype(BF16), queries, (1, 1)), allowed
        )
        grad_weights = dot((values * lanes).astype(BF16), grad_mixed, (1, 1))
        inner = jnp.sum(chances * grad_weights, axis=0, keepdims=True)
        grad_scores = (chances * (grad_weights - inner)).astype(BF16)
        grad_queries.append(dot(keys_t[head * HEAD_DIM : (head + 1) * HEAD_DIM], grad_scores))
        keys_term = dot(grad_scores, queries)
        values_term = dot(chances.astype(BF16), grad_mixed)
        if head == 0:
            grad_keys, grad_values = keys_term, values_term
        else:
            here = lanes > 0.5
            grad_keys = jnp.where(here, keys_term, grad_keys)
            grad_values = jnp.where(here, values_term, grad_values)
    grad_queries = jnp.transpose(jnp.concatenate(grad_queries, axis=0))
    whole = jnp.concatenate(
        [grad_queries.astype(BF16), grad_keys.astype(BF16), grad_values.astype(BF16)], axis=1
    )
    grad_project[0] = whole
    sums[0] = jnp.sum(whole.astype(F32), axis=0, keepdims=True)
    for index, out in enumerate((r0, r1, r2, r3)):
        out[0] = dot(whole[index * part : (index + 1) * part], weight[...], (1, 1)).astype(
            out.dtype
        )


def attend_back(saved, grads, weight, seg_key, seg_query, after):
    count, part, width = grads[0].shape
    depth, wide = weight.shape
    length = 4 * part
    return pl.pallas_call(
        functools.partial(attend_back_kernel, len(after)),
        grid=(count,),
        in_specs=[by_row((1, length, wide))]
        + [by_row((1, part, width))] * 4
        + [
            resident((depth, wide)),
            by_row((1, length, 1)),
            by_row((1, 1, length)),
        ]
        + [ELSEWHERE] * len(after),
        out_specs=[by_row((1, length, wide))]
        + [by_row((1, part, depth))] * 4
        + [by_row((1, 1, wide))],
        out_shape=[jax.ShapeDtypeStruct((count, length, wide), BF16)]
        + [jax.ShapeDtypeStruct((count, part, depth), t) for t in (F32, BF16, F32, BF16)]
        + [jax.ShapeDtypeStruct((count, 1, wide), F32)],
        compiler_params=pltpu.CompilerParams(vmem_limit_bytes=48 * MIB),
        cost_estimate=pl.CostEstimate(
            flops=count * length * wide * (2 * depth + 40 * length // 3),
            bytes_accessed=count * length * (3 * depth + 3 * wide) * 2,
            transcendentals=count * length * length * wide // (3 * HEAD_DIM),
        ),
        name="attend_backward",
    )(saved, *grads, weight, seg_key, seg_query, *after)


def column(shape):
    return pl.BlockSpec(shape, lambda i: (0, i))


def feed_kernel(block, own, other, expand, bias, reduce, act, slope, own_out, other_out, far_sum):
    step = pl.program_id(0)
    rows = own.shape[0]

    @pl.when(step == 0)
    def _():
        own_out[...] = jnp.zeros_like(own_out)
        far_sum[...] = jnp.zeros_like(far_sum)

    for source, total, start in ((own, own_out, 0), (other, far_sum, rows)):
        for index in range(rows // block):
            at = slice(index * block, (index + 1) * block)
            to = slice(start + index * block, start + (index + 1) * block)
            inside = dot(source[at], expand[...]) + bias[...]
            square = inside * inside
            curve = jnp.tanh(0.7978845608028654 * inside * (1.0 + 0.044715 * square))
            half = 0.5 * (1.0 + curve)
            active = (inside * half).astype(BF16)
            act[to] = active
            slope[to] = (
                half
                + 0.5
                * inside
                * (1.0 - curve * curve)
                * (0.7978845608028654 * (1.0 + 3 * 0.044715 * square))
            ).astype(BF16)
            total[at] += dot(active, reduce[...])

    @pl.when(step == pl.num_programs(0) - 1)
    def _():
        other_out[...] = far_sum[...].astype(BF16)


def feed(own, other, expand, bias, reduce):
    rows, depth = own.shape
    hidden = expand.shape[1]
    piece = 512
    return pl.pallas_call(
        functools.partial(feed_kernel, 512),
        grid=(hidden // piece,),
        in_specs=[resident((rows, depth))] * 2
        + [column((depth, piece)), column((1, piece)), by_row((piece, depth))],
        out_specs=[column((2 * rows, piece))] * 2 + [resident((rows, depth))] * 2,
        out_shape=[jax.ShapeDtypeStruct((2 * rows, hidden), BF16)] * 2
        + [
            jax.ShapeDtypeStruct((rows, depth), F32),
            jax.ShapeDtypeStruct((rows, depth), BF16),
        ],
        scratch_shapes=[pltpu.VMEM((rows, depth), F32)],
        compiler_params=pltpu.CompilerParams(vmem_limit_bytes=56 * MIB),
        cost_estimate=pl.CostEstimate(
            flops=8 * rows * depth * hidden,
            bytes_accessed=4 * rows * (2 * hidden + 3 * depth),
            transcendentals=2 * rows * hidden,
        ),
        name="feed_forward",
    )(own, other, expand, bias, reduce)


def feed_back_kernel(
    block,
    own_grad,
    other_grad,
    own_rows,
    other_rows,
    act,
    slope,
    expand,
    reduce,
    expand_grad,
    reduce_grad,
    bias_grad,
    own_out,
    other_out,
    far_sum,
    inside,
):
    step = pl.program_id(0)
    rows = own_grad.shape[0]

    @pl.when(step == 0)
    def _():
        own_out[...] = jnp.zeros_like(own_out)
        far_sum[...] = jnp.zeros_like(far_sum)

    bias_sum = jnp.zeros(bias_grad.shape, F32)
    for source, total, start in ((own_grad, own_out, 0), (other_grad, far_sum, rows)):
        for index in range(rows // block):
            at = slice(index * block, (index + 1) * block)
            to = slice(start + index * block, start + (index + 1) * block)
            grad_act = dot(source[at], reduce[...], (1, 1))
            part = (grad_act * slope[to].astype(F32)).astype(BF16)
            inside[to] = part
            bias_sum += jnp.sum(part.astype(F32), axis=0, keepdims=True)
            total[at] += dot(part, expand[...], (1, 1))
    bias_grad[...] = bias_sum
    reduce_grad[...] = (
        dot(act[:rows], own_grad[...], (0, 0)) + dot(act[rows:], other_grad[...], (0, 0))
    ).astype(BF16)
    flipped = dot(inside[:rows], own_rows[...], (0, 0)) + dot(
        inside[rows:], other_rows[...], (0, 0)
    )
    expand_grad[...] = jnp.transpose(flipped).astype(BF16)

    @pl.when(step == pl.num_programs(0) - 1)
    def _():
        other_out[...] = far_sum[...].astype(BF16)


def feed_back(own_grad, other_grad, own_rows, other_rows, act, slope, expand, reduce):
    rows, depth = own_grad.shape
    hidden = expand.shape[1]
    piece = 256
    return pl.pallas_call(
        functools.partial(feed_back_kernel, 512),
        grid=(hidden // piece,),
        in_specs=[resident((rows, depth))] * 4
        + [column((2 * rows, piece))] * 2
        + [column((depth, piece)), by_row((piece, depth))],
        out_specs=[
            column((depth, piece)),
            by_row((piece, depth)),
            column((1, piece)),
        ]
        + [resident((rows, depth))] * 2,
        out_shape=[
            jax.ShapeDtypeStruct((depth, hidden), BF16),
            jax.ShapeDtypeStruct((hidden, depth), BF16),
            jax.ShapeDtypeStruct((1, hidden), F32),
            jax.ShapeDtypeStruct((rows, depth), F32),
            jax.ShapeDtypeStruct((rows, depth), BF16),
        ],
        scratch_shapes=[
            pltpu.VMEM((rows, depth), F32),
            pltpu.VMEM((2 * rows, piece), BF16),
        ],
        compiler_params=pltpu.CompilerParams(vmem_limit_bytes=56 * MIB),
        cost_estimate=pl.CostEstimate(
            flops=16 * rows * depth * hidden,
            bytes_accessed=4 * rows * (2 * hidden + 5 * depth) + 8 * depth * hidden,
            transcendentals=0,
        ),
        name="feed_backward",
    )(own_grad, other_grad, own_rows, other_rows, act, slope, expand, reduce)


def normalize(values):
    center = values - jnp.mean(values, axis=-1, keepdims=True)
    inverse = lax.rsqrt(jnp.mean(center * center, axis=-1, keepdims=True) + 1e-05)
    return (center * inverse, inverse)


def normalize_back(incoming, scaled, inverse, gain):
    grad_scaled = incoming * gain
    mean_one = jnp.mean(grad_scaled, axis=-1, keepdims=True)
    mean_two = jnp.mean(grad_scaled * scaled, axis=-1, keepdims=True)
    outgoing = inverse * (grad_scaled - mean_one - scaled * mean_two)
    return (outgoing, jnp.sum(incoming * scaled, axis=0), jnp.sum(incoming, axis=0))


def on_device(
    sizes,
    tokens,
    segment_ids,
    project_weight,
    query_bias,
    value_bias,
    output_weight,
    output_bias,
    first_gain,
    first_shift,
    expand_weight,
    expand_bias,
    reduce_weight,
    reduce_bias,
    second_gain,
    second_shift,
    grad_out,
):
    chips = sizes["z"] * sizes["y"] * sizes["x"]
    ctx_size = sizes["x"] * sizes["c"]
    everyone = chips * sizes["c"]
    seq_count, part, width = tokens.shape
    rows_count = seq_count * part
    hidden = expand_weight.shape[1]
    share = width // everyone
    own_hidden = hidden // 2
    lanes = width // ctx_size
    place = lax.axis_index(CTX)
    core = lax.axis_index("c")
    low_core = core == 0

    def hop(array, step):
        return lax.ppermute(array, CTX, [(i, i ^ step) for i in range(ctx_size)])

    def swap(array):
        return lax.ppermute(array, "c", [(0, 1), (1, 0)])

    def chosen(array, index, axis):
        return lax.dynamic_index_in_dim(array, index, axis, keepdims=False)

    def trade(array, name):
        return lax.ppermute(array, name, [(0, 1), (1, 0)])

    def pair(own, other, axis, name):
        return jnp.where(
            lax.axis_index(name) == 0,
            jnp.stack([own, other], axis=axis),
            jnp.stack([other, own], axis=axis),
        )

    def by_core(own, other, axis):
        return pair(own, other, axis, "c")

    def halve(array, axis, name):
        me = lax.axis_index(name)
        return chosen(array, me, axis).astype(F32) + trade(
            chosen(array, 1 - me, axis), name
        ).astype(F32)

    last = sizes["z"] - 1
    up = [(i, i + 1) for i in range(last)]
    down = [(i + 1, i) for i in range(last)]
    height = lax.axis_index("z")

    def chain_gather(block):
        if last > 3:
            return lax.all_gather(block, "z"), [[block]] * 3
        below, above, steps = [], [], []
        low_block, high_block = block, block
        for _ in range(last):
            low_block = lax.ppermute(low_block, "z", up)
            high_block = lax.ppermute(high_block, "z", down)
            below.append(low_block)
            above.append(high_block)
            steps.append([low_block, high_block])
        line = jnp.stack(below[::-1] + [block] + above)
        return lax.dynamic_slice_in_dim(line, last - height, last + 1, 0), steps

    def chain_scatter(blocks, kind=BF16):
        if last > 3:
            return lax.psum_scatter(blocks, "z").astype(F32), [[blocks]] * 3
        low_sum, high_sum, steps = None, None, []
        for step in range(last):
            low_send = chosen(blocks, jnp.minimum(last - step + height, last), 0)
            high_send = chosen(blocks, jnp.maximum(height - last + step, 0), 0)
            if step:
                low_send = (low_send.astype(F32) + low_sum.astype(F32)).astype(kind)
                high_send = (high_send.astype(F32) + high_sum.astype(F32)).astype(kind)
            low_sum = lax.ppermute(low_send, "z", up)
            high_sum = lax.ppermute(high_send, "z", down)
            steps.append([low_sum, high_sum])
        own = chosen(blocks, height, 0).astype(F32)
        return own + low_sum.astype(F32) + high_sum.astype(F32), steps

    pieces = [tokens[i * seq_count // CHUNKS : (i + 1) * seq_count // CHUNKS] for i in range(CHUNKS)]
    gathered = []
    for piece in pieces:
        across = hop(piece, 2)
        gathered.append((piece, swap(piece), across, swap(across)))
    seg_parts = segment_ids.reshape(seq_count, ctx_size, part)
    seg = jnp.concatenate([chosen(seg_parts, place ^ r, 1) for r in range(ctx_size)], axis=1)
    seg_key = seg[:, :, None]
    seg_query = seg[:, None, :]

    vectors = (
        query_bias,
        value_bias,
        output_bias,
        first_gain,
        first_shift,
        reduce_bias,
        second_gain,
        second_shift,
        expand_bias,
    )
    vector_count = 8 * share + expand_bias.shape[0]
    blocks = project_weight.reshape(share, 3, ctx_size, lanes)
    own_vectors = jnp.concatenate(vectors)
    columns_of = [chosen(blocks, place ^ r, 2) for r in range(ctx_size)]
    weights_from = [columns_of[0]] + [hop(columns_of[r], r) for r in (1, 2, 3)]
    vectors_from = [own_vectors] + [hop(own_vectors, r) for r in (1, 2, 3)]
    weights_from = jnp.stack(weights_from).reshape(ctx_size, share, 3 * lanes)
    mine = jnp.concatenate([chosen(weights_from, place ^ r, 0) for r in range(ctx_size)], axis=0)
    vectors_from = jnp.stack(vectors_from)
    vectors_from = jnp.stack([chosen(vectors_from, place ^ r, 0) for r in range(ctx_size)])
    below = 16 * -(-ctx_size * vector_count // (48 * lanes))
    vector_rows = jnp.pad(
        vectors_from.reshape(-1), (0, below * 3 * lanes - ctx_size * vector_count)
    ).reshape(below, 3 * lanes)
    whole_project = lax.all_gather(jnp.concatenate([mine, vector_rows]), SEQ, axis=0)
    whole_project = whole_project.reshape(-1, ctx_size * share + below, 3 * lanes)
    full_project = whole_project[:, : ctx_size * share].reshape(width, 3 * lanes)
    packed = (
        whole_project[:, ctx_size * share :]
        .reshape(-1, below * 3 * lanes)[:, : ctx_size * vector_count]
        .reshape(everyone, vector_count)
        .astype(F32)
    )
    full_query, full_value, out_bias, gain_one, shift_one, red_bias, gain_two, shift_two = [
        packed[:, i * share : (i + 1) * share].reshape(width) for i in range(8)
    ]
    exp_bias = chosen(packed[:, 8 * share :].reshape(chips, 2, -1), core, 1).reshape(1, own_hidden)
    bias_all = jnp.concatenate(
        [
            lax.dynamic_slice_in_dim(full_query, place * lanes, lanes),
            jnp.zeros((lanes,), F32),
            lax.dynamic_slice_in_dim(full_value, place * lanes, lanes),
        ]
    )[None]

    full_reduce = lax.all_gather(reduce_weight, CHIPS, axis=0, tiled=True)
    columns = expand_weight.reshape(share, chips, 2, own_hidden // chips)
    own_columns = chosen(columns, core, 2).reshape(share, own_hidden)
    far_columns = chosen(columns, 1 - core, 2).reshape(share, own_hidden)
    both = by_core(own_columns, swap(far_columns), 0).reshape(2 * share, own_hidden)
    both = pair(both, trade(both, "x"), 0, "x")
    both = pair(both, trade(both, "y"), 0, "y")
    full_expand, expand_steps = chain_gather(both)
    full_expand = full_expand.reshape(width, own_hidden)

    quarter = pair(output_weight, trade(output_weight, "x"), 0, "x")
    quarter, output_steps = chain_gather(quarter)
    out_half = pair(quarter, trade(quarter, "y"), 1, "y").reshape(chips, share, width)
    full_output = by_core(out_half, swap(out_half), 1).reshape(ctx_size, lanes, width)
    full_output = jnp.concatenate(
        [chosen(full_output, place ^ r, 0) for r in range(ctx_size)], axis=0
    )

    saved = []
    kept_rows = []
    mixed_parts = []
    for index in range(CHUNKS):
        at = slice(index * seq_count // CHUNKS, (index + 1) * seq_count // CHUNKS)
        *mixed, all_rows, kept = attend(
            gathered[index],
            full_project,
            bias_all,
            seg_key[at],
            seg_query[at],
            (expand_steps[0], expand_steps[1], [out_half], expand_steps[2])[index],
        )
        kept_rows.append(all_rows.reshape(-1, width))
        saved.append(kept)
        mixed_parts.append(
            jnp.concatenate([mixed[0]] + [hop(mixed[r], r) for r in (1, 2, 3)], axis=2)
        )
    mixed_low = jnp.concatenate(mixed_parts, axis=0).reshape(rows_count, width)

    rows = tokens.reshape(rows_count, width)
    attended = dot(mixed_low, full_output) + out_bias
    scaled_one, inverse_one = normalize(rows.astype(F32) + attended)
    first = scaled_one * gain_one + shift_one
    first_low = first.astype(BF16)
    first_far = swap(first_low)
    act, slope, own_sum, far_sum = feed(first_low, first_far, full_expand, exp_bias, full_reduce)
    reduced = own_sum + swap(far_sum).astype(F32) + red_bias
    scaled_two, inverse_two = normalize(first + reduced)
    layer_work = (scaled_two * gain_two + shift_two).astype(BF16).reshape(tokens.shape)

    grad_rows = grad_out.reshape(rows_count, width).astype(F32)
    grad_second, grad_gain_two, grad_shift_two = normalize_back(
        grad_rows, scaled_two, inverse_two, gain_two
    )
    grad_reduced = grad_second.astype(BF16)
    reduce_bias_grad = jnp.sum(grad_reduced.astype(F32), axis=0)
    expand_grad, reduce_grad, expand_bias_grad, own_back, far_back = feed_back(
        grad_reduced,
        swap(grad_reduced),
        first_low,
        first_far,
        act,
        slope,
        full_expand,
        full_reduce,
    )
    reduce_owned = lax.psum_scatter(reduce_grad, CHIPS, scatter_dimension=0, tiled=True)
    expand_grad = expand_grad.reshape(sizes["z"], 2, sizes["x"], 2 * share, own_hidden)
    expand_half = halve(expand_grad, 1, "y").astype(BF16)
    expand_line, expand_steps = chain_scatter(expand_half)
    grad_first = grad_second + own_back + swap(far_back).astype(F32)
    grad_hidden, grad_gain_one, grad_shift_one = normalize_back(
        grad_first, scaled_one, inverse_one, gain_one
    )
    grad_attended = grad_hidden.astype(BF16)
    output_bias_grad = jnp.sum(grad_attended.astype(F32), axis=0)
    grad_mixed = dot(grad_attended, full_output, (1, 1)).astype(BF16)
    grad_mixed = grad_mixed.reshape(seq_count, part, ctx_size, lanes)

    output_grad = dot(mixed_low, grad_attended, (0, 0)).astype(BF16)
    output_grad = output_grad.reshape(ctx_size, lanes, width)
    output_grad = jnp.concatenate(
        [chosen(output_grad, place ^ r, 0) for r in range(ctx_size)], axis=0
    ).reshape(sizes["z"], 2, sizes["x"], 2, share, width)
    output_half = halve(output_grad, 3, "c").astype(BF16)
    output_half = halve(output_half, 1, "y").astype(BF16)
    output_line, output_steps = chain_scatter(output_half)

    project_parts = []
    work_parts = []
    sum_parts = []
    for index in range(CHUNKS):
        at = slice(index * seq_count // CHUNKS, (index + 1) * seq_count // CHUNKS)
        grads = [grad_mixed[at, :, 0]] + [hop(grad_mixed[at, :, r], r) for r in (1, 2, 3)]
        grad_part, r0, r1, r2, r3, sums = attend_back(
            saved[index],
            grads,
            full_project,
            seg_key[at],
            seg_query[at],
            (
                [],
                [expand_half],
                expand_steps[0] + output_steps[0] + work_parts[:1],
                expand_steps[2] + output_steps[2] + work_parts[1:2] + [reduce_owned],
            )[index],
        )
        across = r2 + swap(r3).astype(F32)
        work_parts.append(
            grad_hidden[index * rows_count // CHUNKS : (index + 1) * rows_count // CHUNKS]
            .reshape(r0.shape)
            + r0
            + swap(r1).astype(F32)
            + hop(across.astype(BF16), 2).astype(F32)
        )
        project_parts.append(grad_part)
        sum_parts.append(sums)
    project_grad = sum(
        dot(all_rows, grad_part.reshape(-1, 3 * lanes), (0, 0))
        for all_rows, grad_part in zip(kept_rows, project_parts)
    )
    grad_work = jnp.concatenate(work_parts, axis=0)
    project_owned, _ = chain_scatter(
        halve(
            project_grad.astype(BF16).reshape(sizes["z"], 2, ctx_size * share, 3 * lanes), 1, "y"
        ).astype(BF16)
    )
    project_owned = lax.all_to_all(
        project_owned.reshape(ctx_size, share, 3, lanes), CTX, 0, 2, tiled=False
    ).reshape(share, 3 * width)
    expand_owned = halve(expand_line.astype(BF16), 0, "x")
    output_owned = halve(output_line.astype(BF16), 0, "x")

    far_rows = expand_owned.reshape(2, share, own_hidden)
    expand_owned = by_core(
        chosen(far_rows, core, 0).reshape(share, chips, -1),
        swap(chosen(far_rows, 1 - core, 0)).reshape(share, chips, -1),
        2,
    ).reshape(share, hidden)

    column_sums = jnp.sum(jnp.concatenate(sum_parts, axis=0), axis=(0, 1))
    zeros = jnp.zeros((width,), F32)
    grad_vectors = (
        lax.dynamic_update_slice_in_dim(zeros, column_sums[:lanes], place * lanes, 0),
        lax.dynamic_update_slice_in_dim(zeros, column_sums[2 * lanes :], place * lanes, 0),
        output_bias_grad,
        grad_gain_one,
        grad_shift_one,
        reduce_bias_grad,
        grad_gain_two,
        grad_shift_two,
    )
    hidden_sums = expand_bias_grad.reshape(chips, 1, own_hidden // chips)
    hidden_sums = jnp.where(
        low_core,
        jnp.concatenate([hidden_sums, jnp.zeros_like(hidden_sums)], axis=1),
        jnp.concatenate([jnp.zeros_like(hidden_sums), hidden_sums], axis=1),
    )
    packed_grads = jnp.concatenate(
        [vector.reshape(everyone, share) for vector in grad_vectors]
        + [hidden_sums.reshape(everyone, -1)],
        axis=1,
    )
    packed_grads = packed_grads.reshape(sizes["z"], 2, sizes["x"], 2, vector_count)
    for axis, name in ((3, "c"), (2, "x"), (1, "y")):
        packed_grads = halve(packed_grads, axis, name)
    owned, _ = chain_scatter(packed_grads, F32)
    small = [owned[i * share : (i + 1) * share] for i in range(8)]
    return (
        layer_work,
        grad_work,
        project_owned.astype(F32),
        small[0],
        small[1],
        output_owned.astype(F32),
        small[2],
        small[3],
        small[4],
        expand_owned.astype(F32),
        owned[8 * share :],
        reduce_owned.astype(F32),
        small[5],
        small[6],
        small[7],
    )


def solution(mesh):
    seq_size, ctx_size = mesh.shape["seq"], mesh.shape["ctx"]
    sizes = {"z": seq_size // 2, "y": 2, "x": ctx_size // 2, "c": 2}
    fine = Mesh(mesh.devices.reshape(tuple(sizes.values())), tuple(sizes))
    rows = P(SEQ, CTX, None)
    matrix = P(ALL, None)
    vector = P(ALL)
    return jax.shard_map(
        functools.partial(on_device, sizes),
        mesh=fine,
        in_specs=(
            rows,
            P(SEQ, None),
            matrix,
            vector,
            vector,
            matrix,
            vector,
            vector,
            vector,
            matrix,
            vector,
            matrix,
            vector,
            vector,
            vector,
            rows,
        ),
        out_specs=(
            rows,
            rows,
            matrix,
            vector,
            vector,
            matrix,
            vector,
            vector,
            vector,
            matrix,
            vector,
            matrix,
            vector,
            vector,
            vector,
        ),
        check_vma=False,
    )
```

```python
import functools

import jax
import jax.numpy as jnp
from jax import lax
from jax.experimental import pallas as pl
from jax.experimental.pallas import tpu as pltpu
from jax.sharding import Mesh
from jax.sharding import PartitionSpec as P

HEADS = 16
HEAD_DIM = 64
CHUNKS = 2
PIECE = 256
MIB = 1 << 20
CHIPS = ("z", "y", "x")
SEQ = ("z", "y")
CTX = ("x", "c")
ALL = ("z", "y", "x", "c")
F32 = jnp.float32
BF16 = jnp.bfloat16
ELSEWHERE = pl.BlockSpec(memory_space=pl.ANY)


def dot(left, right, contract=(1, 0)):
    return lax.dot_general(
        left, right, (((contract[0],), (contract[1],)), ((), ())), preferred_element_type=F32
    )


def resident(shape):
    return pl.BlockSpec(shape, lambda i: (0,) * len(shape), pipeline_mode=pl.Buffered(1))


def by_row(shape):
    return pl.BlockSpec(shape, lambda i: (i,) + (0,) * (len(shape) - 1))


def softmax_down(scores, allowed):
    scores = jnp.where(allowed, scores, -1e30)
    top = jnp.max(scores, axis=0, keepdims=True)
    expo = jnp.exp(scores - top)
    total = jnp.sum(expo, axis=0, keepdims=True)
    return expo * (1.0 / total)


def head_lanes(width, head):
    lane = lax.broadcasted_iota(jnp.int32, (1, width), 1)
    return (lane // HEAD_DIM == head).astype(F32)


def attend_kernel(late, t0, t1, t2, t3, weight, bias, seg_key, seg_query, *refs):
    m0, m1, m2, m3, kept, saved = refs[late:]
    part = t0.shape[1]
    rows = jnp.concatenate([t[0] for t in (t0, t1, t2, t3)], axis=0)
    kept[0] = rows
    project = dot(rows, weight[...]) + bias[...]
    saved[0] = project.astype(BF16)
    width = project.shape[1] // 3
    queries = (project[:, :width].astype(BF16).astype(F32) * HEAD_DIM**-0.5).astype(BF16)
    keys = project[:, width : 2 * width].astype(BF16).astype(F32)
    values_t = jnp.transpose(project[:, 2 * width :]).astype(BF16)
    allowed = seg_key[0] == seg_query[0]
    mixed = []
    for head in range(width // HEAD_DIM):
        own_keys = (keys * head_lanes(width, head)).astype(BF16)
        chances = softmax_down(dot(own_keys, queries, (1, 1)), allowed)
        own_values = values_t[head * HEAD_DIM : (head + 1) * HEAD_DIM]
        mixed.append(dot(own_values, chances.astype(BF16)))
    mixed = jnp.transpose(jnp.concatenate(mixed, axis=0)).astype(BF16)
    for index, out in enumerate((m0, m1, m2, m3)):
        out[0] = mixed[index * part : (index + 1) * part]


def attend(tokens, weight, bias, seg_key, seg_query, first, after):
    count, part, depth = tokens[0].shape
    count = count // CHUNKS
    wide = weight.shape[1]
    length = 4 * part
    return pl.pallas_call(
        functools.partial(attend_kernel, len(after)),
        grid=(count,),
        in_specs=[pl.BlockSpec((1, part, depth), lambda i: (i + first, 0, 0))] * 4
        + [
            resident((depth, wide)),
            resident((1, wide)),
            by_row((1, length, 1)),
            by_row((1, 1, length)),
        ]
        + [ELSEWHERE] * len(after),
        out_specs=[by_row((1, part, wide // 3))] * 4
        + [by_row((1, length, depth)), by_row((1, length, wide))],
        out_shape=[jax.ShapeDtypeStruct((count, part, wide // 3), BF16)] * 4
        + [
            jax.ShapeDtypeStruct((count, length, depth), BF16),
            jax.ShapeDtypeStruct((count, length, wide), BF16),
        ],
        compiler_params=pltpu.CompilerParams(vmem_limit_bytes=40 * MIB),
        cost_estimate=pl.CostEstimate(
            flops=count * length * wide * (2 * depth + 16 * length // 3),
            bytes_accessed=count * length * (depth + 2 * wide) * 2,
            transcendentals=count * length * length * wide // (3 * HEAD_DIM),
        ),
        name="attend_forward",
    )(*tokens, weight, bias, seg_key, seg_query, *after)


def attend_back_kernel(late, saved, g0, g1, g2, g3, weight, seg_key, seg_query, *refs):
    grad_project, r0, r1, r2, r3, sums = refs[late:]
    part = g0.shape[1]
    width = saved.shape[2] // 3
    factor = HEAD_DIM**-0.5
    queries = (saved[0, :, :width].astype(F32) * factor).astype(BF16)
    keys = saved[0, :, width : 2 * width].astype(F32)
    values = saved[0, :, 2 * width :].astype(F32)
    keys_t = jnp.transpose(keys * factor).astype(BF16)
    grad_mixed = jnp.concatenate([g[0] for g in (g0, g1, g2, g3)], axis=0)
    allowed = seg_key[0] == seg_query[0]
    grad_queries = []
    grad_keys = None
    grad_values = None
    for head in range(width // HEAD_DIM):
        lanes = head_lanes(width, head)
        chances = softmax_down(
            dot((keys * lanes).astype(BF16), queries, (1, 1)), allowed
        )
        grad_weights = dot((values * lanes).astype(BF16), grad_mixed, (1, 1))
        inner = jnp.sum(chances * grad_weights, axis=0, keepdims=True)
        grad_scores = (chances * (grad_weights - inner)).astype(BF16)
        grad_queries.append(dot(keys_t[head * HEAD_DIM : (head + 1) * HEAD_DIM], grad_scores))
        keys_term = dot(grad_scores, queries)
        values_term = dot(chances.astype(BF16), grad_mixed)
        if head == 0:
            grad_keys, grad_values = keys_term, values_term
        else:
            here = lanes > 0.5
            grad_keys = jnp.where(here, keys_term, grad_keys)
            grad_values = jnp.where(here, values_term, grad_values)
    grad_queries = jnp.transpose(jnp.concatenate(grad_queries, axis=0))
    whole = jnp.concatenate(
        [grad_queries.astype(BF16), grad_keys.astype(BF16), grad_values.astype(BF16)], axis=1
    )
    grad_project[0] = whole
    sums[0] = jnp.sum(whole.astype(F32), axis=0, keepdims=True)
    for index, out in enumerate((r0, r1, r2, r3)):
        out[0] = dot(whole[index * part : (index + 1) * part], weight[...], (1, 1)).astype(
            out.dtype
        )


def attend_back(saved, grads, weight, seg_key, seg_query, after):
    count, part, width = grads[0].shape
    depth, wide = weight.shape
    length = 4 * part
    return pl.pallas_call(
        functools.partial(attend_back_kernel, len(after)),
        grid=(count,),
        in_specs=[by_row((1, length, wide))]
        + [by_row((1, part, width))] * 4
        + [
            resident((depth, wide)),
            by_row((1, length, 1)),
            by_row((1, 1, length)),
        ]
        + [ELSEWHERE] * len(after),
        out_specs=[by_row((1, length, wide))]
        + [by_row((1, part, depth))] * 4
        + [by_row((1, 1, wide))],
        out_shape=[jax.ShapeDtypeStruct((count, length, wide), BF16)]
        + [jax.ShapeDtypeStruct((count, part, depth), t) for t in (F32, BF16, F32, BF16)]
        + [jax.ShapeDtypeStruct((count, 1, wide), F32)],
        compiler_params=pltpu.CompilerParams(vmem_limit_bytes=48 * MIB),
        cost_estimate=pl.CostEstimate(
            flops=count * length * wide * (2 * depth + 40 * length // 3),
            bytes_accessed=count * length * (3 * depth + 3 * wide) * 2,
            transcendentals=count * length * length * wide // (3 * HEAD_DIM),
        ),
        name="attend_backward",
    )(saved, *grads, weight, seg_key, seg_query, *after)


def column(shape):
    return pl.BlockSpec(shape, lambda i: (0, i))


def flat(block):
    wide = block.shape[-1]
    if block.shape[-2] % 16:
        return block.astype(F32).reshape(-1, wide).astype(BF16)
    return block.reshape(-1, wide)


def expand_piece(ref):
    return jnp.concatenate([flat(ref[:, i]) for i in range(ref.shape[1])], axis=1)


def reduce_piece(ref):
    columns = ref.shape[1] // 2
    halves = [
        jnp.concatenate([ref[:, half * columns + i] for i in range(columns)], axis=2)
        for half in range(2)
    ]
    return flat(jnp.concatenate(halves, axis=1))


def feed_kernel(block, own, other, expand, bias, reduce, act, slope, own_out, other_out, far_sum):
    step = pl.program_id(0)
    rows = own.shape[0]

    @pl.when(step == 0)
    def _():
        own_out[...] = jnp.zeros_like(own_out)
        far_sum[...] = jnp.zeros_like(far_sum)

    into = expand_piece(expand)
    back = reduce_piece(reduce)
    work = [
        (source, total, slice(i * block, (i + 1) * block), slice(start + i * block, start + (i + 1) * block))
        for source, total, start in ((own, own_out, 0), (other, far_sum, rows))
        for i in range(rows // block)
    ]
    ahead = dot(work[0][0][work[0][2]], into) + bias[...]
    for index, (_, total, at, to) in enumerate(work):
        inside = ahead
        if index + 1 < len(work):
            ahead = dot(work[index + 1][0][work[index + 1][2]], into) + bias[...]
        square = inside * inside
        curve = jnp.tanh(inside * (0.7978845608028654 + 0.7978845608028654 * 0.044715 * square))
        half = 0.5 * curve + 0.5
        active = (inside * half).astype(BF16)
        act[to] = active
        tilt = 0.7978845608028654 * 0.5 + 0.7978845608028654 * 1.5 * 0.044715 * square
        slope[to] = (half + inside * (1.0 - curve * curve) * tilt).astype(BF16)
        total[at] += dot(active, back)

    @pl.when(step == pl.num_programs(0) - 1)
    def _():
        other_out[...] = far_sum[...].astype(BF16)


def feed_weights(weights, pieces, columns):
    chips, _, rows, _ = weights.shape
    return [
        pl.BlockSpec((chips, pieces, rows, PIECE), lambda i: (0, i, 0, 0)),
        pl.BlockSpec(
            (pieces * PIECE // (2 * rows), 2 * columns, rows, PIECE), lambda i: (i, 1, 0, 0)
        ),
    ]


def feed(own, other, weights, bias):
    rows, depth = own.shape
    hidden = bias.shape[1]
    pieces = 2
    wide = pieces * PIECE
    expand_spec, reduce_spec = feed_weights(weights, pieces, depth // PIECE)
    return pl.pallas_call(
        functools.partial(feed_kernel, 512),
        grid=(hidden // wide,),
        in_specs=[resident((rows, depth))] * 2
        + [expand_spec, column((1, wide)), reduce_spec],
        out_specs=[column((2 * rows, wide))] * 2 + [resident((rows, depth))] * 2,
        out_shape=[jax.ShapeDtypeStruct((2 * rows, hidden), BF16)] * 2
        + [
            jax.ShapeDtypeStruct((rows, depth), F32),
            jax.ShapeDtypeStruct((rows, depth), BF16),
        ],
        scratch_shapes=[pltpu.VMEM((rows, depth), F32)],
        compiler_params=pltpu.CompilerParams(vmem_limit_bytes=56 * MIB),
        cost_estimate=pl.CostEstimate(
            flops=8 * rows * depth * hidden,
            bytes_accessed=4 * rows * (2 * hidden + 3 * depth),
            transcendentals=2 * rows * hidden,
        ),
        name="feed_forward",
    )(own, other, weights, bias, weights)


def feed_back_kernel(
    block,
    own_grad,
    other_grad,
    own_rows,
    other_rows,
    act,
    slope,
    expand,
    reduce,
    weight_grad,
    bias_grad,
    own_out,
    other_out,
    far_sum,
    inside,
):
    step = pl.program_id(0)
    rows = own_grad.shape[0]

    @pl.when(step == 0)
    def _():
        own_out[...] = jnp.zeros_like(own_out)
        far_sum[...] = jnp.zeros_like(far_sum)

    into = expand_piece(expand)
    back = reduce_piece(reduce)
    bias_sum = jnp.zeros(bias_grad.shape, F32)
    for source, total, start in ((own_grad, own_out, 0), (other_grad, far_sum, rows)):
        for index in range(rows // block):
            at = slice(index * block, (index + 1) * block)
            to = slice(start + index * block, start + (index + 1) * block)
            grad_act = dot(source[at], back, (1, 1))
            part = (grad_act * slope[to].astype(F32)).astype(BF16)
            inside[to] = part
            bias_sum += jnp.sum(part.astype(F32), axis=0, keepdims=True)
            total[at] += dot(part, into, (1, 1))
    bias_grad[...] = bias_sum
    chips, pieces, height, _ = weight_grad.shape
    columns = pieces // 4
    reduce_grad = dot(act[:rows], own_grad[...], (0, 0)) + dot(act[rows:], other_grad[...], (0, 0))
    count = PIECE // (2 * height)
    reduce_grad = reduce_grad.reshape(count, 2 * height, reduce_grad.shape[1]).astype(BF16)
    mine = pl.ds(step * count, count)
    for half in range(2):
        for i in range(columns):
            weight_grad[mine, (2 + half) * columns + i] = reduce_grad[
                :, half * height : (half + 1) * height, i * PIECE : (i + 1) * PIECE
            ]
    flipped = dot(inside[:rows], own_rows[...], (0, 0)) + dot(
        inside[rows:], other_rows[...], (0, 0)
    )
    expand_grad = jnp.transpose(flipped).reshape(chips, height, PIECE).astype(BF16)
    weight_grad[:, step] = expand_grad

    @pl.when(step == pl.num_programs(0) - 1)
    def _():
        other_out[...] = far_sum[...].astype(BF16)


def feed_back(own_grad, other_grad, own_rows, other_rows, act, slope, weights):
    rows, depth = own_grad.shape
    hidden = act.shape[1]
    chips, _, height, _ = weights.shape
    pieces = 2 * hidden // PIECE
    expand_spec, reduce_spec = feed_weights(weights, 1, depth // PIECE)
    return pl.pallas_call(
        functools.partial(feed_back_kernel, 512),
        grid=(hidden // PIECE,),
        in_specs=[resident((rows, depth))] * 4
        + [column((2 * rows, PIECE))] * 2
        + [expand_spec, reduce_spec],
        out_specs=[
            resident((chips, pieces, height, PIECE)),
            column((1, PIECE)),
        ]
        + [resident((rows, depth))] * 2,
        out_shape=[
            jax.ShapeDtypeStruct((chips, pieces, height, PIECE), BF16),
            jax.ShapeDtypeStruct((1, hidden), F32),
            jax.ShapeDtypeStruct((rows, depth), F32),
            jax.ShapeDtypeStruct((rows, depth), BF16),
        ],
        scratch_shapes=[
            pltpu.VMEM((rows, depth), F32),
            pltpu.VMEM((2 * rows, PIECE), BF16),
        ],
        compiler_params=pltpu.CompilerParams(vmem_limit_bytes=56 * MIB),
        cost_estimate=pl.CostEstimate(
            flops=16 * rows * depth * hidden,
            bytes_accessed=4 * rows * (2 * hidden + 5 * depth) + 8 * depth * hidden,
            transcendentals=0,
        ),
        name="feed_backward",
    )(own_grad, other_grad, own_rows, other_rows, act, slope, weights, weights)


def normalize(values):
    center = values - jnp.mean(values, axis=-1, keepdims=True)
    inverse = lax.rsqrt(jnp.mean(center * center, axis=-1, keepdims=True) + 1e-05)
    return (center * inverse, inverse)


def normalize_back(incoming, scaled, inverse, gain):
    grad_scaled = incoming * gain
    mean_one = jnp.mean(grad_scaled, axis=-1, keepdims=True)
    mean_two = jnp.mean(grad_scaled * scaled, axis=-1, keepdims=True)
    outgoing = inverse * (grad_scaled - mean_one - scaled * mean_two)
    return (outgoing, jnp.sum(incoming * scaled, axis=0), jnp.sum(incoming, axis=0))


def on_device(
    sizes,
    tokens,
    segment_ids,
    project_weight,
    query_bias,
    value_bias,
    output_weight,
    output_bias,
    first_gain,
    first_shift,
    expand_weight,
    expand_bias,
    reduce_weight,
    reduce_bias,
    second_gain,
    second_shift,
    grad_out,
):
    chips = sizes["z"] * sizes["y"] * sizes["x"]
    ctx_size = sizes["x"] * sizes["c"]
    everyone = chips * sizes["c"]
    seq_count, part, width = tokens.shape
    rows_count = seq_count * part
    hidden = expand_weight.shape[1]
    share = width // everyone
    own_hidden = hidden // 2
    lanes = width // ctx_size
    place = lax.axis_index(CTX)
    core = lax.axis_index("c")
    low_core = core == 0

    def hop(array, step):
        return lax.ppermute(array, CTX, [(i, i ^ step) for i in range(ctx_size)])

    def swap(array):
        return lax.ppermute(array, "c", [(0, 1), (1, 0)])

    def chosen(array, index, axis):
        return lax.dynamic_index_in_dim(array, index, axis, keepdims=False)

    def pair(own, other, axis, low):
        return jnp.where(
            low, jnp.stack([own, other], axis=axis), jnp.stack([other, own], axis=axis)
        )

    def by_core(own, other, axis):
        return pair(own, other, axis, low_core)

    def bit_of(name, step):
        return (lax.axis_index(name) // step) % 2

    def trade(array, name, step=1):
        return lax.ppermute(array, name, [(i, i ^ step) for i in range(sizes[name])])

    def widen(array, name, axis=0, step=1):
        return pair(array, trade(array, name, step), axis, bit_of(name, step) == 0)

    def halve(array, axis, name, step=1):
        me = bit_of(name, step)
        return chosen(array, me, axis).astype(F32) + trade(
            chosen(array, 1 - me, axis), name, step
        ).astype(F32)

    z_steps = [1 << i for i in range(sizes["z"].bit_length() - 1)]

    def z_gather(array):
        for index, step in enumerate(z_steps[::-1]):
            array = widen(array, "z", index, step)
        return array

    def z_scatter(blocks, kind=BF16):
        for step in z_steps:
            blocks = blocks.reshape((blocks.shape[0] // 2, 2) + blocks.shape[1:])
            blocks = halve(blocks.astype(kind), 1, "z", step)
        return blocks[0]

    across = hop(tokens, 2)
    gathered = (tokens, swap(tokens), across, swap(across))
    seg_parts = segment_ids.reshape(seq_count, ctx_size, part)
    seg = jnp.concatenate([chosen(seg_parts, place ^ r, 1) for r in range(ctx_size)], axis=1)
    seg_key = seg[:, :, None]
    seg_query = seg[:, None, :]

    vectors = (
        query_bias,
        value_bias,
        output_bias,
        first_gain,
        first_shift,
        reduce_bias,
        second_gain,
        second_shift,
        expand_bias,
    )
    vector_count = 8 * share + expand_bias.shape[0]
    blocks = project_weight.reshape(share, 3, ctx_size, lanes)
    own_vectors = jnp.concatenate(vectors)
    below = 16 * -(-ctx_size * vector_count // (48 * lanes))
    held = jnp.concatenate(
        [
            jnp.moveaxis(blocks, 2, 0).reshape(ctx_size, -1),
            jnp.broadcast_to(own_vectors, (ctx_size, vector_count)),
        ],
        axis=1,
    )
    held = lax.all_to_all(held, CTX, 0, 0, tiled=True)
    mine = held[:, : share * 3 * lanes].reshape(ctx_size * share, 3 * lanes)
    vector_rows = jnp.pad(
        held[:, share * 3 * lanes :].reshape(-1),
        (0, below * 3 * lanes - ctx_size * vector_count),
    ).reshape(below, 3 * lanes)
    whole_project = z_gather(widen(jnp.concatenate([mine, vector_rows]), "y"))
    whole_project = whole_project.reshape(-1, ctx_size * share + below, 3 * lanes)
    full_project = whole_project[:, : ctx_size * share].reshape(width, 3 * lanes)
    packed = (
        whole_project[:, ctx_size * share :]
        .reshape(-1, below * 3 * lanes)[:, : ctx_size * vector_count]
        .reshape(everyone, vector_count)
        .astype(F32)
    )
    full_query, full_value, out_bias, gain_one, shift_one, red_bias, gain_two, shift_two = [
        packed[:, i * share : (i + 1) * share].reshape(width) for i in range(8)
    ]
    exp_bias = chosen(packed[:, 8 * share :].reshape(chips, 2, -1), core, 1).reshape(1, own_hidden)
    bias_all = jnp.concatenate(
        [
            lax.dynamic_slice_in_dim(full_query, place * lanes, lanes),
            jnp.zeros((lanes,), F32),
            lax.dynamic_slice_in_dim(full_value, place * lanes, lanes),
        ]
    )[None]

    columns = expand_weight.reshape(share, chips, 2, own_hidden // chips)
    own_columns = chosen(columns, core, 2).reshape(share, own_hidden)
    far_columns = chosen(columns, 1 - core, 2).reshape(share, own_hidden)
    both = by_core(own_columns, swap(far_columns), 0)

    def in_pieces(array):
        rows_of, wide = array.shape
        return jnp.swapaxes(array.reshape(rows_of, wide // PIECE, PIECE), 0, 1).reshape(
            -1, 2 * share, PIECE
        )

    weights = lax.all_gather(
        jnp.concatenate(
            [
                in_pieces(both.reshape(2 * share, own_hidden)),
                jnp.swapaxes(
                    reduce_weight.reshape(2, 2 * share, width // PIECE, PIECE), 1, 2
                ).reshape(-1, 2 * share, PIECE),
                in_pieces(output_weight),
            ]
        ),
        CHIPS,
        axis=0,
    ).reshape(chips, -1, 2 * share, PIECE)
    feed_pieces = (own_hidden + 2 * width) // PIECE
    out_half = jnp.swapaxes(
        weights[:, feed_pieces:].reshape(chips, width // PIECE, share, PIECE), 1, 2
    ).reshape(chips, share, width)
    full_output = by_core(out_half, swap(out_half), 1).reshape(ctx_size, lanes, width)
    full_output = jnp.concatenate(
        [chosen(full_output, place ^ r, 0) for r in range(ctx_size)], axis=0
    )

    saved = []
    kept_rows = []
    mixed_parts = []
    for index in range(CHUNKS):
        at = slice(index * seq_count // CHUNKS, (index + 1) * seq_count // CHUNKS)
        *mixed, all_rows, kept = attend(
            gathered, full_project, bias_all, seg_key[at], seg_query[at], at.start, []
        )
        kept_rows.append(all_rows.reshape(-1, width))
        saved.append(kept)
        mixed_parts.append(
            jnp.concatenate([mixed[0]] + [hop(mixed[r], r) for r in (1, 2, 3)], axis=2)
        )
    mixed_low = jnp.concatenate(mixed_parts, axis=0).reshape(rows_count, width)

    rows = tokens.reshape(rows_count, width)
    attended = dot(mixed_low, full_output) + out_bias
    scaled_one, inverse_one = normalize(rows.astype(F32) + attended)
    first = scaled_one * gain_one + shift_one
    first_low = first.astype(BF16)
    first_far = swap(first_low)
    act, slope, own_sum, far_sum = feed(first_low, first_far, weights, exp_bias)
    reduced = own_sum + swap(far_sum).astype(F32) + red_bias
    scaled_two, inverse_two = normalize(first + reduced)
    layer_work = (scaled_two * gain_two + shift_two).astype(BF16).reshape(tokens.shape)

    grad_rows = grad_out.reshape(rows_count, width).astype(F32)
    grad_second, grad_gain_two, grad_shift_two = normalize_back(
        grad_rows, scaled_two, inverse_two, gain_two
    )
    grad_reduced = grad_second.astype(BF16)
    reduce_bias_grad = jnp.sum(grad_reduced.astype(F32), axis=0)
    weight_grad, expand_bias_grad, own_back, far_back = feed_back(
        grad_reduced, swap(grad_reduced), first_low, first_far, act, slope, weights
    )
    weight_owned = lax.psum_scatter(weight_grad, CHIPS, scatter_dimension=0, tiled=True)[0]
    grad_first = grad_second + own_back + swap(far_back).astype(F32)
    grad_hidden, grad_gain_one, grad_shift_one = normalize_back(
        grad_first, scaled_one, inverse_one, gain_one
    )
    grad_attended = grad_hidden.astype(BF16)
    output_bias_grad = jnp.sum(grad_attended.astype(F32), axis=0)
    grad_mixed = dot(grad_attended, full_output, (1, 1)).astype(BF16)
    grad_mixed = grad_mixed.reshape(seq_count, part, ctx_size, lanes)

    output_grad = dot(mixed_low, grad_attended, (0, 0)).astype(BF16)
    output_grad = output_grad.reshape(ctx_size, lanes, width)
    output_grad = jnp.concatenate(
        [chosen(output_grad, place ^ r, 0) for r in range(ctx_size)], axis=0
    ).reshape(sizes["z"], 2, sizes["x"], 2, share, width)
    output_grad = halve(output_grad, 3, "c").astype(BF16)
    output_grad = halve(output_grad, 2, "x").astype(BF16)
    output_grad = halve(output_grad, 1, "y")
    output_owned = z_scatter(output_grad)

    project_parts = []
    work_parts = []
    sum_parts = []
    for index in range(CHUNKS):
        at = slice(index * seq_count // CHUNKS, (index + 1) * seq_count // CHUNKS)
        grads = [grad_mixed[at, :, 0]] + [hop(grad_mixed[at, :, r], r) for r in (1, 2, 3)]
        grad_part, r0, r1, r2, r3, sums = attend_back(
            saved[index],
            grads,
            full_project,
            seg_key[at],
            seg_query[at],
            [],
        )
        across = r2 + swap(r3).astype(F32)
        work_parts.append(
            grad_hidden[index * rows_count // CHUNKS : (index + 1) * rows_count // CHUNKS]
            .reshape(r0.shape)
            + r0
            + swap(r1).astype(F32)
            + hop(across.astype(BF16), 2).astype(F32)
        )
        project_parts.append(grad_part)
        sum_parts.append(sums)
    project_grad = sum(
        dot(all_rows, grad_part.reshape(-1, 3 * lanes), (0, 0))
        for all_rows, grad_part in zip(kept_rows, project_parts)
    )
    grad_work = jnp.concatenate(work_parts, axis=0)
    project_owned = z_scatter(
        halve(
            project_grad.astype(BF16).reshape(sizes["z"], 2, ctx_size * share, 3 * lanes), 1, "y"
        )
    )
    project_owned = lax.all_to_all(
        project_owned.reshape(ctx_size, share, 3, lanes), CTX, 0, 2, tiled=False
    ).reshape(share, 3 * width)
    expand_pieces = own_hidden // PIECE
    far_rows = jnp.swapaxes(
        weight_owned[:expand_pieces].reshape(expand_pieces, 2, share, PIECE), 0, 1
    )
    expand_owned = by_core(
        jnp.swapaxes(chosen(far_rows, core, 0), 0, 1).reshape(share, chips, -1),
        jnp.swapaxes(swap(chosen(far_rows, 1 - core, 0)), 0, 1).reshape(share, chips, -1),
        2,
    ).reshape(share, hidden)
    reduce_owned = jnp.swapaxes(
        weight_owned[expand_pieces:].reshape(2, width // PIECE, 2 * share, PIECE), 1, 2
    ).reshape(4 * share, width)

    column_sums = jnp.sum(jnp.concatenate(sum_parts, axis=0), axis=(0, 1))
    zeros = jnp.zeros((width,), F32)
    grad_vectors = (
        lax.dynamic_update_slice_in_dim(zeros, column_sums[:lanes], place * lanes, 0),
        lax.dynamic_update_slice_in_dim(zeros, column_sums[2 * lanes :], place * lanes, 0),
        output_bias_grad,
        grad_gain_one,
        grad_shift_one,
        reduce_bias_grad,
        grad_gain_two,
        grad_shift_two,
    )
    hidden_sums = expand_bias_grad.reshape(chips, 1, own_hidden // chips)
    hidden_sums = jnp.where(
        low_core,
        jnp.concatenate([hidden_sums, jnp.zeros_like(hidden_sums)], axis=1),
        jnp.concatenate([jnp.zeros_like(hidden_sums), hidden_sums], axis=1),
    )
    packed_grads = jnp.concatenate(
        [vector.reshape(everyone, share) for vector in grad_vectors]
        + [hidden_sums.reshape(everyone, -1)],
        axis=1,
    )
    packed_grads = packed_grads.reshape(sizes["z"], 2, sizes["x"], 2, vector_count)
    for axis, name in ((3, "c"), (2, "x"), (1, "y")):
        packed_grads = halve(packed_grads, axis, name)
    owned = z_scatter(packed_grads, F32)
    small = [owned[i * share : (i + 1) * share] for i in range(8)]
    return (
        layer_work,
        grad_work,
        project_owned.astype(F32),
        small[0],
        small[1],
        output_owned.astype(F32),
        small[2],
        small[3],
        small[4],
        expand_owned.astype(F32),
        owned[8 * share :],
        reduce_owned.astype(F32),
        small[5],
        small[6],
        small[7],
    )


def solution(mesh):
    seq_size, ctx_size = mesh.shape["seq"], mesh.shape["ctx"]
    sizes = {"z": seq_size // 2, "y": 2, "x": ctx_size // 2, "c": 2}
    fine = Mesh(mesh.devices.reshape(tuple(sizes.values())), tuple(sizes))
    rows = P(SEQ, CTX, None)
    matrix = P(ALL, None)
    vector = P(ALL)
    return jax.shard_map(
        functools.partial(on_device, sizes),
        mesh=fine,
        in_specs=(
            rows,
            P(SEQ, None),
            matrix,
            vector,
            vector,
            matrix,
            vector,
            vector,
            vector,
            matrix,
            vector,
            matrix,
            vector,
            vector,
            vector,
            rows,
        ),
        out_specs=(
            rows,
            rows,
            matrix,
            vector,
            vector,
            matrix,
            vector,
            vector,
            vector,
            matrix,
            vector,
            matrix,
            vector,
            vector,
            vector,
        ),
        check_vma=False,
    )
```

```python
import functools

import jax
import jax.numpy as jnp
from jax import lax
from jax.experimental import pallas as pl
from jax.experimental.pallas import tpu as pltpu
from jax.sharding import Mesh
from jax.sharding import PartitionSpec as P

HEADS = 16
HEAD_DIM = 64
CHUNKS = 2
PIECE = 256
MIB = 1 << 20
CHIPS = ("z", "y", "x")
SEQ = ("z", "y")
CTX = ("x", "c")
ALL = ("z", "y", "x", "c")
F32 = jnp.float32
BF16 = jnp.bfloat16
ELSEWHERE = pl.BlockSpec(memory_space=pl.ANY)


def dot(left, right, contract=(1, 0)):
    return lax.dot_general(
        left, right, (((contract[0],), (contract[1],)), ((), ())), preferred_element_type=F32
    )


def resident(shape):
    return pl.BlockSpec(shape, lambda i: (0,) * len(shape), pipeline_mode=pl.Buffered(1))


def by_row(shape):
    return pl.BlockSpec(shape, lambda i: (i,) + (0,) * (len(shape) - 1))


def softmax_down(scores, allowed):
    scores = jnp.where(allowed, scores, -1e30)
    top = jnp.max(scores, axis=0, keepdims=True)
    expo = jnp.exp(scores - top)
    total = jnp.sum(expo, axis=0, keepdims=True)
    return expo * (1.0 / total)


def head_lanes(width, head):
    lane = lax.broadcasted_iota(jnp.int32, (1, width), 1)
    return (lane // HEAD_DIM == head).astype(F32)


def attend_kernel(late, t0, t1, t2, t3, weight, bias, seg_key, seg_query, *refs):
    m0, m1, m2, m3, kept, saved = refs[late:]
    part = t0.shape[1]
    rows = jnp.concatenate([t[0] for t in (t0, t1, t2, t3)], axis=0)
    kept[0] = rows
    project = dot(rows, weight[...]) + bias[...]
    saved[0] = project.astype(BF16)
    width = project.shape[1] // 3
    queries = (project[:, :width].astype(BF16).astype(F32) * HEAD_DIM**-0.5).astype(BF16)
    keys = project[:, width : 2 * width].astype(BF16).astype(F32)
    values_t = jnp.transpose(project[:, 2 * width :]).astype(BF16)
    allowed = seg_key[0] == seg_query[0]
    mixed = []
    for head in range(width // HEAD_DIM):
        own_keys = (keys * head_lanes(width, head)).astype(BF16)
        chances = softmax_down(dot(own_keys, queries, (1, 1)), allowed)
        own_values = values_t[head * HEAD_DIM : (head + 1) * HEAD_DIM]
        mixed.append(dot(own_values, chances.astype(BF16)))
    mixed = jnp.transpose(jnp.concatenate(mixed, axis=0)).astype(BF16)
    for index, out in enumerate((m0, m1, m2, m3)):
        out[0] = mixed[index * part : (index + 1) * part]


def attend(tokens, weight, bias, seg_key, seg_query, first, after):
    count, part, depth = tokens[0].shape
    count = count // CHUNKS
    wide = weight.shape[1]
    length = 4 * part
    return pl.pallas_call(
        functools.partial(attend_kernel, len(after)),
        grid=(count,),
        in_specs=[pl.BlockSpec((1, part, depth), lambda i: (i + first, 0, 0))] * 4
        + [
            resident((depth, wide)),
            resident((1, wide)),
            by_row((1, length, 1)),
            by_row((1, 1, length)),
        ]
        + [ELSEWHERE] * len(after),
        out_specs=[by_row((1, part, wide // 3))] * 4
        + [by_row((1, length, depth)), by_row((1, length, wide))],
        out_shape=[jax.ShapeDtypeStruct((count, part, wide // 3), BF16)] * 4
        + [
            jax.ShapeDtypeStruct((count, length, depth), BF16),
            jax.ShapeDtypeStruct((count, length, wide), BF16),
        ],
        compiler_params=pltpu.CompilerParams(vmem_limit_bytes=40 * MIB),
        cost_estimate=pl.CostEstimate(
            flops=count * length * wide * (2 * depth + 16 * length // 3),
            bytes_accessed=count * length * (depth + 2 * wide) * 2,
            transcendentals=count * length * length * wide // (3 * HEAD_DIM),
        ),
        name="attend_forward",
    )(*tokens, weight, bias, seg_key, seg_query, *after)


def attend_back_kernel(late, saved, g0, g1, g2, g3, weight, seg_key, seg_query, *refs):
    grad_project, r0, r1, r2, r3, sums = refs[late:]
    part = g0.shape[1]
    width = saved.shape[2] // 3
    factor = HEAD_DIM**-0.5
    queries = (saved[0, :, :width].astype(F32) * factor).astype(BF16)
    keys = saved[0, :, width : 2 * width].astype(F32)
    values = saved[0, :, 2 * width :].astype(F32)
    keys_t = jnp.transpose(keys * factor).astype(BF16)
    grad_mixed = jnp.concatenate([g[0] for g in (g0, g1, g2, g3)], axis=0)
    allowed = seg_key[0] == seg_query[0]
    grad_queries = []
    grad_keys = None
    grad_values = None
    for head in range(width // HEAD_DIM):
        lanes = head_lanes(width, head)
        chances = softmax_down(
            dot((keys * lanes).astype(BF16), queries, (1, 1)), allowed
        )
        grad_weights = dot((values * lanes).astype(BF16), grad_mixed, (1, 1))
        inner = jnp.sum(chances * grad_weights, axis=0, keepdims=True)
        grad_scores = (chances * (grad_weights - inner)).astype(BF16)
        grad_queries.append(dot(keys_t[head * HEAD_DIM : (head + 1) * HEAD_DIM], grad_scores))
        keys_term = dot(grad_scores, queries)
        values_term = dot(chances.astype(BF16), grad_mixed)
        if head == 0:
            grad_keys, grad_values = keys_term, values_term
        else:
            here = lanes > 0.5
            grad_keys = jnp.where(here, keys_term, grad_keys)
            grad_values = jnp.where(here, values_term, grad_values)
    grad_queries = jnp.transpose(jnp.concatenate(grad_queries, axis=0))
    whole = jnp.concatenate(
        [grad_queries.astype(BF16), grad_keys.astype(BF16), grad_values.astype(BF16)], axis=1
    )
    grad_project[0] = whole
    sums[0] = jnp.sum(whole.astype(F32), axis=0, keepdims=True)
    for index, out in enumerate((r0, r1, r2, r3)):
        out[0] = dot(whole[index * part : (index + 1) * part], weight[...], (1, 1)).astype(
            out.dtype
        )


def attend_back(saved, grads, weight, seg_key, seg_query, after):
    count, part, width = grads[0].shape
    depth, wide = weight.shape
    length = 4 * part
    return pl.pallas_call(
        functools.partial(attend_back_kernel, len(after)),
        grid=(count,),
        in_specs=[by_row((1, length, wide))]
        + [by_row((1, part, width))] * 4
        + [
            resident((depth, wide)),
            by_row((1, length, 1)),
            by_row((1, 1, length)),
        ]
        + [ELSEWHERE] * len(after),
        out_specs=[by_row((1, length, wide))]
        + [by_row((1, part, depth))] * 4
        + [by_row((1, 1, wide))],
        out_shape=[jax.ShapeDtypeStruct((count, length, wide), BF16)]
        + [jax.ShapeDtypeStruct((count, part, depth), t) for t in (F32, BF16, F32, BF16)]
        + [jax.ShapeDtypeStruct((count, 1, wide), F32)],
        compiler_params=pltpu.CompilerParams(vmem_limit_bytes=48 * MIB),
        cost_estimate=pl.CostEstimate(
            flops=count * length * wide * (2 * depth + 40 * length // 3),
            bytes_accessed=count * length * (3 * depth + 3 * wide) * 2,
            transcendentals=count * length * length * wide // (3 * HEAD_DIM),
        ),
        name="attend_backward",
    )(saved, *grads, weight, seg_key, seg_query, *after)


def column(shape):
    return pl.BlockSpec(shape, lambda i: (0, i))


def flat(block):
    wide = block.shape[-1]
    if block.shape[-2] % 16:
        return block.astype(F32).reshape(-1, wide).astype(BF16)
    return block.reshape(-1, wide)


def expand_piece(ref):
    return jnp.concatenate([flat(ref[:, i]) for i in range(ref.shape[1])], axis=1)


def reduce_piece(ref):
    columns = ref.shape[1] // 2
    halves = [
        jnp.concatenate([ref[:, half * columns + i] for i in range(columns)], axis=2)
        for half in range(2)
    ]
    return flat(jnp.concatenate(halves, axis=1))


def feed_kernel(*refs):
    sources, (expand, bias, reduce, act, slope, own_out, other_out, far_sum) = (
        refs[: 2 * CHUNKS],
        refs[2 * CHUNKS :],
    )
    step = pl.program_id(0)
    block = sources[0].shape[0]

    @pl.when(step == 0)
    def _():
        own_out[...] = jnp.zeros_like(own_out)
        far_sum[...] = jnp.zeros_like(far_sum)

    into = expand_piece(expand)
    back = reduce_piece(reduce)
    ahead = dot(sources[0][...], into) + bias[...]
    for index in range(2 * CHUNKS):
        inside = ahead
        if index + 1 < 2 * CHUNKS:
            ahead = dot(sources[index + 1][...], into) + bias[...]
        total = own_out if index < CHUNKS else far_sum
        at = slice(index % CHUNKS * block, (index % CHUNKS + 1) * block)
        to = slice(index * block, (index + 1) * block)
        square = inside * inside
        curve = jnp.tanh(inside * (0.7978845608028654 + 0.7978845608028654 * 0.044715 * square))
        half = 0.5 * curve + 0.5
        active = (inside * half).astype(BF16)
        act[to] = active
        tilt = 0.7978845608028654 * 0.5 + 0.7978845608028654 * 1.5 * 0.044715 * square
        slope[to] = (half + inside * (1.0 - curve * curve) * tilt).astype(BF16)
        total[at] += dot(active, back)

    @pl.when(step == pl.num_programs(0) - 1)
    def _():
        other_out[...] = far_sum[...].astype(BF16)


def feed_weights(weights, pieces, columns):
    chips, _, rows, _ = weights.shape
    return [
        pl.BlockSpec((chips, pieces, rows, PIECE), lambda i: (0, i, 0, 0)),
        pl.BlockSpec(
            (pieces * PIECE // (2 * rows), 2 * columns, rows, PIECE), lambda i: (i, 1, 0, 0)
        ),
    ]


def feed(own, other, weights, bias):
    block, depth = own[0].shape
    rows = CHUNKS * block
    hidden = bias.shape[1]
    pieces = 2
    wide = pieces * PIECE
    expand_spec, reduce_spec = feed_weights(weights, pieces, depth // PIECE)
    return pl.pallas_call(
        feed_kernel,
        grid=(hidden // wide,),
        in_specs=[resident((block, depth))] * (2 * CHUNKS)
        + [expand_spec, column((1, wide)), reduce_spec],
        out_specs=[column((2 * rows, wide))] * 2 + [resident((rows, depth))] * 2,
        out_shape=[jax.ShapeDtypeStruct((2 * rows, hidden), BF16)] * 2
        + [
            jax.ShapeDtypeStruct((rows, depth), F32),
            jax.ShapeDtypeStruct((rows, depth), BF16),
        ],
        scratch_shapes=[pltpu.VMEM((rows, depth), F32)],
        compiler_params=pltpu.CompilerParams(vmem_limit_bytes=56 * MIB),
        cost_estimate=pl.CostEstimate(
            flops=8 * rows * depth * hidden,
            bytes_accessed=4 * rows * (2 * hidden + 3 * depth),
            transcendentals=2 * rows * hidden,
        ),
        name="feed_forward",
    )(*own, *other, weights, bias, weights)


def feed_back_kernel(*refs):
    grads, sources = refs[: 2 * CHUNKS], refs[2 * CHUNKS : 4 * CHUNKS]
    act, slope, expand, reduce, weight_grad, bias_grad, own_out, other_out, far_sum, inside = refs[
        4 * CHUNKS :
    ]
    step = pl.program_id(0)
    block = grads[0].shape[0]

    @pl.when(step == 0)
    def _():
        own_out[...] = jnp.zeros_like(own_out)
        far_sum[...] = jnp.zeros_like(far_sum)

    into = expand_piece(expand)
    back = reduce_piece(reduce)
    bias_sum = jnp.zeros(bias_grad.shape, F32)
    for index in range(2 * CHUNKS):
        total = own_out if index < CHUNKS else far_sum
        at = slice(index % CHUNKS * block, (index % CHUNKS + 1) * block)
        to = slice(index * block, (index + 1) * block)
        grad_act = dot(grads[index][...], back, (1, 1))
        part = (grad_act * slope[to].astype(F32)).astype(BF16)
        inside[to] = part
        bias_sum += jnp.sum(part.astype(F32), axis=0, keepdims=True)
        total[at] += dot(part, into, (1, 1))
    bias_grad[...] = bias_sum
    chips, pieces, height, _ = weight_grad.shape
    columns = pieces // 4
    reduce_grad = sum(
        dot(act[i * block : (i + 1) * block], grad[...], (0, 0)) for i, grad in enumerate(grads)
    )
    count = PIECE // (2 * height)
    reduce_grad = reduce_grad.reshape(count, 2 * height, reduce_grad.shape[1]).astype(BF16)
    mine = pl.ds(step * count, count)
    for half in range(2):
        for i in range(columns):
            weight_grad[mine, (2 + half) * columns + i] = reduce_grad[
                :, half * height : (half + 1) * height, i * PIECE : (i + 1) * PIECE
            ]
    flipped = sum(
        dot(inside[i * block : (i + 1) * block], source[...], (0, 0))
        for i, source in enumerate(sources)
    )
    expand_grad = jnp.transpose(flipped).reshape(chips, height, PIECE).astype(BF16)
    weight_grad[:, step] = expand_grad

    @pl.when(step == pl.num_programs(0) - 1)
    def _():
        other_out[...] = far_sum[...].astype(BF16)


def feed_back(grads, sources, act, slope, weights):
    block, depth = grads[0].shape
    rows = CHUNKS * block
    hidden = act.shape[1]
    chips, _, height, _ = weights.shape
    pieces = 2 * hidden // PIECE
    expand_spec, reduce_spec = feed_weights(weights, 1, depth // PIECE)
    return pl.pallas_call(
        feed_back_kernel,
        grid=(hidden // PIECE,),
        in_specs=[resident((block, depth))] * (4 * CHUNKS)
        + [column((2 * rows, PIECE))] * 2
        + [expand_spec, reduce_spec],
        out_specs=[
            resident((chips, pieces, height, PIECE)),
            column((1, PIECE)),
        ]
        + [resident((rows, depth))] * 2,
        out_shape=[
            jax.ShapeDtypeStruct((chips, pieces, height, PIECE), BF16),
            jax.ShapeDtypeStruct((1, hidden), F32),
            jax.ShapeDtypeStruct((rows, depth), F32),
            jax.ShapeDtypeStruct((rows, depth), BF16),
        ],
        scratch_shapes=[
            pltpu.VMEM((rows, depth), F32),
            pltpu.VMEM((2 * rows, PIECE), BF16),
        ],
        compiler_params=pltpu.CompilerParams(vmem_limit_bytes=56 * MIB),
        cost_estimate=pl.CostEstimate(
            flops=16 * rows * depth * hidden,
            bytes_accessed=4 * rows * (2 * hidden + 5 * depth) + 8 * depth * hidden,
            transcendentals=0,
        ),
        name="feed_backward",
    )(*grads, *sources, act, slope, weights, weights)


def normalize(values):
    center = values - jnp.mean(values, axis=-1, keepdims=True)
    inverse = lax.rsqrt(jnp.mean(center * center, axis=-1, keepdims=True) + 1e-05)
    return (center * inverse, inverse)


def normalize_back(incoming, scaled, inverse, gain):
    grad_scaled = incoming * gain
    mean_one = jnp.mean(grad_scaled, axis=-1, keepdims=True)
    mean_two = jnp.mean(grad_scaled * scaled, axis=-1, keepdims=True)
    return inverse * (grad_scaled - mean_one - scaled * mean_two)


def add_sums(out, *rows):
    rows = [jnp.sum(row, axis=0, keepdims=True) for row in rows]
    rows.append(jnp.zeros((out.shape[0] - len(rows), out.shape[1]), F32))
    rows = jnp.concatenate(rows, axis=0)

    @pl.when(pl.program_id(0) == 0)
    def _():
        out[...] = rows

    @pl.when(pl.program_id(0) > 0)
    def _():
        out[...] += rows


OUT_BIAS, GAIN_ONE, SHIFT_ONE, RED_BIAS, GAIN_TWO, SHIFT_TWO = (slice(i, i + 1) for i in range(2, 8))
SCALAR = pl.BlockSpec(memory_space=pltpu.SMEM)
ROW_BLOCK = 256


def row_call(kernel, name, ins, outs, arrays, rows, cost):
    return pl.pallas_call(
        kernel,
        grid=(rows // ROW_BLOCK,),
        in_specs=ins,
        out_specs=[spec for spec, _ in outs],
        out_shape=[shape for _, shape in outs],
        compiler_params=pltpu.CompilerParams(vmem_limit_bytes=48 * MIB),
        cost_estimate=pl.CostEstimate(flops=cost, bytes_accessed=rows << 14, transcendentals=rows),
        name=name,
    )(*arrays)


def row_block(width, first=0):
    return pl.BlockSpec((ROW_BLOCK, width), lambda i: (i + first, 0))


def first_norm_kernel(place, m0, m1, m2, m3, tokens, weight, vectors, low, scaled, inverse, mixed):
    total = tokens[...].astype(F32) + vectors[OUT_BIAS]
    parts = [m[...].reshape(ROW_BLOCK, -1) for m in (m0, m1, m2, m3)]
    mixed[...] = jnp.concatenate(parts, axis=1)
    for step, part in enumerate(parts):
        total += dot(part, weight[place[0] ^ step])
    scaled_one, inverse_one = normalize(total)
    scaled[...] = scaled_one
    inverse[...] = inverse_one
    low[...] = (scaled_one * vectors[GAIN_ONE] + vectors[SHIFT_ONE]).astype(BF16)


def first_norm(place, mixed, rows, weight, vectors, chunk):
    width = rows.shape[1]
    count, part, lanes = mixed[0].shape
    size = count * part
    steps = size // ROW_BLOCK
    return row_call(
        first_norm_kernel,
        "first_norm",
        [SCALAR]
        + [by_row((ROW_BLOCK // part, part, lanes))] * 4
        + [row_block(width, chunk * steps), resident(weight.shape), resident(vectors.shape)],
        [
            (row_block(width), jax.ShapeDtypeStruct((size, width), BF16)),
            (row_block(width), jax.ShapeDtypeStruct((size, width), F32)),
            (row_block(1), jax.ShapeDtypeStruct((size, 1), F32)),
            (row_block(width), jax.ShapeDtypeStruct((size, width), BF16)),
        ],
        (place, *mixed, rows, weight, vectors),
        size,
        2 * size * width * width,
    )


def second_norm_kernel(scaled, own, far, grad_out, vectors, layer, grad, low, sums):
    first = scaled[...] * vectors[GAIN_ONE] + vectors[SHIFT_ONE]
    reduced = own[...] + far[...].astype(F32) + vectors[RED_BIAS]
    scaled_two, inverse_two = normalize(first + reduced)
    layer[...] = (scaled_two * vectors[GAIN_TWO] + vectors[SHIFT_TWO]).astype(BF16)
    incoming = grad_out[...].astype(F32)
    grad_second = normalize_back(incoming, scaled_two, inverse_two, vectors[GAIN_TWO])
    grad[...] = grad_second
    low[...] = grad_second.astype(BF16)
    add_sums(sums, incoming * scaled_two, incoming, grad_second.astype(BF16).astype(F32))


def second_norm(scaled, own, far, grad_rows, vectors, chunk):
    size, width = scaled.shape
    steps = size // ROW_BLOCK
    return row_call(
        second_norm_kernel,
        "second_norm",
        [row_block(width)]
        + [row_block(width, chunk * steps)] * 3
        + [resident(vectors.shape)],
        [
            (row_block(width), jax.ShapeDtypeStruct((size, width), BF16)),
            (row_block(width), jax.ShapeDtypeStruct((size, width), F32)),
            (row_block(width), jax.ShapeDtypeStruct((size, width), BF16)),
            (resident((8, width)), jax.ShapeDtypeStruct((8, width), F32)),
        ],
        (scaled, own, far, grad_rows, vectors),
        size,
        size * width * 40,
    )


def first_back_kernel(
    place, grad, own, far, scaled, inverse, weight, vectors, hidden, low, m0, m1, m2, m3, sums
):
    incoming = grad[...] + own[...] + far[...].astype(F32)
    grad_hidden = normalize_back(incoming, scaled[...], inverse[...], vectors[GAIN_ONE])
    hidden[...] = grad_hidden
    attended = grad_hidden.astype(BF16)
    low[...] = attended
    for step, out in enumerate((m0, m1, m2, m3)):
        out[...] = dot(attended, weight[place[0] ^ step], (1, 1)).astype(BF16).reshape(out.shape)
    add_sums(sums, incoming * scaled[...], incoming, attended.astype(F32))


def first_back(place, grad, own, far, scaled, inverse, weight, vectors, chunk, part):
    size, width = grad.shape
    steps = size // ROW_BLOCK
    lanes = weight.shape[1]
    return row_call(
        first_back_kernel,
        "first_back",
        [SCALAR, row_block(width)]
        + [row_block(width, chunk * steps)] * 2
        + [row_block(width), row_block(1), resident(weight.shape), resident(vectors.shape)],
        [
            (row_block(width), jax.ShapeDtypeStruct((size, width), F32)),
            (row_block(width), jax.ShapeDtypeStruct((size, width), BF16)),
        ]
        + [
            (
                by_row((ROW_BLOCK // part, part, lanes)),
                jax.ShapeDtypeStruct((size // part, part, lanes), BF16),
            )
        ]
        * 4
        + [(resident((8, width)), jax.ShapeDtypeStruct((8, width), F32))],
        (place, grad, own, far, scaled, inverse, weight, vectors),
        size,
        2 * size * width * width,
    )


def output_grad_kernel(place, *refs):
    mixed, grads, out = refs[:CHUNKS], refs[CHUNKS:-1], refs[-1]
    lanes = out.shape[1]
    for step in range(out.shape[0]):
        at = slice(step * lanes, (step + 1) * lanes)
        out[place[0] ^ step] = sum(
            dot(m[:, at], g[...], (0, 0)) for m, g in zip(mixed, grads)
        ).astype(BF16)


def output_back(place, mixed, grads, ctx_size):
    size, width = mixed[0].shape
    shape = (ctx_size, width // ctx_size, width)
    return pl.pallas_call(
        output_grad_kernel,
        grid=(1,),
        in_specs=[SCALAR] + [resident((size, width))] * (2 * CHUNKS),
        out_specs=resident(shape),
        out_shape=jax.ShapeDtypeStruct(shape, BF16),
        compiler_params=pltpu.CompilerParams(vmem_limit_bytes=48 * MIB),
        cost_estimate=pl.CostEstimate(
            flops=2 * CHUNKS * size * width * width,
            bytes_accessed=4 * width * (width + CHUNKS * size),
            transcendentals=0,
        ),
        name="output_backward",
    )(place, *mixed, *grads)


def on_device(
    sizes,
    tokens,
    segment_ids,
    project_weight,
    query_bias,
    value_bias,
    output_weight,
    output_bias,
    first_gain,
    first_shift,
    expand_weight,
    expand_bias,
    reduce_weight,
    reduce_bias,
    second_gain,
    second_shift,
    grad_out,
):
    chips = sizes["z"] * sizes["y"] * sizes["x"]
    ctx_size = sizes["x"] * sizes["c"]
    everyone = chips * sizes["c"]
    seq_count, part, width = tokens.shape
    rows_count = seq_count * part
    hidden = expand_weight.shape[1]
    share = width // everyone
    own_hidden = hidden // 2
    lanes = width // ctx_size
    place = lax.axis_index(CTX)
    core = lax.axis_index("c")
    low_core = core == 0

    def hop(array, step):
        return lax.ppermute(array, CTX, [(i, i ^ step) for i in range(ctx_size)])

    def swap(array):
        return lax.ppermute(array, "c", [(0, 1), (1, 0)])

    def chosen(array, index, axis):
        return lax.dynamic_index_in_dim(array, index, axis, keepdims=False)

    def pair(own, other, axis, low):
        return jnp.where(
            low, jnp.stack([own, other], axis=axis), jnp.stack([other, own], axis=axis)
        )

    def by_core(own, other, axis):
        return pair(own, other, axis, low_core)

    def bit_of(name, step):
        return (lax.axis_index(name) // step) % 2

    def trade(array, name, step=1):
        return lax.ppermute(array, name, [(i, i ^ step) for i in range(sizes[name])])

    def widen(array, name, axis=0, step=1):
        return pair(array, trade(array, name, step), axis, bit_of(name, step) == 0)

    def halve(array, axis, name, step=1):
        me = bit_of(name, step)
        return chosen(array, me, axis).astype(F32) + trade(
            chosen(array, 1 - me, axis), name, step
        ).astype(F32)

    z_steps = [1 << i for i in range(sizes["z"].bit_length() - 1)]

    def z_gather(array):
        for index, step in enumerate(z_steps[::-1]):
            array = widen(array, "z", index, step)
        return array

    def z_scatter(blocks, kind=BF16):
        for step in z_steps:
            blocks = blocks.reshape((blocks.shape[0] // 2, 2) + blocks.shape[1:])
            blocks = halve(blocks.astype(kind), 1, "z", step)
        return blocks[0]

    seg_parts = segment_ids.reshape(seq_count, ctx_size, part)
    seg = jnp.concatenate([chosen(seg_parts, place ^ r, 1) for r in range(ctx_size)], axis=1)
    seg_key = seg[:, :, None]
    seg_query = seg[:, None, :]

    vectors = (
        query_bias,
        value_bias,
        output_bias,
        first_gain,
        first_shift,
        reduce_bias,
        second_gain,
        second_shift,
        expand_bias,
    )
    vector_count = 8 * share + expand_bias.shape[0]
    blocks = project_weight.reshape(share, 3, ctx_size, lanes)
    own_vectors = jnp.concatenate(vectors)
    below = 16 * -(-ctx_size * vector_count // (48 * lanes))
    held = jnp.concatenate(
        [
            jnp.moveaxis(blocks, 2, 0).reshape(ctx_size, -1),
            jnp.broadcast_to(own_vectors, (ctx_size, vector_count)),
        ],
        axis=1,
    )
    held = lax.all_to_all(held, CTX, 0, 0, tiled=True)
    sent, held = lax.optimization_barrier((tokens, held))
    across = hop(sent, 2)
    gathered = (tokens, swap(sent), across, swap(across))
    mine = held[:, : share * 3 * lanes].reshape(ctx_size * share, 3 * lanes)
    vector_rows = jnp.pad(
        held[:, share * 3 * lanes :].reshape(-1),
        (0, below * 3 * lanes - ctx_size * vector_count),
    ).reshape(below, 3 * lanes)
    out_rows = share * width // (3 * lanes)
    out_pad = -out_rows % 16
    out_flat = jnp.pad(output_weight.reshape(-1), (0, 3 * lanes * (out_rows + out_pad) - share * width))
    both_out = widen(out_flat.reshape(-1, 3 * lanes), "x")
    whole_project = lax.all_gather(
        jnp.concatenate([mine, vector_rows, both_out.reshape(-1, 3 * lanes)]), SEQ, axis=0
    )
    first_rows = ctx_size * share + below
    full_project = whole_project[:, : ctx_size * share].reshape(width, 3 * lanes)
    out_half = (
        whole_project[:, first_rows:]
        .reshape(chips, -1)[:, : share * width]
        .reshape(chips, share, width)
    )
    full_output = by_core(out_half, swap(out_half), 1).reshape(ctx_size, lanes, width)
    packed = (
        whole_project[:, ctx_size * share : first_rows]
        .reshape(-1, below * 3 * lanes)[:, : ctx_size * vector_count]
        .reshape(everyone, vector_count)
        .astype(F32)
    )
    vectors = jnp.swapaxes(packed[:, : 8 * share].reshape(everyone, 8, share), 0, 1).reshape(
        8, width
    )
    full_query, full_value = vectors[0], vectors[1]
    exp_bias = chosen(packed[:, 8 * share :].reshape(chips, 2, -1), core, 1).reshape(1, own_hidden)
    bias_all = jnp.concatenate(
        [
            lax.dynamic_slice_in_dim(full_query, place * lanes, lanes),
            jnp.zeros((lanes,), F32),
            lax.dynamic_slice_in_dim(full_value, place * lanes, lanes),
        ]
    )[None]

    columns = expand_weight.reshape(share, chips, 2, own_hidden // chips)
    own_columns = chosen(columns, core, 2).reshape(share, own_hidden)
    far_columns = chosen(columns, 1 - core, 2).reshape(share, own_hidden)
    both = by_core(own_columns, swap(far_columns), 0)

    def in_pieces(array):
        rows_of, wide = array.shape
        return jnp.swapaxes(array.reshape(rows_of, wide // PIECE, PIECE), 0, 1).reshape(
            -1, 2 * share, PIECE
        )

    own_pieces = jnp.concatenate(
        [
            in_pieces(both.reshape(2 * share, own_hidden)),
            jnp.swapaxes(
                reduce_weight.reshape(2, 2 * share, width // PIECE, PIECE), 1, 2
            ).reshape(-1, 2 * share, PIECE),
        ]
    )
    weights = lax.all_gather(widen(own_pieces, "x"), SEQ, axis=0).reshape(
        chips, -1, 2 * share, PIECE
    )

    rows = tokens.reshape(rows_count, width)
    where = place.reshape(1).astype(jnp.int32)
    seqs = seq_count // CHUNKS
    saved, kept_rows, mixed_low, first_low, scaled_one, inverse_one = [], [], [], [], [], []
    for index in range(CHUNKS):
        at = slice(index * seqs, (index + 1) * seqs)
        *mixed, all_rows, kept = attend(
            gathered, full_project, bias_all, seg_key[at], seg_query[at], at.start, []
        )
        kept_rows.append(all_rows.reshape(-1, width))
        saved.append(kept)
        arrived = [mixed[0]] + [hop(mixed[r], r) for r in (1, 2, 3)]
        low, scaled, inverse, joined = first_norm(
            where, arrived, rows, full_output, vectors, index
        )
        mixed_low.append(joined)
        first_low.append(low)
        scaled_one.append(scaled)
        inverse_one.append(inverse)
    first_far = [swap(low) for low in first_low]
    act, slope, own_sum, far_sum = feed(first_low, first_far, weights, exp_bias)
    far_sum = swap(far_sum)

    grad_rows = grad_out.reshape(rows_count, width)
    layer_parts, grad_second, grad_reduced, second_sums = zip(
        *(
            second_norm(scaled_one[index], own_sum, far_sum, grad_rows, vectors, index)
            for index in range(CHUNKS)
        )
    )
    layer_work = jnp.concatenate(layer_parts, axis=0).reshape(tokens.shape)
    weight_grad, expand_bias_grad, own_back, far_back = feed_back(
        grad_reduced + tuple(swap(grad) for grad in grad_reduced),
        first_low + first_far,
        act,
        slope,
        weights,
    )
    weight_owned = lax.psum_scatter(
        weight_grad.reshape((-1, sizes["x"]) + weight_grad.shape[1:]),
        SEQ,
        scatter_dimension=0,
        tiled=True,
    )[0]
    far_back = swap(far_back)
    grad_hidden, grad_attended, grad_mixed, first_sums = [], [], [], []
    for index in range(CHUNKS):
        grad, low, *mixed, sums = first_back(
            where,
            grad_second[index],
            own_back,
            far_back,
            scaled_one[index],
            inverse_one[index],
            full_output,
            vectors,
            index,
            part,
        )
        grad_hidden.append(grad.reshape(seqs, part, width))
        grad_attended.append(low)
        grad_mixed.append([mixed[0]] + [hop(mixed[r], r) for r in (1, 2, 3)])
        first_sums.append(sums)
    output_grad = output_back(where, mixed_low, grad_attended, ctx_size).reshape(
        sizes["z"], 2, sizes["x"], 2, share, width
    )
    output_grad = halve(output_grad, 3, "c").astype(BF16)
    output_grad = halve(output_grad, 2, "x").astype(BF16)
    output_grad = halve(output_grad, 1, "y")
    output_owned = z_scatter(output_grad)

    project_parts = []
    work_parts = []
    sum_parts = []
    for index in range(CHUNKS):
        at = slice(index * seq_count // CHUNKS, (index + 1) * seq_count // CHUNKS)
        grad_part, r0, r1, r2, r3, sums = attend_back(
            saved[index],
            grad_mixed[index],
            full_project,
            seg_key[at],
            seg_query[at],
            [],
        )
        across = r2 + swap(r3).astype(F32)
        work_parts.append(
            grad_hidden[index]
            + r0
            + swap(r1).astype(F32)
            + hop(across.astype(BF16), 2).astype(F32)
        )
        project_parts.append(grad_part)
        sum_parts.append(sums)
    project_grad = sum(
        dot(all_rows, grad_part.reshape(-1, 3 * lanes), (0, 0))
        for all_rows, grad_part in zip(kept_rows, project_parts)
    )
    grad_work = jnp.concatenate(work_parts, axis=0)
    project_owned = z_scatter(
        halve(
            project_grad.astype(BF16).reshape(sizes["z"], 2, ctx_size * share, 3 * lanes), 1, "y"
        )
    )
    project_owned = lax.all_to_all(
        project_owned.reshape(ctx_size, share, 3, lanes), CTX, 0, 2, tiled=False
    ).reshape(share, 3 * width)
    weight_owned = halve(weight_owned, 0, "x")
    expand_pieces = own_hidden // PIECE
    far_rows = jnp.swapaxes(
        weight_owned[:expand_pieces].reshape(expand_pieces, 2, share, PIECE), 0, 1
    )
    expand_owned = by_core(
        jnp.swapaxes(chosen(far_rows, core, 0), 0, 1).reshape(share, chips, -1),
        jnp.swapaxes(swap(chosen(far_rows, 1 - core, 0)), 0, 1).reshape(share, chips, -1),
        2,
    ).reshape(share, hidden)
    reduce_owned = jnp.swapaxes(
        weight_owned[expand_pieces:].reshape(2, width // PIECE, 2 * share, PIECE), 1, 2
    ).reshape(4 * share, width)

    column_sums = jnp.sum(jnp.concatenate(sum_parts, axis=0), axis=(0, 1))
    zeros = jnp.zeros((width,), F32)
    first_sums, second_sums = sum(first_sums), sum(second_sums)
    grad_vectors = (
        lax.dynamic_update_slice_in_dim(zeros, column_sums[:lanes], place * lanes, 0),
        lax.dynamic_update_slice_in_dim(zeros, column_sums[2 * lanes :], place * lanes, 0),
        first_sums[2],
        first_sums[0],
        first_sums[1],
        second_sums[2],
        second_sums[0],
        second_sums[1],
    )
    hidden_sums = expand_bias_grad.reshape(chips, 1, own_hidden // chips)
    hidden_sums = jnp.where(
        low_core,
        jnp.concatenate([hidden_sums, jnp.zeros_like(hidden_sums)], axis=1),
        jnp.concatenate([jnp.zeros_like(hidden_sums), hidden_sums], axis=1),
    )
    packed_grads = jnp.concatenate(
        [vector.reshape(everyone, share) for vector in grad_vectors]
        + [hidden_sums.reshape(everyone, -1)],
        axis=1,
    )
    packed_grads = packed_grads.reshape(sizes["z"], 2, sizes["x"], 2, vector_count)
    for axis, name in ((3, "c"), (2, "x"), (1, "y")):
        packed_grads = halve(packed_grads, axis, name)
    owned = z_scatter(packed_grads, F32)
    small = [owned[i * share : (i + 1) * share] for i in range(8)]
    return (
        layer_work,
        grad_work,
        project_owned.astype(F32),
        small[0],
        small[1],
        output_owned.astype(F32),
        small[2],
        small[3],
        small[4],
        expand_owned.astype(F32),
        owned[8 * share :],
        reduce_owned.astype(F32),
        small[5],
        small[6],
        small[7],
    )


def solution(mesh):
    seq_size, ctx_size = mesh.shape["seq"], mesh.shape["ctx"]
    sizes = {"z": seq_size // 2, "y": 2, "x": ctx_size // 2, "c": 2}
    fine = Mesh(mesh.devices.reshape(tuple(sizes.values())), tuple(sizes))
    rows = P(SEQ, CTX, None)
    matrix = P(ALL, None)
    vector = P(ALL)
    return jax.shard_map(
        functools.partial(on_device, sizes),
        mesh=fine,
        in_specs=(
            rows,
            P(SEQ, None),
            matrix,
            vector,
            vector,
            matrix,
            vector,
            vector,
            vector,
            matrix,
            vector,
            matrix,
            vector,
            vector,
            vector,
            rows,
        ),
        out_specs=(
            rows,
            rows,
            matrix,
            vector,
            vector,
            matrix,
            vector,
            vector,
            vector,
            matrix,
            vector,
            matrix,
            vector,
            vector,
            vector,
        ),
        check_vma=False,
    )
```

```python
import functools

import jax
import jax.numpy as jnp
from jax import lax
from jax.experimental import pallas as pl
from jax.experimental.pallas import tpu as pltpu
from jax.sharding import Mesh
from jax.sharding import PartitionSpec as P

HEADS = 16
HEAD_DIM = 64
CHUNKS = 2
PIECE = 256
MIB = 1 << 20
CHIPS = ("z", "y", "x")
SEQ = ("z", "y")
CTX = ("x", "c")
ALL = ("z", "y", "x", "c")
F32 = jnp.float32
BF16 = jnp.bfloat16
ELSEWHERE = pl.BlockSpec(memory_space=pl.ANY)


def dot(left, right, contract=(1, 0)):
    return lax.dot_general(
        left, right, (((contract[0],), (contract[1],)), ((), ())), preferred_element_type=F32
    )


def resident(shape):
    return pl.BlockSpec(shape, lambda i: (0,) * len(shape), pipeline_mode=pl.Buffered(1))


def by_row(shape):
    return pl.BlockSpec(shape, lambda i: (i,) + (0,) * (len(shape) - 1))


def flat(block):
    wide = block.shape[-1]
    if block.shape[-2] % 16:
        return block.astype(F32).reshape(-1, wide).astype(BF16)
    return block.reshape(-1, wide)


def hold_kernel(source, *refs):
    refs[-1][...] = source[...]


def hold(array, after):
    return pl.pallas_call(
        hold_kernel,
        grid=(1,),
        in_specs=[resident(array.shape)] + [ELSEWHERE] * len(after),
        out_specs=resident(array.shape),
        out_shape=jax.ShapeDtypeStruct(array.shape, array.dtype),
        compiler_params=pltpu.CompilerParams(vmem_limit_bytes=16 * MIB),
        name="hold",
    )(array, *after)


def softmax_down(scores, allowed):
    scores = jnp.where(allowed, scores, -1e30)
    top = jnp.max(scores, axis=0, keepdims=True)
    expo = jnp.exp(scores - top)
    total = jnp.sum(expo, axis=0, keepdims=True)
    return expo * (1.0 / total)


def head_lanes(width, head):
    lane = lax.broadcasted_iota(jnp.int32, (1, width), 1)
    return (lane // HEAD_DIM == head).astype(F32)


def attend_kernel(late, t0, t1, t2, t3, wq, wk, wv, bias, seg_key, seg_query, *refs):
    m0, m1, m2, m3, kept, saved = refs[late:]
    part = t0.shape[1]
    rows = jnp.concatenate([t[0] for t in (t0, t1, t2, t3)], axis=0)
    kept[0] = rows
    width = wq.shape[2]
    queries, keys, values = [
        dot(rows, flat(w[...])) + bias[:, i * width : (i + 1) * width]
        for i, w in enumerate((wq, wk, wv))
    ]
    for i, part_of in enumerate((queries, keys, values)):
        saved[0, :, i * width : (i + 1) * width] = part_of.astype(BF16)
    queries = (queries.astype(BF16).astype(F32) * HEAD_DIM**-0.5).astype(BF16)
    keys = keys.astype(BF16).astype(F32)
    values_t = jnp.transpose(values).astype(BF16)
    allowed = seg_key[0] == seg_query[0]
    mixed = []
    for head in range(width // HEAD_DIM):
        own_keys = (keys * head_lanes(width, head)).astype(BF16)
        chances = softmax_down(dot(own_keys, queries, (1, 1)), allowed)
        own_values = values_t[head * HEAD_DIM : (head + 1) * HEAD_DIM]
        mixed.append(dot(own_values, chances.astype(BF16)))
    mixed = jnp.transpose(jnp.concatenate(mixed, axis=0)).astype(BF16)
    for index, out in enumerate((m0, m1, m2, m3)):
        out[0] = mixed[index * part : (index + 1) * part]


def project_specs(weight, depth):
    shape = (weight.shape[0], depth // weight.shape[0], weight.shape[2])
    return [
        pl.BlockSpec(shape, lambda i, j=j: (0, j, 0), pipeline_mode=pl.Buffered(1))
        for j in range(3)
    ]


def attend(tokens, weight, bias, seg_key, seg_query, first, after):
    count, part, depth = tokens[0].shape
    count = count // CHUNKS
    wide = bias.shape[1]
    length = 4 * part
    return pl.pallas_call(
        functools.partial(attend_kernel, len(after)),
        grid=(count,),
        in_specs=[pl.BlockSpec((1, part, depth), lambda i: (i + first, 0, 0))] * 4
        + project_specs(weight, depth)
        + [
            resident((1, wide)),
            by_row((1, length, 1)),
            by_row((1, 1, length)),
        ]
        + [ELSEWHERE] * len(after),
        out_specs=[by_row((1, part, wide // 3))] * 4
        + [by_row((1, length, depth)), by_row((1, length, wide))],
        out_shape=[jax.ShapeDtypeStruct((count, part, wide // 3), BF16)] * 4
        + [
            jax.ShapeDtypeStruct((count, length, depth), BF16),
            jax.ShapeDtypeStruct((count, length, wide), BF16),
        ],
        compiler_params=pltpu.CompilerParams(vmem_limit_bytes=40 * MIB),
        cost_estimate=pl.CostEstimate(
            flops=count * length * wide * (2 * depth + 16 * length // 3),
            bytes_accessed=count * length * (depth + 2 * wide) * 2,
            transcendentals=count * length * length * wide // (3 * HEAD_DIM),
        ),
        name="attend_forward",
    )(*tokens, weight, weight, weight, bias, seg_key, seg_query, *after)


def attend_back_kernel(late, saved, g0, g1, g2, g3, wq, wk, wv, seg_key, seg_query, *refs):
    grad_project, r0, r1, r2, r3, sums = refs[late:]
    part = g0.shape[1]
    width = saved.shape[2] // 3
    factor = HEAD_DIM**-0.5
    queries = (saved[0, :, :width].astype(F32) * factor).astype(BF16)
    keys = saved[0, :, width : 2 * width].astype(F32)
    values = saved[0, :, 2 * width :].astype(F32)
    keys_t = jnp.transpose(keys * factor).astype(BF16)
    grad_mixed = jnp.concatenate([g[0] for g in (g0, g1, g2, g3)], axis=0)
    allowed = seg_key[0] == seg_query[0]
    grad_queries = []
    grad_keys = None
    grad_values = None
    for head in range(width // HEAD_DIM):
        lanes = head_lanes(width, head)
        chances = softmax_down(
            dot((keys * lanes).astype(BF16), queries, (1, 1)), allowed
        )
        grad_weights = dot((values * lanes).astype(BF16), grad_mixed, (1, 1))
        inner = jnp.sum(chances * grad_weights, axis=0, keepdims=True)
        grad_scores = (chances * (grad_weights - inner)).astype(BF16)
        grad_queries.append(dot(keys_t[head * HEAD_DIM : (head + 1) * HEAD_DIM], grad_scores))
        keys_term = dot(grad_scores, queries)
        values_term = dot(chances.astype(BF16), grad_mixed)
        if head == 0:
            grad_keys, grad_values = keys_term, values_term
        else:
            here = lanes > 0.5
            grad_keys = jnp.where(here, keys_term, grad_keys)
            grad_values = jnp.where(here, values_term, grad_values)
    grad_queries = jnp.transpose(jnp.concatenate(grad_queries, axis=0))
    terms = [grad_queries.astype(BF16), grad_keys.astype(BF16), grad_values.astype(BF16)]
    for i, term in enumerate(terms):
        grad_project[0, :, i * width : (i + 1) * width] = term
        sums[0, :, i * width : (i + 1) * width] = jnp.sum(
            term.astype(F32), axis=0, keepdims=True
        )
    rows = sum(dot(term, flat(w[...]), (1, 1)) for term, w in zip(terms, (wq, wk, wv)))
    for index, out in enumerate((r0, r1, r2, r3)):
        out[0] = rows[index * part : (index + 1) * part].astype(out.dtype)


def attend_back(saved, grads, weight, seg_key, seg_query, after):
    count, part, width = grads[0].shape
    depth, wide = width * 4, width * 3
    length = 4 * part
    return pl.pallas_call(
        functools.partial(attend_back_kernel, len(after)),
        grid=(count,),
        in_specs=[by_row((1, length, wide))]
        + [by_row((1, part, width))] * 4
        + project_specs(weight, depth)
        + [
            by_row((1, length, 1)),
            by_row((1, 1, length)),
        ]
        + [ELSEWHERE] * len(after),
        out_specs=[by_row((1, length, wide))]
        + [by_row((1, part, depth))] * 4
        + [by_row((1, 1, wide))],
        out_shape=[jax.ShapeDtypeStruct((count, length, wide), BF16)]
        + [jax.ShapeDtypeStruct((count, part, depth), t) for t in (F32, BF16, F32, BF16)]
        + [jax.ShapeDtypeStruct((count, 1, wide), F32)],
        compiler_params=pltpu.CompilerParams(vmem_limit_bytes=48 * MIB),
        cost_estimate=pl.CostEstimate(
            flops=count * length * wide * (2 * depth + 40 * length // 3),
            bytes_accessed=count * length * (3 * depth + 3 * wide) * 2,
            transcendentals=count * length * length * wide // (3 * HEAD_DIM),
        ),
        name="attend_backward",
    )(saved, *grads, weight, weight, weight, seg_key, seg_query, *after)


def column(shape):
    return pl.BlockSpec(shape, lambda i: (0, i))


def expand_piece(ref):
    return jnp.concatenate([flat(ref[:, i]) for i in range(ref.shape[1])], axis=1)


def reduce_piece(ref):
    columns = ref.shape[1] // 2
    halves = [
        jnp.concatenate([ref[:, half * columns + i] for i in range(columns)], axis=2)
        for half in range(2)
    ]
    return flat(jnp.concatenate(halves, axis=1))


def feed_kernel(*refs):
    sources, (expand, bias, reduce, act, slope, own_out, other_out, far_sum) = (
        refs[: 2 * CHUNKS],
        refs[2 * CHUNKS :],
    )
    step = pl.program_id(0)
    block = sources[0].shape[0]

    @pl.when(step == 0)
    def _():
        own_out[...] = jnp.zeros_like(own_out)
        far_sum[...] = jnp.zeros_like(far_sum)

    into = expand_piece(expand)
    back = reduce_piece(reduce)
    ahead = dot(sources[0][...], into) + bias[...]
    for index in range(2 * CHUNKS):
        inside = ahead
        if index + 1 < 2 * CHUNKS:
            ahead = dot(sources[index + 1][...], into) + bias[...]
        total = own_out if index < CHUNKS else far_sum
        at = slice(index % CHUNKS * block, (index % CHUNKS + 1) * block)
        to = slice(index * block, (index + 1) * block)
        square = inside * inside
        curve = jnp.tanh(inside * (0.7978845608028654 + 0.7978845608028654 * 0.044715 * square))
        half = 0.5 * curve + 0.5
        active = (inside * half).astype(BF16)
        act[to] = active
        tilt = 0.7978845608028654 * 0.5 + 0.7978845608028654 * 1.5 * 0.044715 * square
        slope[to] = (half + inside * (1.0 - curve * curve) * tilt).astype(BF16)
        total[at] += dot(active, back)

    @pl.when(step == pl.num_programs(0) - 1)
    def _():
        other_out[...] = far_sum[...].astype(BF16)


def feed_weights(weights, pieces, columns):
    chips, _, rows, _ = weights.shape
    return [
        pl.BlockSpec((chips, pieces, rows, PIECE), lambda i: (0, i, 0, 0)),
        pl.BlockSpec(
            (pieces * PIECE // (2 * rows), 2 * columns, rows, PIECE), lambda i: (i, 1, 0, 0)
        ),
    ]


def feed(own, other, weights, bias):
    block, depth = own[0].shape
    rows = CHUNKS * block
    hidden = bias.shape[1]
    pieces = 2
    wide = pieces * PIECE
    expand_spec, reduce_spec = feed_weights(weights, pieces, depth // PIECE)
    return pl.pallas_call(
        feed_kernel,
        grid=(hidden // wide,),
        in_specs=[resident((block, depth))] * (2 * CHUNKS)
        + [expand_spec, column((1, wide)), reduce_spec],
        out_specs=[column((2 * rows, wide))] * 2 + [resident((rows, depth))] * 2,
        out_shape=[jax.ShapeDtypeStruct((2 * rows, hidden), BF16)] * 2
        + [
            jax.ShapeDtypeStruct((rows, depth), F32),
            jax.ShapeDtypeStruct((rows, depth), BF16),
        ],
        scratch_shapes=[pltpu.VMEM((rows, depth), F32)],
        compiler_params=pltpu.CompilerParams(vmem_limit_bytes=56 * MIB),
        cost_estimate=pl.CostEstimate(
            flops=8 * rows * depth * hidden,
            bytes_accessed=4 * rows * (2 * hidden + 3 * depth),
            transcendentals=2 * rows * hidden,
        ),
        name="feed_forward",
    )(*own, *other, weights, bias, weights)


def feed_back_kernel(*refs):
    grads, sources = refs[: 2 * CHUNKS], refs[2 * CHUNKS : 4 * CHUNKS]
    act, slope, expand, reduce, weight_grad, bias_grad, own_out, other_out, far_sum, inside = refs[
        4 * CHUNKS :
    ]
    step = pl.program_id(0)
    block = grads[0].shape[0]

    @pl.when(step == 0)
    def _():
        own_out[...] = jnp.zeros_like(own_out)
        far_sum[...] = jnp.zeros_like(far_sum)

    into = expand_piece(expand)
    back = reduce_piece(reduce)
    bias_sum = jnp.zeros(bias_grad.shape, F32)
    for index in range(2 * CHUNKS):
        total = own_out if index < CHUNKS else far_sum
        at = slice(index % CHUNKS * block, (index % CHUNKS + 1) * block)
        to = slice(index * block, (index + 1) * block)
        grad_act = dot(grads[index][...], back, (1, 1))
        part = (grad_act * slope[to].astype(F32)).astype(BF16)
        inside[to] = part
        bias_sum += jnp.sum(part.astype(F32), axis=0, keepdims=True)
        total[at] += dot(part, into, (1, 1))
    bias_grad[...] = bias_sum
    chips, pieces, height, _ = weight_grad.shape
    columns = pieces // 4
    reduce_grad = sum(
        dot(act[i * block : (i + 1) * block], grad[...], (0, 0)) for i, grad in enumerate(grads)
    )
    count = PIECE // (2 * height)
    reduce_grad = reduce_grad.reshape(count, 2 * height, reduce_grad.shape[1]).astype(BF16)
    mine = pl.ds(step * count, count)
    for half in range(2):
        for i in range(columns):
            weight_grad[mine, (2 + half) * columns + i] = reduce_grad[
                :, half * height : (half + 1) * height, i * PIECE : (i + 1) * PIECE
            ]
    flipped = sum(
        dot(inside[i * block : (i + 1) * block], source[...], (0, 0))
        for i, source in enumerate(sources)
    )
    expand_grad = jnp.transpose(flipped).reshape(chips, height, PIECE).astype(BF16)
    weight_grad[:, step] = expand_grad

    @pl.when(step == pl.num_programs(0) - 1)
    def _():
        other_out[...] = far_sum[...].astype(BF16)


def feed_back(grads, sources, act, slope, weights):
    block, depth = grads[0].shape
    rows = CHUNKS * block
    hidden = act.shape[1]
    chips, _, height, _ = weights.shape
    pieces = 2 * hidden // PIECE
    expand_spec, reduce_spec = feed_weights(weights, 1, depth // PIECE)
    return pl.pallas_call(
        feed_back_kernel,
        grid=(hidden // PIECE,),
        in_specs=[resident((block, depth))] * (4 * CHUNKS)
        + [column((2 * rows, PIECE))] * 2
        + [expand_spec, reduce_spec],
        out_specs=[
            resident((chips, pieces, height, PIECE)),
            column((1, PIECE)),
        ]
        + [resident((rows, depth))] * 2,
        out_shape=[
            jax.ShapeDtypeStruct((chips, pieces, height, PIECE), BF16),
            jax.ShapeDtypeStruct((1, hidden), F32),
            jax.ShapeDtypeStruct((rows, depth), F32),
            jax.ShapeDtypeStruct((rows, depth), BF16),
        ],
        scratch_shapes=[
            pltpu.VMEM((rows, depth), F32),
            pltpu.VMEM((2 * rows, PIECE), BF16),
        ],
        compiler_params=pltpu.CompilerParams(vmem_limit_bytes=56 * MIB),
        cost_estimate=pl.CostEstimate(
            flops=16 * rows * depth * hidden,
            bytes_accessed=4 * rows * (2 * hidden + 5 * depth) + 8 * depth * hidden,
            transcendentals=0,
        ),
        name="feed_backward",
    )(*grads, *sources, act, slope, weights, weights)


def normalize(values):
    center = values - jnp.mean(values, axis=-1, keepdims=True)
    inverse = lax.rsqrt(jnp.mean(center * center, axis=-1, keepdims=True) + 1e-05)
    return (center * inverse, inverse)


def normalize_back(incoming, scaled, inverse, gain):
    grad_scaled = incoming * gain
    mean_one = jnp.mean(grad_scaled, axis=-1, keepdims=True)
    mean_two = jnp.mean(grad_scaled * scaled, axis=-1, keepdims=True)
    return inverse * (grad_scaled - mean_one - scaled * mean_two)


def add_sums(out, *rows):
    rows = [jnp.sum(row, axis=0, keepdims=True) for row in rows]
    rows.append(jnp.zeros((out.shape[0] - len(rows), out.shape[1]), F32))
    rows = jnp.concatenate(rows, axis=0)

    @pl.when(pl.program_id(0) == 0)
    def _():
        out[...] = rows

    @pl.when(pl.program_id(0) > 0)
    def _():
        out[...] += rows


OUT_BIAS, GAIN_ONE, SHIFT_ONE, RED_BIAS, GAIN_TWO, SHIFT_TWO = (slice(i, i + 1) for i in range(2, 8))
SCALAR = pl.BlockSpec(memory_space=pltpu.SMEM)
ROW_BLOCK = 256


def row_call(kernel, name, ins, outs, arrays, rows, cost):
    return pl.pallas_call(
        kernel,
        grid=(rows // ROW_BLOCK,),
        in_specs=ins,
        out_specs=[spec for spec, _ in outs],
        out_shape=[shape for _, shape in outs],
        compiler_params=pltpu.CompilerParams(vmem_limit_bytes=48 * MIB),
        cost_estimate=pl.CostEstimate(flops=cost, bytes_accessed=rows << 14, transcendentals=rows),
        name=name,
    )(*arrays)


def row_block(width, first=0):
    return pl.BlockSpec((ROW_BLOCK, width), lambda i: (i + first, 0))


def first_norm_kernel(place, m0, m1, m2, m3, tokens, weight, vectors, low, scaled, inverse, mixed):
    total = tokens[...].astype(F32) + vectors[OUT_BIAS]
    parts = [m[...].reshape(ROW_BLOCK, -1) for m in (m0, m1, m2, m3)]
    mixed[...] = jnp.concatenate(parts, axis=1)
    for step, part in enumerate(parts):
        total += dot(part, weight[place[0] ^ step])
    scaled_one, inverse_one = normalize(total)
    scaled[...] = scaled_one
    inverse[...] = inverse_one
    low[...] = (scaled_one * vectors[GAIN_ONE] + vectors[SHIFT_ONE]).astype(BF16)


def first_norm(place, mixed, rows, weight, vectors, chunk):
    width = rows.shape[1]
    count, part, lanes = mixed[0].shape
    size = count * part
    steps = size // ROW_BLOCK
    return row_call(
        first_norm_kernel,
        "first_norm",
        [SCALAR]
        + [by_row((ROW_BLOCK // part, part, lanes))] * 4
        + [row_block(width, chunk * steps), resident(weight.shape), resident(vectors.shape)],
        [
            (row_block(width), jax.ShapeDtypeStruct((size, width), BF16)),
            (row_block(width), jax.ShapeDtypeStruct((size, width), F32)),
            (row_block(1), jax.ShapeDtypeStruct((size, 1), F32)),
            (row_block(width), jax.ShapeDtypeStruct((size, width), BF16)),
        ],
        (place, *mixed, rows, weight, vectors),
        size,
        2 * size * width * width,
    )


def second_norm_kernel(scaled, own, far, grad_out, vectors, layer, grad, low, sums):
    first = scaled[...] * vectors[GAIN_ONE] + vectors[SHIFT_ONE]
    reduced = own[...] + far[...].astype(F32) + vectors[RED_BIAS]
    scaled_two, inverse_two = normalize(first + reduced)
    layer[...] = (scaled_two * vectors[GAIN_TWO] + vectors[SHIFT_TWO]).astype(BF16)
    incoming = grad_out[...].astype(F32)
    grad_second = normalize_back(incoming, scaled_two, inverse_two, vectors[GAIN_TWO])
    grad[...] = grad_second
    low[...] = grad_second.astype(BF16)
    add_sums(sums, incoming * scaled_two, incoming, grad_second.astype(BF16).astype(F32))


def second_norm(scaled, own, far, grad_rows, vectors, chunk):
    size, width = scaled.shape
    steps = size // ROW_BLOCK
    return row_call(
        second_norm_kernel,
        "second_norm",
        [row_block(width)]
        + [row_block(width, chunk * steps)] * 3
        + [resident(vectors.shape)],
        [
            (row_block(width), jax.ShapeDtypeStruct((size, width), BF16)),
            (row_block(width), jax.ShapeDtypeStruct((size, width), F32)),
            (row_block(width), jax.ShapeDtypeStruct((size, width), BF16)),
            (resident((8, width)), jax.ShapeDtypeStruct((8, width), F32)),
        ],
        (scaled, own, far, grad_rows, vectors),
        size,
        size * width * 40,
    )


def first_back_kernel(
    place, grad, own, far, scaled, inverse, weight, vectors, hidden, low, m0, m1, m2, m3, sums
):
    incoming = grad[...] + own[...] + far[...].astype(F32)
    grad_hidden = normalize_back(incoming, scaled[...], inverse[...], vectors[GAIN_ONE])
    hidden[...] = grad_hidden
    attended = grad_hidden.astype(BF16)
    low[...] = attended
    for step, out in enumerate((m0, m1, m2, m3)):
        out[...] = dot(attended, weight[place[0] ^ step], (1, 1)).astype(BF16).reshape(out.shape)
    add_sums(sums, incoming * scaled[...], incoming, attended.astype(F32))


def first_back(place, grad, own, far, scaled, inverse, weight, vectors, chunk, part):
    size, width = grad.shape
    steps = size // ROW_BLOCK
    lanes = weight.shape[1]
    return row_call(
        first_back_kernel,
        "first_back",
        [SCALAR, row_block(width)]
        + [row_block(width, chunk * steps)] * 2
        + [row_block(width), row_block(1), resident(weight.shape), resident(vectors.shape)],
        [
            (row_block(width), jax.ShapeDtypeStruct((size, width), F32)),
            (row_block(width), jax.ShapeDtypeStruct((size, width), BF16)),
        ]
        + [
            (
                by_row((ROW_BLOCK // part, part, lanes)),
                jax.ShapeDtypeStruct((size // part, part, lanes), BF16),
            )
        ]
        * 4
        + [(resident((8, width)), jax.ShapeDtypeStruct((8, width), F32))],
        (place, grad, own, far, scaled, inverse, weight, vectors),
        size,
        2 * size * width * width,
    )


def output_grad_kernel(place, *refs):
    mixed, grads, out = refs[:CHUNKS], refs[CHUNKS:-1], refs[-1]
    lanes = out.shape[1]
    for step in range(out.shape[0]):
        at = slice(step * lanes, (step + 1) * lanes)
        out[place[0] ^ step] = sum(
            dot(m[:, at], g[...], (0, 0)) for m, g in zip(mixed, grads)
        ).astype(BF16)


def output_back(place, mixed, grads, ctx_size):
    size, width = mixed[0].shape
    shape = (ctx_size, width // ctx_size, width)
    return pl.pallas_call(
        output_grad_kernel,
        grid=(1,),
        in_specs=[SCALAR] + [resident((size, width))] * (2 * CHUNKS),
        out_specs=resident(shape),
        out_shape=jax.ShapeDtypeStruct(shape, BF16),
        compiler_params=pltpu.CompilerParams(vmem_limit_bytes=48 * MIB),
        cost_estimate=pl.CostEstimate(
            flops=2 * CHUNKS * size * width * width,
            bytes_accessed=4 * width * (width + CHUNKS * size),
            transcendentals=0,
        ),
        name="output_backward",
    )(place, *mixed, *grads)


def on_device(
    sizes,
    tokens,
    segment_ids,
    project_weight,
    query_bias,
    value_bias,
    output_weight,
    output_bias,
    first_gain,
    first_shift,
    expand_weight,
    expand_bias,
    reduce_weight,
    reduce_bias,
    second_gain,
    second_shift,
    grad_out,
):
    chips = sizes["z"] * sizes["y"] * sizes["x"]
    ctx_size = sizes["x"] * sizes["c"]
    everyone = chips * sizes["c"]
    seq_count, part, width = tokens.shape
    rows_count = seq_count * part
    hidden = expand_weight.shape[1]
    share = width // everyone
    own_hidden = hidden // 2
    lanes = width // ctx_size
    place = lax.axis_index(CTX)
    core = lax.axis_index("c")
    low_core = core == 0

    def hop(array, step):
        return lax.ppermute(array, CTX, [(i, i ^ step) for i in range(ctx_size)])

    def swap(array):
        return lax.ppermute(array, "c", [(0, 1), (1, 0)])

    def chosen(array, index, axis):
        return lax.dynamic_index_in_dim(array, index, axis, keepdims=False)

    def pair(own, other, axis, low):
        return jnp.where(
            low, jnp.stack([own, other], axis=axis), jnp.stack([other, own], axis=axis)
        )

    def by_core(own, other, axis):
        return pair(own, other, axis, low_core)

    def bit_of(name, step):
        return (lax.axis_index(name) // step) % 2

    def trade(array, name, step=1):
        return lax.ppermute(array, name, [(i, i ^ step) for i in range(sizes[name])])

    def widen(array, name, axis=0, step=1):
        return pair(array, trade(array, name, step), axis, bit_of(name, step) == 0)

    def halve(array, axis, name, step=1):
        me = bit_of(name, step)
        return chosen(array, me, axis).astype(F32) + trade(
            chosen(array, 1 - me, axis), name, step
        ).astype(F32)

    z_steps = [1 << i for i in range(sizes["z"].bit_length() - 1)]

    def z_gather(array):
        for index, step in enumerate(z_steps[::-1]):
            array = widen(array, "z", index, step)
        return array

    def z_scatter(blocks, kind=BF16):
        for step in z_steps:
            blocks = blocks.reshape((blocks.shape[0] // 2, 2) + blocks.shape[1:])
            blocks = halve(blocks.astype(kind), 1, "z", step)
        return blocks[0]

    seg_parts = segment_ids.reshape(seq_count, ctx_size, part)
    seg = jnp.concatenate([chosen(seg_parts, place ^ r, 1) for r in range(ctx_size)], axis=1)
    seg_key = seg[:, :, None]
    seg_query = seg[:, None, :]

    vectors = (
        query_bias,
        value_bias,
        output_bias,
        first_gain,
        first_shift,
        reduce_bias,
        second_gain,
        second_shift,
        expand_bias,
    )
    vector_count = 8 * share + expand_bias.shape[0]
    blocks = project_weight.reshape(share, 3, ctx_size, lanes)
    own_vectors = jnp.concatenate(vectors)
    vector_row = jnp.pad(own_vectors, (0, 3 * lanes - vector_count)).reshape(1, 3, 1, lanes)
    held = jnp.concatenate(
        [
            blocks,
            jnp.broadcast_to(vector_row, (1, 3, ctx_size, lanes)),
            jnp.zeros((15, 3, ctx_size, lanes), BF16),
        ]
    )
    held = lax.all_to_all(held, CTX, 2, 0, tiled=False)
    sent, held = lax.optimization_barrier((tokens, held))
    across = hop(sent, 2)
    gathered = (tokens, swap(sent), across, swap(across))
    mine = jnp.moveaxis(held[:, :share], 2, 0).reshape(-1, lanes)
    vector_rows = held[:, share].reshape(ctx_size, 3 * lanes)[:, :vector_count].reshape(-1)
    vector_rows = jnp.pad(vector_rows, (0, 16 * lanes - vector_rows.shape[0])).reshape(16, lanes)
    out_pieces = jnp.swapaxes(output_weight.reshape(share, ctx_size, lanes), 0, 1)
    whole_project = lax.all_gather(
        jnp.concatenate(
            [mine, vector_rows, widen(out_pieces.reshape(-1, lanes), "x").reshape(-1, lanes)]
        ),
        SEQ,
        axis=0,
    )
    first_rows = mine.shape[0]
    full_project = whole_project
    out_half = jnp.swapaxes(
        whole_project[:, first_rows + 16 :].reshape(chips, ctx_size, share, lanes), 1, 2
    ).reshape(chips, share, width)
    full_output = by_core(out_half, swap(out_half), 1).reshape(ctx_size, lanes, width)
    packed = (
        whole_project[:, first_rows : first_rows + 16]
        .reshape(-1, 16 * lanes)[:, : ctx_size * vector_count]
        .reshape(everyone, vector_count)
        .astype(F32)
    )
    vectors = jnp.swapaxes(packed[:, : 8 * share].reshape(everyone, 8, share), 0, 1).reshape(
        8, width
    )
    full_query, full_value = vectors[0], vectors[1]
    exp_bias = chosen(packed[:, 8 * share :].reshape(chips, 2, -1), core, 1).reshape(1, own_hidden)
    bias_all = jnp.concatenate(
        [
            lax.dynamic_slice_in_dim(full_query, place * lanes, lanes),
            jnp.zeros((lanes,), F32),
            lax.dynamic_slice_in_dim(full_value, place * lanes, lanes),
        ]
    )[None]

    columns = expand_weight.reshape(share, chips, 2, own_hidden // chips)
    own_columns = chosen(columns, core, 2).reshape(share, own_hidden)
    far_columns = chosen(columns, 1 - core, 2).reshape(share, own_hidden)
    both = by_core(own_columns, swap(far_columns), 0)

    def in_pieces(array):
        rows_of, wide = array.shape
        return jnp.swapaxes(array.reshape(rows_of, wide // PIECE, PIECE), 0, 1).reshape(
            -1, 2 * share, PIECE
        )

    own_pieces = jnp.concatenate(
        [
            in_pieces(both.reshape(2 * share, own_hidden)),
            jnp.swapaxes(
                reduce_weight.reshape(2, 2 * share, width // PIECE, PIECE), 1, 2
            ).reshape(-1, 2 * share, PIECE),
        ]
    )
    own_pieces = hold(own_pieces, [across])
    weights = lax.all_gather(widen(own_pieces, "x"), SEQ, axis=0).reshape(
        chips, -1, 2 * share, PIECE
    )

    rows = tokens.reshape(rows_count, width)
    where = place.reshape(1).astype(jnp.int32)
    seqs = seq_count // CHUNKS
    saved, kept_rows, mixed_low, first_low, scaled_one, inverse_one = [], [], [], [], [], []
    for index in range(CHUNKS):
        at = slice(index * seqs, (index + 1) * seqs)
        *mixed, all_rows, kept = attend(
            gathered, full_project, bias_all, seg_key[at], seg_query[at], at.start, []
        )
        kept_rows.append(all_rows.reshape(-1, width))
        saved.append(kept)
        arrived = [mixed[0]] + [hop(mixed[r], r) for r in (1, 2, 3)]
        low, scaled, inverse, joined = first_norm(
            where, arrived, rows, full_output, vectors, index
        )
        mixed_low.append(joined)
        first_low.append(low)
        scaled_one.append(scaled)
        inverse_one.append(inverse)
    first_far = [swap(low) for low in first_low]
    act, slope, own_sum, far_sum = feed(first_low, first_far, weights, exp_bias)
    far_sum = swap(far_sum)

    grad_rows = grad_out.reshape(rows_count, width)
    layer_parts, grad_second, grad_reduced, second_sums = zip(
        *(
            second_norm(scaled_one[index], own_sum, far_sum, grad_rows, vectors, index)
            for index in range(CHUNKS)
        )
    )
    layer_work = jnp.concatenate(layer_parts, axis=0).reshape(tokens.shape)
    weight_grad, expand_bias_grad, own_back, far_back = feed_back(
        grad_reduced + tuple(swap(grad) for grad in grad_reduced),
        first_low + first_far,
        act,
        slope,
        weights,
    )
    weight_owned = lax.psum_scatter(
        weight_grad.reshape((-1, sizes["x"]) + weight_grad.shape[1:]),
        SEQ,
        scatter_dimension=0,
        tiled=True,
    )[0]
    far_back = swap(far_back)
    grad_hidden, grad_attended, grad_mixed, first_sums = [], [], [], []
    for index in range(CHUNKS):
        grad, low, *mixed, sums = first_back(
            where,
            grad_second[index],
            own_back,
            far_back,
            scaled_one[index],
            inverse_one[index],
            full_output,
            vectors,
            index,
            part,
        )
        grad_hidden.append(grad.reshape(seqs, part, width))
        grad_attended.append(low)
        grad_mixed.append([mixed[0]] + [hop(mixed[r], r) for r in (1, 2, 3)])
        first_sums.append(sums)
    output_grad = output_back(where, mixed_low, grad_attended, ctx_size).reshape(
        sizes["z"], 2, sizes["x"], 2, share, width
    )
    output_grad = halve(output_grad, 3, "c").astype(BF16)
    output_grad = halve(output_grad, 2, "x").astype(BF16)
    output_grad = halve(output_grad, 1, "y")
    output_owned = z_scatter(output_grad)

    project_parts = []
    work_parts = []
    across_sums = []
    work_hops = []
    sum_parts = []
    for index in range(CHUNKS):
        at = slice(index * seq_count // CHUNKS, (index + 1) * seq_count // CHUNKS)
        grad_part, r0, r1, r2, r3, sums = attend_back(
            saved[index],
            grad_mixed[index],
            full_project,
            seg_key[at],
            seg_query[at],
            across_sums[:index],
        )
        across_sums.append((r2 + swap(r3).astype(F32)).astype(BF16))
        work_hops.append(hop(across_sums[index], 2))
        work_parts.append(
            grad_hidden[index] + r0 + swap(r1).astype(F32) + work_hops[index].astype(F32)
        )
        project_parts.append(grad_part)
        sum_parts.append(sums)
    project_grad = sum(
        dot(all_rows, grad_part.reshape(-1, 3 * lanes), (0, 0))
        for all_rows, grad_part in zip(kept_rows, project_parts)
    )
    grad_work = jnp.concatenate(work_parts, axis=0)
    project_grad = hold(project_grad.astype(BF16), work_hops[:1])
    project_half = halve(
        project_grad.reshape(sizes["z"], 2, ctx_size * share, 3 * lanes), 1, "y"
    )
    project_owned = z_scatter(hold(project_half.astype(BF16), work_hops[1:]))
    project_owned = lax.all_to_all(
        project_owned.reshape(ctx_size, share, 3, lanes), CTX, 0, 2, tiled=False
    ).reshape(share, 3 * width)
    weight_owned = halve(weight_owned, 0, "x")
    expand_pieces = own_hidden // PIECE
    far_rows = jnp.swapaxes(
        weight_owned[:expand_pieces].reshape(expand_pieces, 2, share, PIECE), 0, 1
    )
    expand_owned = by_core(
        jnp.swapaxes(chosen(far_rows, core, 0), 0, 1).reshape(share, chips, -1),
        jnp.swapaxes(swap(chosen(far_rows, 1 - core, 0)), 0, 1).reshape(share, chips, -1),
        2,
    ).reshape(share, hidden)
    reduce_owned = jnp.swapaxes(
        weight_owned[expand_pieces:].reshape(2, width // PIECE, 2 * share, PIECE), 1, 2
    ).reshape(4 * share, width)

    column_sums = jnp.sum(jnp.concatenate(sum_parts, axis=0), axis=(0, 1))
    zeros = jnp.zeros((width,), F32)
    first_sums, second_sums = sum(first_sums), sum(second_sums)
    grad_vectors = (
        lax.dynamic_update_slice_in_dim(zeros, column_sums[:lanes], place * lanes, 0),
        lax.dynamic_update_slice_in_dim(zeros, column_sums[2 * lanes :], place * lanes, 0),
        first_sums[2],
        first_sums[0],
        first_sums[1],
        second_sums[2],
        second_sums[0],
        second_sums[1],
    )
    hidden_sums = expand_bias_grad.reshape(chips, 1, own_hidden // chips)
    hidden_sums = jnp.where(
        low_core,
        jnp.concatenate([hidden_sums, jnp.zeros_like(hidden_sums)], axis=1),
        jnp.concatenate([jnp.zeros_like(hidden_sums), hidden_sums], axis=1),
    )
    packed_grads = jnp.concatenate(
        [vector.reshape(everyone, share) for vector in grad_vectors]
        + [hidden_sums.reshape(everyone, -1)],
        axis=1,
    )
    packed_grads = packed_grads.reshape(sizes["z"], 2, sizes["x"], 2, vector_count)
    for axis, name in ((3, "c"), (2, "x"), (1, "y")):
        packed_grads = halve(packed_grads, axis, name)
    owned = z_scatter(packed_grads, F32)
    small = [owned[i * share : (i + 1) * share] for i in range(8)]
    return (
        layer_work,
        grad_work,
        project_owned.astype(F32),
        small[0],
        small[1],
        output_owned.astype(F32),
        small[2],
        small[3],
        small[4],
        expand_owned.astype(F32),
        owned[8 * share :],
        reduce_owned.astype(F32),
        small[5],
        small[6],
        small[7],
    )


def solution(mesh):
    seq_size, ctx_size = mesh.shape["seq"], mesh.shape["ctx"]
    sizes = {"z": seq_size // 2, "y": 2, "x": ctx_size // 2, "c": 2}
    fine = Mesh(mesh.devices.reshape(tuple(sizes.values())), tuple(sizes))
    rows = P(SEQ, CTX, None)
    matrix = P(ALL, None)
    vector = P(ALL)
    return jax.shard_map(
        functools.partial(on_device, sizes),
        mesh=fine,
        in_specs=(
            rows,
            P(SEQ, None),
            matrix,
            vector,
            vector,
            matrix,
            vector,
            vector,
            vector,
            matrix,
            vector,
            matrix,
            vector,
            vector,
            vector,
            rows,
        ),
        out_specs=(
            rows,
            rows,
            matrix,
            vector,
            vector,
            matrix,
            vector,
            vector,
            vector,
            matrix,
            vector,
            matrix,
            vector,
            vector,
            vector,
        ),
        check_vma=False,
    )
```

```python
import functools

import jax
import jax.numpy as jnp
from jax import lax
from jax.experimental import pallas as pl
from jax.experimental.pallas import tpu as pltpu
from jax.sharding import Mesh
from jax.sharding import PartitionSpec as P

HEADS = 16
HEAD_DIM = 64
CHUNKS = 2
PIECE = 256
MIB = 1 << 20
CHIPS = ("z", "y", "x")
SEQ = ("z", "y")
CTX = ("x", "c")
ALL = ("z", "y", "x", "c")
F32 = jnp.float32
BF16 = jnp.bfloat16
ELSEWHERE = pl.BlockSpec(memory_space=pl.ANY)


def dot(left, right, contract=(1, 0)):
    return lax.dot_general(
        left, right, (((contract[0],), (contract[1],)), ((), ())), preferred_element_type=F32
    )


def resident(shape):
    return pl.BlockSpec(shape, lambda i: (0,) * len(shape), pipeline_mode=pl.Buffered(1))


def by_row(shape):
    return pl.BlockSpec(shape, lambda i: (i,) + (0,) * (len(shape) - 1))


def flat(block):
    wide = block.shape[-1]
    if block.shape[-2] % 16:
        return block.astype(F32).reshape(-1, wide).astype(BF16)
    return block.reshape(-1, wide)


def hold_kernel(source, *refs):
    refs[-1][...] = source[...]


def hold(array, after):
    return pl.pallas_call(
        hold_kernel,
        grid=(1,),
        in_specs=[resident(array.shape)] + [ELSEWHERE] * len(after),
        out_specs=resident(array.shape),
        out_shape=jax.ShapeDtypeStruct(array.shape, array.dtype),
        compiler_params=pltpu.CompilerParams(vmem_limit_bytes=16 * MIB),
        name="hold",
    )(array, *after)


def unpack_kernel(pieces, *refs):
    out = refs[-1]
    height, lanes = out.shape[2], pieces.shape[2]
    for half in range(2):
        for i in range(out.shape[3] // lanes):
            start = (half * (out.shape[3] // lanes) + i) * height
            out[:, half, :, i * lanes : (i + 1) * lanes] = pieces[:, start : start + height]


def unpack(gathered, share, width, after):
    count, _, lanes = gathered.shape
    columns = width // lanes
    if share % 16:
        pieces = gathered[:, : 2 * columns * share].reshape(count, 2, columns, share, lanes)
        return jnp.swapaxes(pieces, 2, 3).reshape(2 * count, share, width)
    return pl.pallas_call(
        unpack_kernel,
        grid=(1,),
        in_specs=[pl.BlockSpec((count, 2 * columns * share, lanes), lambda i: (0, 0, 0))]
        + [ELSEWHERE] * len(after),
        out_specs=pl.BlockSpec((count, 2, share, width), lambda i: (0, 0, 0, 0)),
        out_shape=jax.ShapeDtypeStruct((count, 2, share, width), BF16),
        compiler_params=pltpu.CompilerParams(vmem_limit_bytes=16 * MIB),
        name="unpack",
    )(gathered, *after).reshape(2 * count, share, width)


def softmax_down(scores, allowed):
    scores = jnp.where(allowed, scores, -1e30)
    top = jnp.max(scores, axis=0, keepdims=True)
    expo = jnp.exp(scores - top)
    total = jnp.sum(expo, axis=0, keepdims=True)
    return expo * (1.0 / total)


def head_lanes(width, head):
    lane = lax.broadcasted_iota(jnp.int32, (1, width), 1)
    return (lane // HEAD_DIM == head).astype(F32)


def attend_kernel(late, t0, t1, t2, t3, wq, wk, wv, bias, seg_key, seg_query, *refs):
    m0, m1, m2, m3, kept, saved = refs[late:]
    part = t0.shape[1]
    rows = jnp.concatenate([t[0] for t in (t0, t1, t2, t3)], axis=0)
    kept[0] = rows
    width = wq.shape[2]
    queries, keys, values = [
        dot(rows, flat(w[...])) + bias[:, i * width : (i + 1) * width]
        for i, w in enumerate((wq, wk, wv))
    ]
    for i, part_of in enumerate((queries, keys, values)):
        saved[0, :, i * width : (i + 1) * width] = part_of.astype(BF16)
    queries = (queries.astype(BF16).astype(F32) * HEAD_DIM**-0.5).astype(BF16)
    keys = keys.astype(BF16).astype(F32)
    values_t = jnp.transpose(values).astype(BF16)
    allowed = seg_key[0] == seg_query[0]
    mixed = []
    for head in range(width // HEAD_DIM):
        own_keys = (keys * head_lanes(width, head)).astype(BF16)
        chances = softmax_down(dot(own_keys, queries, (1, 1)), allowed)
        own_values = values_t[head * HEAD_DIM : (head + 1) * HEAD_DIM]
        mixed.append(dot(own_values, chances.astype(BF16)))
    mixed = jnp.transpose(jnp.concatenate(mixed, axis=0)).astype(BF16)
    for index, out in enumerate((m0, m1, m2, m3)):
        out[0] = mixed[index * part : (index + 1) * part]


def project_specs(weight, depth):
    shape = (weight.shape[0], depth // weight.shape[0], weight.shape[2])
    return [
        pl.BlockSpec(shape, lambda i, j=j: (0, j + 2, 0), pipeline_mode=pl.Buffered(1))
        for j in range(3)
    ]


def attend(tokens, weight, bias, seg_key, seg_query, first, after):
    count, part, depth = tokens[0].shape
    count = count // CHUNKS
    wide = bias.shape[1]
    length = 4 * part
    return pl.pallas_call(
        functools.partial(attend_kernel, len(after)),
        grid=(count,),
        in_specs=[pl.BlockSpec((1, part, depth), lambda i: (i + first, 0, 0))] * 4
        + project_specs(weight, depth)
        + [
            resident((1, wide)),
            by_row((1, length, 1)),
            by_row((1, 1, length)),
        ]
        + [ELSEWHERE] * len(after),
        out_specs=[by_row((1, part, wide // 3))] * 4
        + [by_row((1, length, depth)), by_row((1, length, wide))],
        out_shape=[jax.ShapeDtypeStruct((count, part, wide // 3), BF16)] * 4
        + [
            jax.ShapeDtypeStruct((count, length, depth), BF16),
            jax.ShapeDtypeStruct((count, length, wide), BF16),
        ],
        compiler_params=pltpu.CompilerParams(vmem_limit_bytes=40 * MIB),
        cost_estimate=pl.CostEstimate(
            flops=count * length * wide * (2 * depth + 16 * length // 3),
            bytes_accessed=count * length * (depth + 2 * wide) * 2,
            transcendentals=count * length * length * wide // (3 * HEAD_DIM),
        ),
        name="attend_forward",
    )(*tokens, weight, weight, weight, bias, seg_key, seg_query, *after)


def attend_back_kernel(
    late, earlier, saved, kept, g0, g1, g2, g3, wq, wk, wv, seg_key, seg_query, *refs
):
    grad_weight, r0, r1, r2, r3, sums, total = refs[late + earlier :]

    @pl.when(pl.program_id(0) == 0)
    def _():
        total[...] = refs[0][...] if earlier else jnp.zeros_like(total)

    part = g0.shape[1]
    width = saved.shape[2] // 3
    factor = HEAD_DIM**-0.5
    queries = (saved[0, :, :width].astype(F32) * factor).astype(BF16)
    keys = saved[0, :, width : 2 * width].astype(F32)
    values = saved[0, :, 2 * width :].astype(F32)
    keys_t = jnp.transpose(keys * factor).astype(BF16)
    grad_mixed = jnp.concatenate([g[0] for g in (g0, g1, g2, g3)], axis=0)
    allowed = seg_key[0] == seg_query[0]
    grad_queries = []
    grad_keys = None
    grad_values = None
    for head in range(width // HEAD_DIM):
        lanes = head_lanes(width, head)
        chances = softmax_down(
            dot((keys * lanes).astype(BF16), queries, (1, 1)), allowed
        )
        grad_weights = dot((values * lanes).astype(BF16), grad_mixed, (1, 1))
        inner = jnp.sum(chances * grad_weights, axis=0, keepdims=True)
        grad_scores = (chances * (grad_weights - inner)).astype(BF16)
        grad_queries.append(dot(keys_t[head * HEAD_DIM : (head + 1) * HEAD_DIM], grad_scores))
        keys_term = dot(grad_scores, queries)
        values_term = dot(chances.astype(BF16), grad_mixed)
        if head == 0:
            grad_keys, grad_values = keys_term, values_term
        else:
            here = lanes > 0.5
            grad_keys = jnp.where(here, keys_term, grad_keys)
            grad_values = jnp.where(here, values_term, grad_values)
    grad_queries = jnp.concatenate(grad_queries, axis=0)
    terms = [
        jnp.transpose(grad_queries).astype(BF16),
        grad_keys.astype(BF16),
        grad_values.astype(BF16),
    ]
    total[:width] += dot(grad_queries.astype(BF16), kept[0])
    for i, term in enumerate(terms):
        sums[0, :, i * width : (i + 1) * width] = jnp.sum(
            term.astype(F32), axis=0, keepdims=True
        )
        if i:
            total[i * width : (i + 1) * width] += dot(term, kept[0], (0, 0))
    rows = sum(dot(term, flat(w[...]), (1, 1)) for term, w in zip(terms, (wq, wk, wv)))
    for index, out in enumerate((r0, r1, r2, r3)):
        out[0] = rows[index * part : (index + 1) * part].astype(out.dtype)

    @pl.when(pl.program_id(0) == pl.num_programs(0) - 1)
    def _():
        if grad_weight.dtype == BF16:
            grad_weight[...] = jnp.transpose(total[...]).astype(BF16)
        else:
            grad_weight[...] = total[...]


def attend_back(saved, kept, grads, weight, seg_key, seg_query, earlier, done, after):
    count, part, width = grads[0].shape
    depth, wide = width * 4, width * 3
    length = 4 * part
    shape, kind = ((depth, wide), BF16) if done else ((wide, depth), F32)
    return pl.pallas_call(
        functools.partial(attend_back_kernel, len(after), len(earlier)),
        grid=(count,),
        in_specs=[by_row((1, length, wide)), by_row((1, length, depth))]
        + [by_row((1, part, width))] * 4
        + project_specs(weight, depth)
        + [
            by_row((1, length, 1)),
            by_row((1, 1, length)),
        ]
        + [resident((wide, depth))] * len(earlier)
        + [ELSEWHERE] * len(after),
        out_specs=[resident(shape)]
        + [by_row((1, part, depth))] * 4
        + [by_row((1, 1, wide))],
        out_shape=[jax.ShapeDtypeStruct(shape, kind)]
        + [jax.ShapeDtypeStruct((count, part, depth), t) for t in (F32, BF16, F32, BF16)]
        + [jax.ShapeDtypeStruct((count, 1, wide), F32)],
        scratch_shapes=[pltpu.VMEM((wide, depth), F32)],
        compiler_params=pltpu.CompilerParams(vmem_limit_bytes=52 * MIB),
        cost_estimate=pl.CostEstimate(
            flops=count * length * wide * (4 * depth + 40 * length // 3),
            bytes_accessed=count * length * (3 * depth + 3 * wide) * 2,
            transcendentals=count * length * length * wide // (3 * HEAD_DIM),
        ),
        name="attend_backward",
    )(saved, kept, *grads, weight, weight, weight, seg_key, seg_query, *earlier, *after)


def column(shape):
    return pl.BlockSpec(shape, lambda i: (0, i))


def expand_piece(ref):
    return jnp.concatenate([flat(ref[:, i]) for i in range(ref.shape[1])], axis=1)


def reduce_piece(ref):
    columns = ref.shape[1] // 2
    halves = [
        jnp.concatenate([ref[:, half * columns + i] for i in range(columns)], axis=2)
        for half in range(2)
    ]
    return flat(jnp.concatenate(halves, axis=1))


def feed_kernel(*refs):
    sources, (expand, bias, reduce, act, slope, own_out, other_out, far_sum) = (
        refs[: 2 * CHUNKS],
        refs[2 * CHUNKS :],
    )
    step = pl.program_id(0)

    @pl.when(step == 0)
    def _():
        own_out[...] = jnp.zeros_like(own_out)
        far_sum[...] = jnp.zeros_like(far_sum)

    into = expand_piece(expand)
    back = reduce_piece(reduce)
    block = 256
    per = sources[0].shape[0] // block
    half_count = CHUNKS * per

    def inner(index):
        start = index % per * block
        return dot(sources[index // per][start : start + block], into) + bias[...]

    ahead = inner(0)
    for index in range(2 * half_count):
        inside = ahead
        if index + 1 < 2 * half_count:
            ahead = inner(index + 1)
        total = own_out if index < half_count else far_sum
        at = slice(index % half_count * block, (index % half_count + 1) * block)
        to = slice(index * block, (index + 1) * block)
        square = inside * inside
        curve = jnp.tanh(inside * (0.7978845608028654 + 0.7978845608028654 * 0.044715 * square))
        half = 0.5 * curve + 0.5
        active = (inside * half).astype(BF16)
        act[to] = active
        tilt = 0.7978845608028654 * 0.5 + 0.7978845608028654 * 1.5 * 0.044715 * square
        slope[to] = (half + inside * (1.0 - curve * curve) * tilt).astype(BF16)
        total[at] += dot(active, back)

    @pl.when(step == pl.num_programs(0) - 1)
    def _():
        other_out[...] = far_sum[...].astype(BF16)


def feed_weights(weights, pieces, columns):
    chips, _, rows, _ = weights.shape
    return [
        pl.BlockSpec((chips, pieces, rows, PIECE), lambda i: (0, i, 0, 0)),
        pl.BlockSpec(
            (pieces * PIECE // (2 * rows), 2 * columns, rows, PIECE), lambda i: (i, 1, 0, 0)
        ),
    ]


def feed(own, other, weights, bias):
    block, depth = own[0].shape
    rows = CHUNKS * block
    hidden = bias.shape[1]
    pieces = 2
    wide = pieces * PIECE
    expand_spec, reduce_spec = feed_weights(weights, pieces, depth // PIECE)
    return pl.pallas_call(
        feed_kernel,
        grid=(hidden // wide,),
        in_specs=[resident((block, depth))] * (2 * CHUNKS)
        + [expand_spec, column((1, wide)), reduce_spec],
        out_specs=[column((2 * rows, wide))] * 2 + [resident((rows, depth))] * 2,
        out_shape=[jax.ShapeDtypeStruct((2 * rows, hidden), BF16)] * 2
        + [
            jax.ShapeDtypeStruct((rows, depth), F32),
            jax.ShapeDtypeStruct((rows, depth), BF16),
        ],
        scratch_shapes=[pltpu.VMEM((rows, depth), F32)],
        compiler_params=pltpu.CompilerParams(vmem_limit_bytes=56 * MIB),
        cost_estimate=pl.CostEstimate(
            flops=8 * rows * depth * hidden,
            bytes_accessed=4 * rows * (2 * hidden + 3 * depth),
            transcendentals=2 * rows * hidden,
        ),
        name="feed_forward",
    )(*own, *other, weights, bias, weights)


def feed_back_kernel(*refs):
    grads, sources = refs[: 2 * CHUNKS], refs[2 * CHUNKS : 4 * CHUNKS]
    act, slope, expand, reduce, weight_grad, bias_grad, own_out, other_out, far_sum, inside = refs[
        4 * CHUNKS :
    ]
    step = pl.program_id(0)
    block = grads[0].shape[0]

    @pl.when(step == 0)
    def _():
        own_out[...] = jnp.zeros_like(own_out)
        far_sum[...] = jnp.zeros_like(far_sum)

    into = expand_piece(expand)
    back = reduce_piece(reduce)
    bias_sum = jnp.zeros(bias_grad.shape, F32)
    for index in range(2 * CHUNKS):
        total = own_out if index < CHUNKS else far_sum
        at = slice(index % CHUNKS * block, (index % CHUNKS + 1) * block)
        to = slice(index * block, (index + 1) * block)
        grad_act = dot(grads[index][...], back, (1, 1))
        part = (grad_act * slope[to].astype(F32)).astype(BF16)
        inside[to] = part
        bias_sum += jnp.sum(part.astype(F32), axis=0, keepdims=True)
        total[at] += dot(part, into, (1, 1))
    bias_grad[...] = bias_sum
    chips, pieces, height, _ = weight_grad.shape
    columns = pieces // 4
    reduce_grad = sum(
        dot(act[i * block : (i + 1) * block], grad[...], (0, 0)) for i, grad in enumerate(grads)
    )
    count = PIECE // (2 * height)
    reduce_grad = reduce_grad.reshape(count, 2 * height, reduce_grad.shape[1]).astype(BF16)
    mine = pl.ds(step * count, count)
    for half in range(2):
        for i in range(columns):
            weight_grad[mine, (2 + half) * columns + i] = reduce_grad[
                :, half * height : (half + 1) * height, i * PIECE : (i + 1) * PIECE
            ]
    flipped = sum(
        dot(inside[i * block : (i + 1) * block], source[...], (0, 0))
        for i, source in enumerate(sources)
    )
    expand_grad = jnp.transpose(flipped).reshape(chips, height, PIECE).astype(BF16)
    weight_grad[:, step] = expand_grad

    @pl.when(step == pl.num_programs(0) - 1)
    def _():
        other_out[...] = far_sum[...].astype(BF16)


def feed_back(grads, sources, act, slope, weights):
    block, depth = grads[0].shape
    rows = CHUNKS * block
    hidden = act.shape[1]
    chips, _, height, _ = weights.shape
    pieces = 2 * hidden // PIECE
    expand_spec, reduce_spec = feed_weights(weights, 1, depth // PIECE)
    return pl.pallas_call(
        feed_back_kernel,
        grid=(hidden // PIECE,),
        in_specs=[resident((block, depth))] * (4 * CHUNKS)
        + [column((2 * rows, PIECE))] * 2
        + [expand_spec, reduce_spec],
        out_specs=[
            resident((chips, pieces, height, PIECE)),
            column((1, PIECE)),
        ]
        + [resident((rows, depth))] * 2,
        out_shape=[
            jax.ShapeDtypeStruct((chips, pieces, height, PIECE), BF16),
            jax.ShapeDtypeStruct((1, hidden), F32),
            jax.ShapeDtypeStruct((rows, depth), F32),
            jax.ShapeDtypeStruct((rows, depth), BF16),
        ],
        scratch_shapes=[
            pltpu.VMEM((rows, depth), F32),
            pltpu.VMEM((2 * rows, PIECE), BF16),
        ],
        compiler_params=pltpu.CompilerParams(vmem_limit_bytes=56 * MIB),
        cost_estimate=pl.CostEstimate(
            flops=16 * rows * depth * hidden,
            bytes_accessed=4 * rows * (2 * hidden + 5 * depth) + 8 * depth * hidden,
            transcendentals=0,
        ),
        name="feed_backward",
    )(*grads, *sources, act, slope, weights, weights)


def normalize(values):
    center = values - jnp.mean(values, axis=-1, keepdims=True)
    inverse = lax.rsqrt(jnp.mean(center * center, axis=-1, keepdims=True) + 1e-05)
    return (center * inverse, inverse)


def normalize_back(incoming, scaled, inverse, gain):
    grad_scaled = incoming * gain
    mean_one = jnp.mean(grad_scaled, axis=-1, keepdims=True)
    mean_two = jnp.mean(grad_scaled * scaled, axis=-1, keepdims=True)
    return inverse * (grad_scaled - mean_one - scaled * mean_two)


def add_sums(out, *rows):
    rows = [jnp.sum(row, axis=0, keepdims=True) for row in rows]
    rows.append(jnp.zeros((out.shape[0] - len(rows), out.shape[1]), F32))
    rows = jnp.concatenate(rows, axis=0)

    @pl.when(pl.program_id(0) == 0)
    def _():
        out[...] = rows

    @pl.when(pl.program_id(0) > 0)
    def _():
        out[...] += rows


OUT_BIAS, GAIN_ONE, SHIFT_ONE, RED_BIAS, GAIN_TWO, SHIFT_TWO = (slice(i, i + 1) for i in range(2, 8))
SCALAR = pl.BlockSpec(memory_space=pltpu.SMEM)
ROW_BLOCK = 256


def row_call(kernel, name, ins, outs, arrays, rows, cost):
    return pl.pallas_call(
        kernel,
        grid=(rows // ROW_BLOCK,),
        in_specs=ins,
        out_specs=[spec for spec, _ in outs],
        out_shape=[shape for _, shape in outs],
        compiler_params=pltpu.CompilerParams(vmem_limit_bytes=48 * MIB),
        cost_estimate=pl.CostEstimate(flops=cost, bytes_accessed=rows << 14, transcendentals=rows),
        name=name,
    )(*arrays)


def row_block(width, first=0):
    return pl.BlockSpec((ROW_BLOCK, width), lambda i: (i + first, 0))


def first_norm_kernel(place, m0, m1, m2, m3, tokens, weight, vectors, low, scaled, inverse, mixed):
    total = tokens[...].astype(F32) + vectors[OUT_BIAS]
    parts = [m[...].reshape(ROW_BLOCK, -1) for m in (m0, m1, m2, m3)]
    mixed[...] = jnp.concatenate(parts, axis=1)
    for step, part in enumerate(parts):
        total += dot(part, weight[place[0] ^ step])
    scaled_one, inverse_one = normalize(total)
    scaled[...] = scaled_one
    inverse[...] = inverse_one
    low[...] = (scaled_one * vectors[GAIN_ONE] + vectors[SHIFT_ONE]).astype(BF16)


def first_norm(place, mixed, rows, weight, vectors, chunk):
    width = rows.shape[1]
    count, part, lanes = mixed[0].shape
    size = count * part
    steps = size // ROW_BLOCK
    return row_call(
        first_norm_kernel,
        "first_norm",
        [SCALAR]
        + [by_row((ROW_BLOCK // part, part, lanes))] * 4
        + [row_block(width, chunk * steps), resident(weight.shape), resident(vectors.shape)],
        [
            (row_block(width), jax.ShapeDtypeStruct((size, width), BF16)),
            (row_block(width), jax.ShapeDtypeStruct((size, width), F32)),
            (row_block(1), jax.ShapeDtypeStruct((size, 1), F32)),
            (row_block(width), jax.ShapeDtypeStruct((size, width), BF16)),
        ],
        (place, *mixed, rows, weight, vectors),
        size,
        2 * size * width * width,
    )


def second_norm_kernel(scaled, own, far, grad_out, vectors, layer, grad, low, sums):
    first = scaled[...] * vectors[GAIN_ONE] + vectors[SHIFT_ONE]
    reduced = own[...] + far[...].astype(F32) + vectors[RED_BIAS]
    scaled_two, inverse_two = normalize(first + reduced)
    layer[...] = (scaled_two * vectors[GAIN_TWO] + vectors[SHIFT_TWO]).astype(BF16)
    incoming = grad_out[...].astype(F32)
    grad_second = normalize_back(incoming, scaled_two, inverse_two, vectors[GAIN_TWO])
    grad[...] = grad_second
    low[...] = grad_second.astype(BF16)
    add_sums(sums, incoming * scaled_two, incoming, grad_second.astype(BF16).astype(F32))


def second_norm(scaled, own, far, grad_rows, vectors, chunk):
    size, width = scaled.shape
    steps = size // ROW_BLOCK
    return row_call(
        second_norm_kernel,
        "second_norm",
        [row_block(width)]
        + [row_block(width, chunk * steps)] * 3
        + [resident(vectors.shape)],
        [
            (row_block(width), jax.ShapeDtypeStruct((size, width), BF16)),
            (row_block(width), jax.ShapeDtypeStruct((size, width), F32)),
            (row_block(width), jax.ShapeDtypeStruct((size, width), BF16)),
            (resident((8, width)), jax.ShapeDtypeStruct((8, width), F32)),
        ],
        (scaled, own, far, grad_rows, vectors),
        size,
        size * width * 40,
    )


def first_back_kernel(
    place, grad, own, far, scaled, inverse, weight, vectors, hidden, low, m0, m1, m2, m3, sums
):
    incoming = grad[...] + own[...] + far[...].astype(F32)
    grad_hidden = normalize_back(incoming, scaled[...], inverse[...], vectors[GAIN_ONE])
    hidden[...] = grad_hidden
    attended = grad_hidden.astype(BF16)
    low[...] = attended
    for step, out in enumerate((m0, m1, m2, m3)):
        out[...] = dot(attended, weight[place[0] ^ step], (1, 1)).astype(BF16).reshape(out.shape)
    add_sums(sums, incoming * scaled[...], incoming, attended.astype(F32))


def first_back(place, grad, own, far, scaled, inverse, weight, vectors, chunk, part):
    size, width = grad.shape
    steps = size // ROW_BLOCK
    lanes = weight.shape[1]
    return row_call(
        first_back_kernel,
        "first_back",
        [SCALAR, row_block(width)]
        + [row_block(width, chunk * steps)] * 2
        + [row_block(width), row_block(1), resident(weight.shape), resident(vectors.shape)],
        [
            (row_block(width), jax.ShapeDtypeStruct((size, width), F32)),
            (row_block(width), jax.ShapeDtypeStruct((size, width), BF16)),
        ]
        + [
            (
                by_row((ROW_BLOCK // part, part, lanes)),
                jax.ShapeDtypeStruct((size // part, part, lanes), BF16),
            )
        ]
        * 4
        + [(resident((8, width)), jax.ShapeDtypeStruct((8, width), F32))],
        (place, grad, own, far, scaled, inverse, weight, vectors),
        size,
        2 * size * width * width,
    )


def output_grad_kernel(place, *refs):
    mixed, grads, out = refs[:CHUNKS], refs[CHUNKS:-1], refs[-1]
    lanes = out.shape[1]
    for step in range(out.shape[0]):
        at = slice(step * lanes, (step + 1) * lanes)
        out[place[0] ^ step] = sum(
            dot(m[:, at], g[...], (0, 0)) for m, g in zip(mixed, grads)
        ).astype(BF16)


def output_back(place, mixed, grads, ctx_size):
    size, width = mixed[0].shape
    shape = (ctx_size, width // ctx_size, width)
    return pl.pallas_call(
        output_grad_kernel,
        grid=(1,),
        in_specs=[SCALAR] + [resident((size, width))] * (2 * CHUNKS),
        out_specs=resident(shape),
        out_shape=jax.ShapeDtypeStruct(shape, BF16),
        compiler_params=pltpu.CompilerParams(vmem_limit_bytes=48 * MIB),
        cost_estimate=pl.CostEstimate(
            flops=2 * CHUNKS * size * width * width,
            bytes_accessed=4 * width * (width + CHUNKS * size),
            transcendentals=0,
        ),
        name="output_backward",
    )(place, *mixed, *grads)


def on_device(
    sizes,
    tokens,
    segment_ids,
    project_weight,
    query_bias,
    value_bias,
    output_weight,
    output_bias,
    first_gain,
    first_shift,
    expand_weight,
    expand_bias,
    reduce_weight,
    reduce_bias,
    second_gain,
    second_shift,
    grad_out,
):
    chips = sizes["z"] * sizes["y"] * sizes["x"]
    ctx_size = sizes["x"] * sizes["c"]
    everyone = chips * sizes["c"]
    seq_count, part, width = tokens.shape
    rows_count = seq_count * part
    hidden = expand_weight.shape[1]
    share = width // everyone
    own_hidden = hidden // 2
    lanes = width // ctx_size
    place = lax.axis_index(CTX)
    core = lax.axis_index("c")
    low_core = core == 0

    def hop(array, step):
        return lax.ppermute(array, CTX, [(i, i ^ step) for i in range(ctx_size)])

    def swap(array):
        return lax.ppermute(array, "c", [(0, 1), (1, 0)])

    def chosen(array, index, axis):
        return lax.dynamic_index_in_dim(array, index, axis, keepdims=False)

    def pair(own, other, axis, low):
        return jnp.where(
            low, jnp.stack([own, other], axis=axis), jnp.stack([other, own], axis=axis)
        )

    def by_core(own, other, axis):
        return pair(own, other, axis, low_core)

    def bit_of(name, step):
        return (lax.axis_index(name) // step) % 2

    def trade(array, name, step=1):
        return lax.ppermute(array, name, [(i, i ^ step) for i in range(sizes[name])])

    def widen(array, name, axis=0, step=1):
        return pair(array, trade(array, name, step), axis, bit_of(name, step) == 0)

    def halve(array, axis, name, step=1):
        me = bit_of(name, step)
        return chosen(array, me, axis).astype(F32) + trade(
            chosen(array, 1 - me, axis), name, step
        ).astype(F32)

    z_steps = [1 << i for i in range(sizes["z"].bit_length() - 1)]

    def z_gather(array):
        for index, step in enumerate(z_steps[::-1]):
            array = widen(array, "z", index, step)
        return array

    def z_scatter(blocks, kind=BF16):
        for step in z_steps:
            blocks = blocks.reshape((blocks.shape[0] // 2, 2) + blocks.shape[1:])
            blocks = halve(blocks.astype(kind), 1, "z", step)
        return blocks[0]

    seg_parts = segment_ids.reshape(seq_count, ctx_size, part)
    seg = jnp.concatenate([chosen(seg_parts, place ^ r, 1) for r in range(ctx_size)], axis=1)
    seg_key = seg[:, :, None]
    seg_query = seg[:, None, :]

    vectors = (
        query_bias,
        value_bias,
        output_bias,
        first_gain,
        first_shift,
        reduce_bias,
        second_gain,
        second_shift,
        expand_bias,
    )
    vector_count = 8 * share + expand_bias.shape[0]
    own_vectors = jnp.concatenate(vectors)
    vector_row = jnp.pad(own_vectors, (0, 3 * lanes - vector_count))[None]
    filler = jnp.concatenate([vector_row, jnp.zeros((15, 3 * lanes), BF16)])
    held = jnp.stack(
        [
            jnp.concatenate(
                [
                    jnp.concatenate(
                        [
                            project_weight[:, (ctx_size * j + p) * lanes :][:, :lanes]
                            for j in range(3)
                        ],
                        axis=1,
                    ),
                    filler,
                ]
            )
            for p in range(ctx_size)
        ]
    )
    held = lax.all_to_all(held, CTX, 0, 0, tiled=True)
    sent, held = lax.optimization_barrier((tokens, held))
    across = hop(sent, 2)
    gathered = (tokens, swap(sent), across, swap(across))
    mine = jnp.concatenate(
        [held[:, :share, j * lanes : (j + 1) * lanes].reshape(-1, lanes) for j in range(3)]
    )
    vector_rows = held[:, share, :vector_count].reshape(-1)
    vector_rows = jnp.pad(vector_rows, (0, 16 * lanes - vector_rows.shape[0])).reshape(16, lanes)
    out_pieces = jnp.concatenate(
        [output_weight[:, i * lanes : (i + 1) * lanes] for i in range(ctx_size)]
    )
    full_project = lax.all_gather(
        jnp.concatenate([widen(out_pieces, "x").reshape(-1, lanes), mine, vector_rows]),
        SEQ,
        axis=0,
    )
    packed = (
        full_project[:, -16:]
        .reshape(-1, 16 * lanes)[:, : ctx_size * vector_count]
        .reshape(everyone, vector_count)
        .astype(F32)
    )
    vectors = jnp.swapaxes(packed[:, : 8 * share].reshape(everyone, 8, share), 0, 1).reshape(
        8, width
    )
    full_query, full_value = vectors[0], vectors[1]
    exp_bias = chosen(packed[:, 8 * share :].reshape(chips, 2, -1), core, 1).reshape(1, own_hidden)
    bias_all = jnp.concatenate(
        [
            lax.dynamic_slice_in_dim(full_query, place * lanes, lanes),
            jnp.zeros((lanes,), F32),
            lax.dynamic_slice_in_dim(full_value, place * lanes, lanes),
        ]
    )[None]

    columns = expand_weight.reshape(share, chips, 2, own_hidden // chips)
    own_columns = chosen(columns, core, 2).reshape(share, own_hidden)
    far_columns = chosen(columns, 1 - core, 2).reshape(share, own_hidden)
    both = by_core(own_columns, swap(far_columns), 0)

    def in_pieces(array):
        rows_of, wide = array.shape
        return jnp.swapaxes(array.reshape(rows_of, wide // PIECE, PIECE), 0, 1).reshape(
            -1, 2 * share, PIECE
        )

    own_pieces = jnp.concatenate(
        [
            in_pieces(both.reshape(2 * share, own_hidden)),
            jnp.swapaxes(
                reduce_weight.reshape(2, 2 * share, width // PIECE, PIECE), 1, 2
            ).reshape(-1, 2 * share, PIECE),
        ]
    )
    own_pieces = hold(own_pieces, [across])
    weights = lax.all_gather(widen(own_pieces, "x"), SEQ, axis=0).reshape(
        chips, -1, 2 * share, PIECE
    )

    rows = tokens.reshape(rows_count, width)
    where = place.reshape(1).astype(jnp.int32)
    seqs = seq_count // CHUNKS
    saved, kept_rows, mixed_low, first_low, scaled_one, inverse_one = [], [], [], [], [], []
    for index in range(CHUNKS):
        at = slice(index * seqs, (index + 1) * seqs)
        *mixed, all_rows, kept = attend(
            gathered, full_project, bias_all, seg_key[at], seg_query[at], at.start, []
        )
        kept_rows.append(all_rows)
        saved.append(kept)
        if index == 0:
            out_half = unpack(full_project, share, width, mixed[:1])
            full_output = by_core(out_half, swap(out_half), 1).reshape(ctx_size, lanes, width)
        arrived = [mixed[0]] + [hop(mixed[r], r) for r in (1, 2, 3)]
        low, scaled, inverse, joined = first_norm(
            where, arrived, rows, full_output, vectors, index
        )
        mixed_low.append(joined)
        first_low.append(low)
        scaled_one.append(scaled)
        inverse_one.append(inverse)
    first_far = [swap(low) for low in first_low]
    act, slope, own_sum, far_sum = feed(first_low, first_far, weights, exp_bias)
    far_sum = swap(far_sum)

    grad_rows = grad_out.reshape(rows_count, width)
    layer_parts, grad_second, grad_reduced, second_sums = zip(
        *(
            second_norm(scaled_one[index], own_sum, far_sum, grad_rows, vectors, index)
            for index in range(CHUNKS)
        )
    )
    layer_work = jnp.concatenate(layer_parts, axis=0).reshape(tokens.shape)
    weight_grad, expand_bias_grad, own_back, far_back = feed_back(
        grad_reduced + tuple(swap(grad) for grad in grad_reduced),
        first_low + first_far,
        act,
        slope,
        weights,
    )
    weight_owned = lax.psum_scatter(
        weight_grad.reshape((-1, sizes["x"]) + weight_grad.shape[1:]),
        SEQ,
        scatter_dimension=0,
        tiled=True,
    )[0]
    far_back = swap(far_back)
    grad_hidden, grad_attended, grad_mixed, first_sums = [], [], [], []
    for index in range(CHUNKS):
        grad, low, *mixed, sums = first_back(
            where,
            grad_second[index],
            own_back,
            far_back,
            scaled_one[index],
            inverse_one[index],
            full_output,
            vectors,
            index,
            part,
        )
        grad_hidden.append(grad.reshape(seqs, part, width))
        grad_attended.append(low)
        grad_mixed.append([mixed[0]] + [hop(mixed[r], r) for r in (1, 2, 3)])
        first_sums.append(sums)
    output_grad = output_back(where, mixed_low, grad_attended, ctx_size).reshape(
        sizes["z"], 2, sizes["x"], 2, share, width
    )
    output_grad = halve(output_grad, 3, "c").astype(BF16)
    output_grad = halve(output_grad, 2, "x").astype(BF16)
    output_grad = halve(output_grad, 1, "y")
    output_owned = z_scatter(output_grad)

    project_grad = []
    work_parts = []
    across_sums = []
    work_hops = []
    sum_parts = []
    for index in range(CHUNKS):
        at = slice(index * seqs, (index + 1) * seqs)
        project_part, r0, r1, r2, r3, sums = attend_back(
            saved[index],
            kept_rows[index],
            grad_mixed[index],
            full_project,
            seg_key[at],
            seg_query[at],
            project_grad,
            index == CHUNKS - 1,
            across_sums[:index],
        )
        project_grad = [project_part]
        across_sums.append((r2 + swap(r3).astype(F32)).astype(BF16))
        work_hops.append(hop(across_sums[index], 2))
        work_parts.append(
            grad_hidden[index] + r0 + swap(r1).astype(F32) + work_hops[index].astype(F32)
        )
        sum_parts.append(sums)
    grad_work = jnp.concatenate(work_parts, axis=0)
    project_grad = hold(project_grad[0], work_hops[:1])
    blocks = halve(project_grad.reshape(sizes["z"], 2, ctx_size * share, 3 * lanes), 1, "y")
    for step in z_steps:
        blocks = blocks.astype(BF16).reshape((blocks.shape[0] // 2, 2) + blocks.shape[1:])
        blocks = halve(blocks, 1, "z", step)
        if step == 1:
            blocks = hold(blocks.astype(BF16), work_hops[1:])
    weight_owned = halve(weight_owned, 0, "x")
    held = lax.all_to_all(
        hold(blocks.astype(F32).reshape(ctx_size, share, 3 * lanes), [weight_owned]),
        CTX,
        0,
        0,
        tiled=True,
    )
    project_owned = jnp.concatenate(
        [
            held[p, :, j * lanes : (j + 1) * lanes]
            for j in range(3)
            for p in range(ctx_size)
        ],
        axis=1,
    )
    expand_pieces = own_hidden // PIECE
    far_rows = jnp.swapaxes(
        weight_owned[:expand_pieces].reshape(expand_pieces, 2, share, PIECE), 0, 1
    )
    expand_owned = by_core(
        jnp.swapaxes(chosen(far_rows, core, 0), 0, 1).reshape(share, chips, -1),
        jnp.swapaxes(swap(chosen(far_rows, 1 - core, 0)), 0, 1).reshape(share, chips, -1),
        2,
    ).reshape(share, hidden)
    reduce_owned = jnp.swapaxes(
        weight_owned[expand_pieces:].reshape(2, width // PIECE, 2 * share, PIECE), 1, 2
    ).reshape(4 * share, width)

    column_sums = jnp.sum(jnp.concatenate(sum_parts, axis=0), axis=(0, 1))
    zeros = jnp.zeros((width,), F32)
    first_sums, second_sums = sum(first_sums), sum(second_sums)
    grad_vectors = (
        lax.dynamic_update_slice_in_dim(zeros, column_sums[:lanes], place * lanes, 0),
        lax.dynamic_update_slice_in_dim(zeros, column_sums[2 * lanes :], place * lanes, 0),
        first_sums[2],
        first_sums[0],
        first_sums[1],
        second_sums[2],
        second_sums[0],
        second_sums[1],
    )
    hidden_sums = expand_bias_grad.reshape(chips, 1, own_hidden // chips)
    hidden_sums = jnp.where(
        low_core,
        jnp.concatenate([hidden_sums, jnp.zeros_like(hidden_sums)], axis=1),
        jnp.concatenate([jnp.zeros_like(hidden_sums), hidden_sums], axis=1),
    )
    packed_grads = jnp.concatenate(
        [vector.reshape(everyone, share) for vector in grad_vectors]
        + [hidden_sums.reshape(everyone, -1)],
        axis=1,
    )
    packed_grads = packed_grads.reshape(sizes["z"], 2, sizes["x"], 2, vector_count)
    for axis, name in ((3, "c"), (2, "x"), (1, "y")):
        packed_grads = halve(packed_grads, axis, name)
    owned = z_scatter(packed_grads, F32)
    small = [owned[i * share : (i + 1) * share] for i in range(8)]
    return (
        layer_work,
        grad_work,
        project_owned.astype(F32),
        small[0],
        small[1],
        output_owned.astype(F32),
        small[2],
        small[3],
        small[4],
        expand_owned.astype(F32),
        owned[8 * share :],
        reduce_owned.astype(F32),
        small[5],
        small[6],
        small[7],
    )


def solution(mesh):
    seq_size, ctx_size = mesh.shape["seq"], mesh.shape["ctx"]
    sizes = {"z": seq_size // 2, "y": 2, "x": ctx_size // 2, "c": 2}
    fine = Mesh(mesh.devices.reshape(tuple(sizes.values())), tuple(sizes))
    rows = P(SEQ, CTX, None)
    matrix = P(ALL, None)
    vector = P(ALL)
    return jax.shard_map(
        functools.partial(on_device, sizes),
        mesh=fine,
        in_specs=(
            rows,
            P(SEQ, None),
            matrix,
            vector,
            vector,
            matrix,
            vector,
            vector,
            vector,
            matrix,
            vector,
            matrix,
            vector,
            vector,
            vector,
            rows,
        ),
        out_specs=(
            rows,
            rows,
            matrix,
            vector,
            vector,
            matrix,
            vector,
            vector,
            vector,
            matrix,
            vector,
            matrix,
            vector,
            vector,
            vector,
        ),
        check_vma=False,
    )
```

```python
import functools

import jax
import jax.numpy as jnp
from jax import lax
from jax.experimental import pallas as pl
from jax.experimental.pallas import tpu as pltpu
from jax.sharding import Mesh
from jax.sharding import PartitionSpec as P

HEADS = 16
HEAD_DIM = 64
CHUNKS = 2
PIECE = 256
MIB = 1 << 20
CHIPS = ("z", "y", "x")
SEQ = ("z", "y")
CTX = ("x", "c")
ALL = ("z", "y", "x", "c")
F32 = jnp.float32
BF16 = jnp.bfloat16
ELSEWHERE = pl.BlockSpec(memory_space=pl.ANY)


def dot(left, right, contract=(1, 0)):
    return lax.dot_general(
        left, right, (((contract[0],), (contract[1],)), ((), ())), preferred_element_type=F32
    )


def resident(shape):
    return pl.BlockSpec(shape, lambda i: (0,) * len(shape), pipeline_mode=pl.Buffered(1))


def by_row(shape):
    return pl.BlockSpec(shape, lambda i: (i,) + (0,) * (len(shape) - 1))


def flat(block):
    wide = block.shape[-1]
    if block.shape[-2] % 16:
        return block.astype(F32).reshape(-1, wide).astype(BF16)
    return block.reshape(-1, wide)


def hold_kernel(source, *refs):
    refs[-1][...] = source[...]


def hold(array, after):
    return pl.pallas_call(
        hold_kernel,
        grid=(1,),
        in_specs=[resident(array.shape)] + [ELSEWHERE] * len(after),
        out_specs=resident(array.shape),
        out_shape=jax.ShapeDtypeStruct(array.shape, array.dtype),
        compiler_params=pltpu.CompilerParams(vmem_limit_bytes=16 * MIB),
        name="hold",
    )(array, *after)


def unpack_kernel(pieces, *refs):
    out = refs[-1]
    height, lanes = out.shape[2], pieces.shape[2]
    for half in range(2):
        for i in range(out.shape[3] // lanes):
            start = (half * (out.shape[3] // lanes) + i) * height
            out[:, half, :, i * lanes : (i + 1) * lanes] = pieces[:, start : start + height]


def unpack(gathered, share, width, after):
    count, _, lanes = gathered.shape
    columns = width // lanes
    if share % 16:
        pieces = gathered[:, : 2 * columns * share].reshape(count, 2, columns, share, lanes)
        return jnp.swapaxes(pieces, 2, 3).reshape(2 * count, share, width)
    return pl.pallas_call(
        unpack_kernel,
        grid=(1,),
        in_specs=[pl.BlockSpec((count, 2 * columns * share, lanes), lambda i: (0, 0, 0))]
        + [ELSEWHERE] * len(after),
        out_specs=pl.BlockSpec((count, 2, share, width), lambda i: (0, 0, 0, 0)),
        out_shape=jax.ShapeDtypeStruct((count, 2, share, width), BF16),
        compiler_params=pltpu.CompilerParams(vmem_limit_bytes=16 * MIB),
        name="unpack",
    )(gathered, *after).reshape(2 * count, share, width)


def softmax_down(scores, allowed):
    scores = jnp.where(allowed, scores, -1e30)
    top = jnp.max(scores, axis=0, keepdims=True)
    expo = jnp.exp(scores - top)
    total = jnp.sum(expo, axis=0, keepdims=True)
    return expo * (1.0 / total)


def head_lanes(width, head):
    lane = lax.broadcasted_iota(jnp.int32, (1, width), 1)
    return (lane // HEAD_DIM == head).astype(F32)


def attend_kernel(late, t0, t1, t2, t3, wq, wk, wv, bias, seg_key, seg_query, *refs):
    m0, m1, m2, m3, kept, saved = refs[late:]
    part = t0.shape[1]
    rows = jnp.concatenate([t[0] for t in (t0, t1, t2, t3)], axis=0)
    kept[0] = rows
    width = wq.shape[2]
    queries, keys, values = [
        dot(rows, flat(w[...])) + bias[:, i * width : (i + 1) * width]
        for i, w in enumerate((wq, wk, wv))
    ]
    for i, part_of in enumerate((queries, keys, values)):
        saved[0, :, i * width : (i + 1) * width] = part_of.astype(BF16)
    queries = (queries.astype(BF16).astype(F32) * HEAD_DIM**-0.5).astype(BF16)
    keys = keys.astype(BF16).astype(F32)
    values_t = jnp.transpose(values).astype(BF16)
    allowed = seg_key[0] == seg_query[0]
    mixed = []
    for head in range(width // HEAD_DIM):
        own_keys = (keys * head_lanes(width, head)).astype(BF16)
        chances = softmax_down(dot(own_keys, queries, (1, 1)), allowed)
        own_values = values_t[head * HEAD_DIM : (head + 1) * HEAD_DIM]
        mixed.append(dot(own_values, chances.astype(BF16)))
    mixed = jnp.transpose(jnp.concatenate(mixed, axis=0)).astype(BF16)
    for index, out in enumerate((m0, m1, m2, m3)):
        out[0] = mixed[index * part : (index + 1) * part]


def project_specs(weight, depth):
    shape = (weight.shape[0], depth // weight.shape[0], weight.shape[2])
    return [
        pl.BlockSpec(shape, lambda i, j=j: (0, j + 2, 0), pipeline_mode=pl.Buffered(1))
        for j in range(3)
    ]


def attend(tokens, weight, bias, seg_key, seg_query, first, after):
    count, part, depth = tokens[0].shape
    count = count // CHUNKS
    wide = bias.shape[1]
    length = 4 * part
    return pl.pallas_call(
        functools.partial(attend_kernel, len(after)),
        grid=(count,),
        in_specs=[pl.BlockSpec((1, part, depth), lambda i: (i + first, 0, 0))] * 4
        + project_specs(weight, depth)
        + [
            resident((1, wide)),
            by_row((1, length, 1)),
            by_row((1, 1, length)),
        ]
        + [ELSEWHERE] * len(after),
        out_specs=[by_row((1, part, wide // 3))] * 4
        + [by_row((1, length, depth)), by_row((1, length, wide))],
        out_shape=[jax.ShapeDtypeStruct((count, part, wide // 3), BF16)] * 4
        + [
            jax.ShapeDtypeStruct((count, length, depth), BF16),
            jax.ShapeDtypeStruct((count, length, wide), BF16),
        ],
        compiler_params=pltpu.CompilerParams(vmem_limit_bytes=40 * MIB),
        cost_estimate=pl.CostEstimate(
            flops=count * length * wide * (2 * depth + 16 * length // 3),
            bytes_accessed=count * length * (depth + 2 * wide) * 2,
            transcendentals=count * length * length * wide // (3 * HEAD_DIM),
        ),
        name="attend_forward",
    )(*tokens, weight, weight, weight, bias, seg_key, seg_query, *after)


def attend_back_kernel(
    late, earlier, saved, kept, g0, g1, g2, g3, wq, wk, wv, seg_key, seg_query, *refs
):
    grad_weight, r0, r1, r2, r3, sums, total = refs[late + earlier :]

    @pl.when(pl.program_id(0) == 0)
    def _():
        total[...] = refs[0][...] if earlier else jnp.zeros_like(total)

    part = g0.shape[1]
    width = saved.shape[2] // 3
    factor = HEAD_DIM**-0.5
    queries = (saved[0, :, :width].astype(F32) * factor).astype(BF16)
    keys = saved[0, :, width : 2 * width].astype(F32)
    values = saved[0, :, 2 * width :].astype(F32)
    keys_t = jnp.transpose(keys * factor).astype(BF16)
    grad_mixed = jnp.concatenate([g[0] for g in (g0, g1, g2, g3)], axis=0)
    allowed = seg_key[0] == seg_query[0]
    grad_queries = []
    grad_keys = None
    grad_values = None
    for head in range(width // HEAD_DIM):
        lanes = head_lanes(width, head)
        chances = softmax_down(
            dot((keys * lanes).astype(BF16), queries, (1, 1)), allowed
        )
        grad_weights = dot((values * lanes).astype(BF16), grad_mixed, (1, 1))
        inner = jnp.sum(chances * grad_weights, axis=0, keepdims=True)
        grad_scores = (chances * (grad_weights - inner)).astype(BF16)
        grad_queries.append(dot(keys_t[head * HEAD_DIM : (head + 1) * HEAD_DIM], grad_scores))
        keys_term = dot(grad_scores, queries)
        values_term = dot(chances.astype(BF16), grad_mixed)
        if head == 0:
            grad_keys, grad_values = keys_term, values_term
        else:
            here = lanes > 0.5
            grad_keys = jnp.where(here, keys_term, grad_keys)
            grad_values = jnp.where(here, values_term, grad_values)
    grad_queries = jnp.concatenate(grad_queries, axis=0)
    terms = [
        jnp.transpose(grad_queries).astype(BF16),
        grad_keys.astype(BF16),
        grad_values.astype(BF16),
    ]
    total[:width] += dot(grad_queries.astype(BF16), kept[0])
    for i, term in enumerate(terms):
        sums[0, :, i * width : (i + 1) * width] = jnp.sum(
            term.astype(F32), axis=0, keepdims=True
        )
        if i:
            total[i * width : (i + 1) * width] += dot(term, kept[0], (0, 0))
    rows = sum(dot(term, flat(w[...]), (1, 1)) for term, w in zip(terms, (wq, wk, wv)))
    for index, out in enumerate((r0, r1, r2, r3)):
        out[0] = rows[index * part : (index + 1) * part].astype(out.dtype)

    @pl.when(pl.program_id(0) == pl.num_programs(0) - 1)
    def _():
        if grad_weight.dtype == BF16:
            grad_weight[...] = jnp.transpose(total[...]).astype(BF16)
        else:
            grad_weight[...] = total[...]


def attend_back(saved, kept, grads, weight, seg_key, seg_query, earlier, done, after):
    count, part, width = grads[0].shape
    depth, wide = width * 4, width * 3
    length = 4 * part
    shape, kind = ((depth, wide), BF16) if done else ((wide, depth), F32)
    return pl.pallas_call(
        functools.partial(attend_back_kernel, len(after), len(earlier)),
        grid=(count,),
        in_specs=[by_row((1, length, wide)), by_row((1, length, depth))]
        + [by_row((1, part, width))] * 4
        + project_specs(weight, depth)
        + [
            by_row((1, length, 1)),
            by_row((1, 1, length)),
        ]
        + [resident((wide, depth))] * len(earlier)
        + [ELSEWHERE] * len(after),
        out_specs=[resident(shape)]
        + [by_row((1, part, depth))] * 4
        + [by_row((1, 1, wide))],
        out_shape=[jax.ShapeDtypeStruct(shape, kind)]
        + [jax.ShapeDtypeStruct((count, part, depth), t) for t in (F32, BF16, F32, BF16)]
        + [jax.ShapeDtypeStruct((count, 1, wide), F32)],
        scratch_shapes=[pltpu.VMEM((wide, depth), F32)],
        compiler_params=pltpu.CompilerParams(vmem_limit_bytes=52 * MIB),
        cost_estimate=pl.CostEstimate(
            flops=count * length * wide * (4 * depth + 40 * length // 3),
            bytes_accessed=count * length * (3 * depth + 3 * wide) * 2,
            transcendentals=count * length * length * wide // (3 * HEAD_DIM),
        ),
        name="attend_backward",
    )(saved, kept, *grads, weight, weight, weight, seg_key, seg_query, *earlier, *after)


def column(shape):
    return pl.BlockSpec(shape, lambda i: (0, i))


def expand_piece(ref):
    return jnp.concatenate([flat(ref[:, i]) for i in range(ref.shape[1])], axis=1)


def reduce_piece(ref):
    columns = ref.shape[1] // 2
    halves = [
        jnp.concatenate([ref[:, half * columns + i] for i in range(columns)], axis=2)
        for half in range(2)
    ]
    return flat(jnp.concatenate(halves, axis=1))


def feed_kernel(*refs):
    sources, (expand, bias, reduce, act, slope, own_out, other_out, far_sum) = (
        refs[: 2 * CHUNKS],
        refs[2 * CHUNKS :],
    )
    step = pl.program_id(0)

    @pl.when(step == 0)
    def _():
        own_out[...] = jnp.zeros_like(own_out)
        far_sum[...] = jnp.zeros_like(far_sum)

    into = expand_piece(expand)
    back = reduce_piece(reduce)
    block = 256
    per = sources[0].shape[0] // block
    half_count = CHUNKS * per

    def inner(index):
        start = index % per * block
        return dot(sources[index // per][start : start + block], into) + bias[...]

    ahead = inner(0)
    for index in range(2 * half_count):
        inside = ahead
        if index + 1 < 2 * half_count:
            ahead = inner(index + 1)
        total = own_out if index < half_count else far_sum
        at = slice(index % half_count * block, (index % half_count + 1) * block)
        to = slice(index * block, (index + 1) * block)
        square = inside * inside
        curve = jnp.tanh(inside * (0.7978845608028654 + 0.7978845608028654 * 0.044715 * square))
        half = 0.5 * curve + 0.5
        active = (inside * half).astype(BF16)
        act[to] = active
        tilt = 0.7978845608028654 * 0.5 + 0.7978845608028654 * 1.5 * 0.044715 * square
        slope[to] = (half + inside * (1.0 - curve * curve) * tilt).astype(BF16)
        total[at] += dot(active, back)

    @pl.when(step == pl.num_programs(0) - 1)
    def _():
        other_out[...] = far_sum[...].astype(BF16)


def feed_weights(weights, pieces, columns):
    chips, _, rows, _ = weights.shape
    return [
        pl.BlockSpec((chips, pieces, rows, PIECE), lambda i: (0, i, 0, 0)),
        pl.BlockSpec(
            (pieces * PIECE // (2 * rows), 2 * columns, rows, PIECE), lambda i: (i, 1, 0, 0)
        ),
    ]


def feed(own, other, weights, bias):
    block, depth = own[0].shape
    rows = CHUNKS * block
    hidden = bias.shape[1]
    pieces = 2
    wide = pieces * PIECE
    expand_spec, reduce_spec = feed_weights(weights, pieces, depth // PIECE)
    return pl.pallas_call(
        feed_kernel,
        grid=(hidden // wide,),
        in_specs=[resident((block, depth))] * (2 * CHUNKS)
        + [expand_spec, column((1, wide)), reduce_spec],
        out_specs=[column((2 * rows, wide))] * 2 + [resident((rows, depth))] * 2,
        out_shape=[jax.ShapeDtypeStruct((2 * rows, hidden), BF16)] * 2
        + [
            jax.ShapeDtypeStruct((rows, depth), F32),
            jax.ShapeDtypeStruct((rows, depth), BF16),
        ],
        scratch_shapes=[pltpu.VMEM((rows, depth), F32)],
        compiler_params=pltpu.CompilerParams(vmem_limit_bytes=56 * MIB),
        cost_estimate=pl.CostEstimate(
            flops=8 * rows * depth * hidden,
            bytes_accessed=4 * rows * (2 * hidden + 3 * depth),
            transcendentals=2 * rows * hidden,
        ),
        name="feed_forward",
    )(*own, *other, weights, bias, weights)


def feed_back_kernel(*refs):
    grads, sources = refs[: 2 * CHUNKS], refs[2 * CHUNKS : 4 * CHUNKS]
    act, slope, expand, reduce, weight_grad, bias_grad, own_out, other_out, far_sum, inside = refs[
        4 * CHUNKS :
    ]
    step = pl.program_id(0)
    block = grads[0].shape[0]

    @pl.when(step == 0)
    def _():
        own_out[...] = jnp.zeros_like(own_out)
        far_sum[...] = jnp.zeros_like(far_sum)

    into = expand_piece(expand)
    back = reduce_piece(reduce)
    bias_sum = jnp.zeros(bias_grad.shape, F32)
    for index in range(2 * CHUNKS):
        total = own_out if index < CHUNKS else far_sum
        at = slice(index % CHUNKS * block, (index % CHUNKS + 1) * block)
        to = slice(index * block, (index + 1) * block)
        grad_act = dot(grads[index][...], back, (1, 1))
        part = (grad_act * slope[to].astype(F32)).astype(BF16)
        inside[to] = part
        bias_sum += jnp.sum(part.astype(F32), axis=0, keepdims=True)
        total[at] += dot(part, into, (1, 1))
    bias_grad[...] = bias_sum
    chips, pieces, height, _ = weight_grad.shape
    columns = pieces // 4
    wide = inside.shape[1]
    reduce_grad = sum(
        dot(act[i * block : (i + 1) * block], grad[...], (0, 0)) for i, grad in enumerate(grads)
    )
    count = wide // (2 * height)
    reduce_grad = reduce_grad.reshape(count, 2 * height, reduce_grad.shape[1]).astype(BF16)
    mine = pl.ds(step * count, count)
    for half in range(2):
        for i in range(columns):
            weight_grad[mine, (2 + half) * columns + i] = reduce_grad[
                :, half * height : (half + 1) * height, i * PIECE : (i + 1) * PIECE
            ]
    flipped = sum(
        dot(inside[i * block : (i + 1) * block], source[...], (0, 0))
        for i, source in enumerate(sources)
    )
    expand_grad = jnp.transpose(flipped).reshape(chips, height, wide).astype(BF16)
    for i in range(wide // PIECE):
        weight_grad[:, step * (wide // PIECE) + i] = expand_grad[
            :, :, i * PIECE : (i + 1) * PIECE
        ]

    @pl.when(step == pl.num_programs(0) - 1)
    def _():
        other_out[...] = far_sum[...].astype(BF16)


def feed_back(grads, sources, act, slope, weights):
    block, depth = grads[0].shape
    rows = CHUNKS * block
    hidden = act.shape[1]
    chips, _, height, _ = weights.shape
    pieces = 2 * hidden // PIECE
    expand_spec, reduce_spec = feed_weights(weights, 2, depth // PIECE)
    wide = 2 * PIECE
    return pl.pallas_call(
        feed_back_kernel,
        grid=(hidden // wide,),
        in_specs=[resident((block, depth))] * (4 * CHUNKS)
        + [column((2 * rows, wide))] * 2
        + [expand_spec, reduce_spec],
        out_specs=[
            resident((chips, pieces, height, PIECE)),
            column((1, wide)),
        ]
        + [resident((rows, depth))] * 2,
        out_shape=[
            jax.ShapeDtypeStruct((chips, pieces, height, PIECE), BF16),
            jax.ShapeDtypeStruct((1, hidden), F32),
            jax.ShapeDtypeStruct((rows, depth), F32),
            jax.ShapeDtypeStruct((rows, depth), BF16),
        ],
        scratch_shapes=[
            pltpu.VMEM((rows, depth), F32),
            pltpu.VMEM((2 * rows, wide), BF16),
        ],
        compiler_params=pltpu.CompilerParams(vmem_limit_bytes=56 * MIB),
        cost_estimate=pl.CostEstimate(
            flops=16 * rows * depth * hidden,
            bytes_accessed=4 * rows * (2 * hidden + 5 * depth) + 8 * depth * hidden,
            transcendentals=0,
        ),
        name="feed_backward",
    )(*grads, *sources, act, slope, weights, weights)


def normalize(values):
    center = values - jnp.mean(values, axis=-1, keepdims=True)
    inverse = lax.rsqrt(jnp.mean(center * center, axis=-1, keepdims=True) + 1e-05)
    return (center * inverse, inverse)


def normalize_back(incoming, scaled, inverse, gain):
    grad_scaled = incoming * gain
    mean_one = jnp.mean(grad_scaled, axis=-1, keepdims=True)
    mean_two = jnp.mean(grad_scaled * scaled, axis=-1, keepdims=True)
    return inverse * (grad_scaled - mean_one - scaled * mean_two)


def add_sums(out, *rows):
    rows = [jnp.sum(row, axis=0, keepdims=True) for row in rows]
    rows.append(jnp.zeros((out.shape[0] - len(rows), out.shape[1]), F32))
    rows = jnp.concatenate(rows, axis=0)

    @pl.when(pl.program_id(0) == 0)
    def _():
        out[...] = rows

    @pl.when(pl.program_id(0) > 0)
    def _():
        out[...] += rows


OUT_BIAS, GAIN_ONE, SHIFT_ONE, RED_BIAS, GAIN_TWO, SHIFT_TWO = (slice(i, i + 1) for i in range(2, 8))
SCALAR = pl.BlockSpec(memory_space=pltpu.SMEM)
ROW_BLOCK = 256


def row_call(kernel, name, ins, outs, arrays, rows, cost):
    return pl.pallas_call(
        kernel,
        grid=(rows // ROW_BLOCK,),
        in_specs=ins,
        out_specs=[spec for spec, _ in outs],
        out_shape=[shape for _, shape in outs],
        compiler_params=pltpu.CompilerParams(vmem_limit_bytes=48 * MIB),
        cost_estimate=pl.CostEstimate(flops=cost, bytes_accessed=rows << 14, transcendentals=rows),
        name=name,
    )(*arrays)


def row_block(width, first=0):
    return pl.BlockSpec((ROW_BLOCK, width), lambda i: (i + first, 0))


def first_norm_kernel(place, m0, m1, m2, m3, tokens, weight, vectors, low, scaled, inverse, mixed):
    total = tokens[...].astype(F32) + vectors[OUT_BIAS]
    parts = [m[...].reshape(ROW_BLOCK, -1) for m in (m0, m1, m2, m3)]
    mixed[...] = jnp.concatenate(parts, axis=1)
    for step, part in enumerate(parts):
        total += dot(part, weight[place[0] ^ step])
    scaled_one, inverse_one = normalize(total)
    scaled[...] = scaled_one
    inverse[...] = inverse_one
    low[...] = (scaled_one * vectors[GAIN_ONE] + vectors[SHIFT_ONE]).astype(BF16)


def first_norm(place, mixed, rows, weight, vectors, chunk):
    width = rows.shape[1]
    count, part, lanes = mixed[0].shape
    size = count * part
    steps = size // ROW_BLOCK
    return row_call(
        first_norm_kernel,
        "first_norm",
        [SCALAR]
        + [by_row((ROW_BLOCK // part, part, lanes))] * 4
        + [row_block(width, chunk * steps), resident(weight.shape), resident(vectors.shape)],
        [
            (row_block(width), jax.ShapeDtypeStruct((size, width), BF16)),
            (row_block(width), jax.ShapeDtypeStruct((size, width), F32)),
            (row_block(1), jax.ShapeDtypeStruct((size, 1), F32)),
            (row_block(width), jax.ShapeDtypeStruct((size, width), BF16)),
        ],
        (place, *mixed, rows, weight, vectors),
        size,
        2 * size * width * width,
    )


def second_norm_kernel(scaled, own, far, grad_out, vectors, layer, grad, low, sums):
    first = scaled[...] * vectors[GAIN_ONE] + vectors[SHIFT_ONE]
    reduced = own[...] + far[...].astype(F32) + vectors[RED_BIAS]
    scaled_two, inverse_two = normalize(first + reduced)
    layer[...] = (scaled_two * vectors[GAIN_TWO] + vectors[SHIFT_TWO]).astype(BF16)
    incoming = grad_out[...].astype(F32)
    grad_second = normalize_back(incoming, scaled_two, inverse_two, vectors[GAIN_TWO])
    grad[...] = grad_second
    low[...] = grad_second.astype(BF16)
    add_sums(sums, incoming * scaled_two, incoming, grad_second.astype(BF16).astype(F32))


def second_norm(scaled, own, far, grad_rows, vectors, chunk):
    size, width = scaled.shape
    steps = size // ROW_BLOCK
    return row_call(
        second_norm_kernel,
        "second_norm",
        [row_block(width)]
        + [row_block(width, chunk * steps)] * 3
        + [resident(vectors.shape)],
        [
            (row_block(width), jax.ShapeDtypeStruct((size, width), BF16)),
            (row_block(width), jax.ShapeDtypeStruct((size, width), F32)),
            (row_block(width), jax.ShapeDtypeStruct((size, width), BF16)),
            (resident((8, width)), jax.ShapeDtypeStruct((8, width), F32)),
        ],
        (scaled, own, far, grad_rows, vectors),
        size,
        size * width * 40,
    )


def first_back_kernel(
    place, grad, own, far, scaled, inverse, weight, vectors, hidden, low, m0, m1, m2, m3, sums
):
    incoming = grad[...] + own[...] + far[...].astype(F32)
    grad_hidden = normalize_back(incoming, scaled[...], inverse[...], vectors[GAIN_ONE])
    hidden[...] = grad_hidden
    attended = grad_hidden.astype(BF16)
    low[...] = attended
    for step, out in enumerate((m0, m1, m2, m3)):
        out[...] = dot(attended, weight[place[0] ^ step], (1, 1)).astype(BF16).reshape(out.shape)
    add_sums(sums, incoming * scaled[...], incoming, attended.astype(F32))


def first_back(place, grad, own, far, scaled, inverse, weight, vectors, chunk, part):
    size, width = grad.shape
    steps = size // ROW_BLOCK
    lanes = weight.shape[1]
    return row_call(
        first_back_kernel,
        "first_back",
        [SCALAR, row_block(width)]
        + [row_block(width, chunk * steps)] * 2
        + [row_block(width), row_block(1), resident(weight.shape), resident(vectors.shape)],
        [
            (row_block(width), jax.ShapeDtypeStruct((size, width), F32)),
            (row_block(width), jax.ShapeDtypeStruct((size, width), BF16)),
        ]
        + [
            (
                by_row((ROW_BLOCK // part, part, lanes)),
                jax.ShapeDtypeStruct((size // part, part, lanes), BF16),
            )
        ]
        * 4
        + [(resident((8, width)), jax.ShapeDtypeStruct((8, width), F32))],
        (place, grad, own, far, scaled, inverse, weight, vectors),
        size,
        2 * size * width * width,
    )


def output_grad_kernel(place, *refs):
    mixed, grads, out = refs[:CHUNKS], refs[CHUNKS:-1], refs[-1]
    lanes = out.shape[1]
    for step in range(out.shape[0]):
        at = slice(step * lanes, (step + 1) * lanes)
        out[place[0] ^ step] = sum(
            dot(m[:, at], g[...], (0, 0)) for m, g in zip(mixed, grads)
        ).astype(BF16)


def output_back(place, mixed, grads, ctx_size):
    size, width = mixed[0].shape
    shape = (ctx_size, width // ctx_size, width)
    return pl.pallas_call(
        output_grad_kernel,
        grid=(1,),
        in_specs=[SCALAR] + [resident((size, width))] * (2 * CHUNKS),
        out_specs=resident(shape),
        out_shape=jax.ShapeDtypeStruct(shape, BF16),
        compiler_params=pltpu.CompilerParams(vmem_limit_bytes=48 * MIB),
        cost_estimate=pl.CostEstimate(
            flops=2 * CHUNKS * size * width * width,
            bytes_accessed=4 * width * (width + CHUNKS * size),
            transcendentals=0,
        ),
        name="output_backward",
    )(place, *mixed, *grads)


def on_device(
    sizes,
    tokens,
    segment_ids,
    project_weight,
    query_bias,
    value_bias,
    output_weight,
    output_bias,
    first_gain,
    first_shift,
    expand_weight,
    expand_bias,
    reduce_weight,
    reduce_bias,
    second_gain,
    second_shift,
    grad_out,
):
    chips = sizes["z"] * sizes["y"] * sizes["x"]
    ctx_size = sizes["x"] * sizes["c"]
    everyone = chips * sizes["c"]
    seq_count, part, width = tokens.shape
    rows_count = seq_count * part
    hidden = expand_weight.shape[1]
    share = width // everyone
    own_hidden = hidden // 2
    lanes = width // ctx_size
    place = lax.axis_index(CTX)
    core = lax.axis_index("c")
    low_core = core == 0

    def hop(array, step):
        return lax.ppermute(array, CTX, [(i, i ^ step) for i in range(ctx_size)])

    def swap(array):
        return lax.ppermute(array, "c", [(0, 1), (1, 0)])

    def chosen(array, index, axis):
        return lax.dynamic_index_in_dim(array, index, axis, keepdims=False)

    def pair(own, other, axis, low):
        return jnp.where(
            low, jnp.stack([own, other], axis=axis), jnp.stack([other, own], axis=axis)
        )

    def by_core(own, other, axis):
        return pair(own, other, axis, low_core)

    def bit_of(name, step):
        return (lax.axis_index(name) // step) % 2

    def trade(array, name, step=1):
        return lax.ppermute(array, name, [(i, i ^ step) for i in range(sizes[name])])

    def widen(array, name, axis=0, step=1):
        return pair(array, trade(array, name, step), axis, bit_of(name, step) == 0)

    def halve(array, axis, name, step=1):
        me = bit_of(name, step)
        return chosen(array, me, axis).astype(F32) + trade(
            chosen(array, 1 - me, axis), name, step
        ).astype(F32)

    z_steps = [1 << i for i in range(sizes["z"].bit_length() - 1)]

    def z_gather(array):
        for index, step in enumerate(z_steps[::-1]):
            array = widen(array, "z", index, step)
        return array

    def z_scatter(blocks, kind=BF16):
        for step in z_steps:
            blocks = blocks.reshape((blocks.shape[0] // 2, 2) + blocks.shape[1:])
            blocks = halve(blocks.astype(kind), 1, "z", step)
        return blocks[0]

    seg_parts = segment_ids.reshape(seq_count, ctx_size, part)
    seg = jnp.concatenate([chosen(seg_parts, place ^ r, 1) for r in range(ctx_size)], axis=1)
    seg_key = seg[:, :, None]
    seg_query = seg[:, None, :]

    vectors = (
        query_bias,
        value_bias,
        output_bias,
        first_gain,
        first_shift,
        reduce_bias,
        second_gain,
        second_shift,
        expand_bias,
    )
    vector_count = 8 * share + expand_bias.shape[0]
    filler = jnp.concatenate(
        [jnp.pad(v[None], ((0, 0), (0, 3 * lanes - v.shape[0]))) for v in vectors]
        + [jnp.zeros((16 - len(vectors), 3 * lanes), BF16)]
    )
    held = jnp.stack(
        [
            jnp.concatenate(
                [
                    jnp.concatenate(
                        [
                            project_weight[:, (ctx_size * j + p) * lanes :][:, :lanes]
                            for j in range(3)
                        ],
                        axis=1,
                    ),
                    filler,
                ]
            )
            for p in range(ctx_size)
        ]
    )
    held = lax.all_to_all(held, CTX, 0, 0, tiled=True)
    sent, held = lax.optimization_barrier((tokens, held))
    across = hop(sent, 2)
    gathered = (tokens, swap(sent), across, swap(across))
    mine = jnp.concatenate(
        [held[:, :share, j * lanes : (j + 1) * lanes].reshape(-1, lanes) for j in range(3)]
    )
    vector_rows = held[:, share:, :lanes].reshape(-1, lanes)
    out_pieces = jnp.concatenate(
        [output_weight[:, i * lanes : (i + 1) * lanes] for i in range(ctx_size)]
    )
    full_project = lax.all_gather(
        jnp.concatenate([widen(out_pieces, "x").reshape(-1, lanes), mine, vector_rows]),
        SEQ,
        axis=0,
    )
    packed = full_project[:, -16 * ctx_size :].reshape(everyone, 16, lanes).astype(F32)
    exp_bias = chosen(
        packed[:, 8, : expand_bias.shape[0]].reshape(chips, 2, -1), core, 1
    ).reshape(1, own_hidden)
    vectors = jnp.swapaxes(packed[:, :8, :share], 0, 1).reshape(8, width)
    full_query, full_value = vectors[0], vectors[1]
    bias_all = jnp.concatenate(
        [
            lax.dynamic_slice_in_dim(full_query, place * lanes, lanes),
            jnp.zeros((lanes,), F32),
            lax.dynamic_slice_in_dim(full_value, place * lanes, lanes),
        ]
    )[None]

    columns = expand_weight.reshape(share, chips, 2, own_hidden // chips)
    own_columns = chosen(columns, core, 2).reshape(share, own_hidden)
    far_columns = chosen(columns, 1 - core, 2).reshape(share, own_hidden)
    both = by_core(own_columns, swap(far_columns), 0)

    def in_pieces(array):
        rows_of, wide = array.shape
        return jnp.swapaxes(array.reshape(rows_of, wide // PIECE, PIECE), 0, 1).reshape(
            -1, 2 * share, PIECE
        )

    own_pieces = jnp.concatenate(
        [
            in_pieces(both.reshape(2 * share, own_hidden)),
            jnp.swapaxes(
                reduce_weight.reshape(2, 2 * share, width // PIECE, PIECE), 1, 2
            ).reshape(-1, 2 * share, PIECE),
        ]
    )
    own_pieces = hold(own_pieces, [across])
    weights = lax.all_gather(widen(own_pieces, "x"), SEQ, axis=0).reshape(
        chips, -1, 2 * share, PIECE
    )

    rows = tokens.reshape(rows_count, width)
    where = place.reshape(1).astype(jnp.int32)
    seqs = seq_count // CHUNKS
    saved, kept_rows, mixed_low, first_low, scaled_one, inverse_one = [], [], [], [], [], []
    for index in range(CHUNKS):
        at = slice(index * seqs, (index + 1) * seqs)
        *mixed, all_rows, kept = attend(
            gathered, full_project, bias_all, seg_key[at], seg_query[at], at.start, []
        )
        kept_rows.append(all_rows)
        saved.append(kept)
        if index == 0:
            out_half = unpack(full_project, share, width, mixed[:1])
            full_output = by_core(out_half, swap(out_half), 1).reshape(ctx_size, lanes, width)
        arrived = [mixed[0]] + [hop(mixed[r], r) for r in (1, 2, 3)]
        low, scaled, inverse, joined = first_norm(
            where, arrived, rows, full_output, vectors, index
        )
        mixed_low.append(joined)
        first_low.append(low)
        scaled_one.append(scaled)
        inverse_one.append(inverse)
    first_far = [swap(low) for low in first_low]
    act, slope, own_sum, far_sum = feed(first_low, first_far, weights, exp_bias)
    far_sum = swap(far_sum)

    grad_rows = grad_out.reshape(rows_count, width)
    layer_parts, grad_second, grad_reduced, second_sums = zip(
        *(
            second_norm(scaled_one[index], own_sum, far_sum, grad_rows, vectors, index)
            for index in range(CHUNKS)
        )
    )
    layer_work = jnp.concatenate(layer_parts, axis=0).reshape(tokens.shape)
    weight_grad, expand_bias_grad, own_back, far_back = feed_back(
        grad_reduced + tuple(swap(grad) for grad in grad_reduced),
        first_low + first_far,
        act,
        slope,
        weights,
    )
    weight_owned = lax.psum_scatter(
        weight_grad.reshape((-1, sizes["x"]) + weight_grad.shape[1:]),
        SEQ,
        scatter_dimension=0,
        tiled=True,
    )[0]
    far_back = swap(far_back)
    grad_hidden, grad_attended, grad_mixed, first_sums = [], [], [], []
    for index in range(CHUNKS):
        grad, low, *mixed, sums = first_back(
            where,
            grad_second[index],
            own_back,
            far_back,
            scaled_one[index],
            inverse_one[index],
            full_output,
            vectors,
            index,
            part,
        )
        grad_hidden.append(grad.reshape(seqs, part, width))
        grad_attended.append(low)
        grad_mixed.append([mixed[0]] + [hop(mixed[r], r) for r in (1, 2, 3)])
        first_sums.append(sums)
    output_grad = output_back(where, mixed_low, grad_attended, ctx_size).reshape(
        sizes["z"], 2, sizes["x"], 2, share, width
    )
    output_grad = halve(output_grad, 3, "c").astype(BF16)

    project_grad = []
    work_parts = []
    across_sums = []
    work_hops = []
    sum_parts = []
    for index in range(CHUNKS):
        at = slice(index * seqs, (index + 1) * seqs)
        project_part, r0, r1, r2, r3, sums = attend_back(
            saved[index],
            kept_rows[index],
            grad_mixed[index],
            full_project,
            seg_key[at],
            seg_query[at],
            project_grad,
            index == CHUNKS - 1,
            work_hops[:index],
        )
        project_grad = [project_part]
        across_sums.append((r2 + swap(r3).astype(F32)).astype(BF16))
        work_hops.append(hop(across_sums[index], 2))
        work_parts.append(
            grad_hidden[index] + r0 + swap(r1).astype(F32) + work_hops[index].astype(F32)
        )
        sum_parts.append(sums)
    grad_work = jnp.concatenate(work_parts, axis=0)
    blocks = halve(
        project_grad[0].reshape(sizes["z"], 2, ctx_size * share, 3 * lanes), 1, "y"
    ).astype(BF16)
    later = [blocks, work_hops[1]]
    output_grad = halve(hold(output_grad, later), 2, "x").astype(BF16)
    output_grad = halve(output_grad, 1, "y")
    output_owned = z_scatter(output_grad)
    for step in z_steps:
        blocks = blocks.astype(BF16).reshape((blocks.shape[0] // 2, 2) + blocks.shape[1:])
        blocks = halve(blocks, 1, "z", step)
    weight_owned = halve(weight_owned, 0, "x")
    held = lax.all_to_all(
        hold(blocks.astype(F32).reshape(ctx_size, share, 3 * lanes), [weight_owned]),
        CTX,
        0,
        0,
        tiled=True,
    )
    project_owned = jnp.concatenate(
        [
            held[p, :, j * lanes : (j + 1) * lanes]
            for j in range(3)
            for p in range(ctx_size)
        ],
        axis=1,
    )
    expand_pieces = own_hidden // PIECE
    far_rows = jnp.swapaxes(
        weight_owned[:expand_pieces].reshape(expand_pieces, 2, share, PIECE), 0, 1
    )
    expand_owned = by_core(
        jnp.swapaxes(chosen(far_rows, core, 0), 0, 1).reshape(share, chips, -1),
        jnp.swapaxes(swap(chosen(far_rows, 1 - core, 0)), 0, 1).reshape(share, chips, -1),
        2,
    ).reshape(share, hidden)
    reduce_owned = jnp.swapaxes(
        weight_owned[expand_pieces:].reshape(2, width // PIECE, 2 * share, PIECE), 1, 2
    ).reshape(4 * share, width)

    column_sums = jnp.sum(jnp.concatenate(sum_parts, axis=0), axis=(0, 1))
    zeros = jnp.zeros((width,), F32)
    first_sums, second_sums = sum(first_sums), sum(second_sums)
    grad_vectors = (
        lax.dynamic_update_slice_in_dim(zeros, column_sums[:lanes], place * lanes, 0),
        lax.dynamic_update_slice_in_dim(zeros, column_sums[2 * lanes :], place * lanes, 0),
        first_sums[2],
        first_sums[0],
        first_sums[1],
        second_sums[2],
        second_sums[0],
        second_sums[1],
    )
    hidden_sums = expand_bias_grad.reshape(chips, 1, own_hidden // chips)
    hidden_sums = jnp.where(
        low_core,
        jnp.concatenate([hidden_sums, jnp.zeros_like(hidden_sums)], axis=1),
        jnp.concatenate([jnp.zeros_like(hidden_sums), hidden_sums], axis=1),
    )
    packed_grads = jnp.concatenate(
        [vector.reshape(everyone, share) for vector in grad_vectors]
        + [hidden_sums.reshape(everyone, -1)],
        axis=1,
    )
    packed_grads = hold(packed_grads, later).reshape(
        sizes["z"], 2, sizes["x"], 2, vector_count
    )
    for axis, name in ((3, "c"), (2, "x"), (1, "y")):
        packed_grads = halve(packed_grads, axis, name)
    owned = z_scatter(packed_grads, F32)
    small = [owned[i * share : (i + 1) * share] for i in range(8)]
    return (
        layer_work,
        grad_work,
        project_owned.astype(F32),
        small[0],
        small[1],
        output_owned.astype(F32),
        small[2],
        small[3],
        small[4],
        expand_owned.astype(F32),
        owned[8 * share :],
        reduce_owned.astype(F32),
        small[5],
        small[6],
        small[7],
    )


def solution(mesh):
    seq_size, ctx_size = mesh.shape["seq"], mesh.shape["ctx"]
    sizes = {"z": seq_size // 2, "y": 2, "x": ctx_size // 2, "c": 2}
    fine = Mesh(mesh.devices.reshape(tuple(sizes.values())), tuple(sizes))
    rows = P(SEQ, CTX, None)
    matrix = P(ALL, None)
    vector = P(ALL)
    return jax.shard_map(
        functools.partial(on_device, sizes),
        mesh=fine,
        in_specs=(
            rows,
            P(SEQ, None),
            matrix,
            vector,
            vector,
            matrix,
            vector,
            vector,
            vector,
            matrix,
            vector,
            matrix,
            vector,
            vector,
            vector,
            rows,
        ),
        out_specs=(
            rows,
            rows,
            matrix,
            vector,
            vector,
            matrix,
            vector,
            vector,
            vector,
            matrix,
            vector,
            matrix,
            vector,
            vector,
            vector,
        ),
        check_vma=False,
    )
```

```python
import functools

import jax
import jax.numpy as jnp
from jax import lax
from jax.experimental import pallas as pl
from jax.experimental.pallas import tpu as pltpu
from jax.sharding import Mesh
from jax.sharding import PartitionSpec as P

HEADS = 16
HEAD_DIM = 64
CHUNKS = 2
PIECE = 256
MIB = 1 << 20
CHIPS = ("z", "y", "x")
SEQ = ("z", "y")
CTX = ("x", "c")
ALL = ("z", "y", "x", "c")
F32 = jnp.float32
BF16 = jnp.bfloat16
ELSEWHERE = pl.BlockSpec(memory_space=pl.ANY)


def dot(left, right, contract=(1, 0)):
    return lax.dot_general(
        left, right, (((contract[0],), (contract[1],)), ((), ())), preferred_element_type=F32
    )


def resident(shape):
    return pl.BlockSpec(shape, lambda i: (0,) * len(shape), pipeline_mode=pl.Buffered(1))


def by_row(shape):
    return pl.BlockSpec(shape, lambda i: (i,) + (0,) * (len(shape) - 1))


def flat(block):
    wide = block.shape[-1]
    if block.shape[-2] % 16:
        return block.astype(F32).reshape(-1, wide).astype(BF16)
    return block.reshape(-1, wide)


def hold_kernel(source, *refs):
    refs[-1][...] = source[...]


def hold(array, after):
    return pl.pallas_call(
        hold_kernel,
        grid=(1,),
        in_specs=[resident(array.shape)] + [ELSEWHERE] * len(after),
        out_specs=resident(array.shape),
        out_shape=jax.ShapeDtypeStruct(array.shape, array.dtype),
        compiler_params=pltpu.CompilerParams(vmem_limit_bytes=16 * MIB),
        name="hold",
    )(array, *after)


def unpack_kernel(pieces, *refs):
    out = refs[-1]
    height, lanes = out.shape[2], pieces.shape[2]
    for half in range(2):
        for i in range(out.shape[3] // lanes):
            start = (half * (out.shape[3] // lanes) + i) * height
            out[:, half, :, i * lanes : (i + 1) * lanes] = pieces[:, start : start + height]


def unpack(gathered, share, width, after):
    count, _, lanes = gathered.shape
    columns = width // lanes
    if share % 16:
        pieces = gathered[:, : 2 * columns * share].reshape(count, 2, columns, share, lanes)
        return jnp.swapaxes(pieces, 2, 3).reshape(2 * count, share, width)
    return pl.pallas_call(
        unpack_kernel,
        grid=(1,),
        in_specs=[pl.BlockSpec((count, 2 * columns * share, lanes), lambda i: (0, 0, 0))]
        + [ELSEWHERE] * len(after),
        out_specs=pl.BlockSpec((count, 2, share, width), lambda i: (0, 0, 0, 0)),
        out_shape=jax.ShapeDtypeStruct((count, 2, share, width), BF16),
        compiler_params=pltpu.CompilerParams(vmem_limit_bytes=16 * MIB),
        name="unpack",
    )(gathered, *after).reshape(2 * count, share, width)


def softmax_down(scores, allowed):
    scores = jnp.where(allowed, scores, -1e30)
    top = jnp.max(scores, axis=0, keepdims=True)
    expo = jnp.exp(scores - top)
    total = jnp.sum(expo, axis=0, keepdims=True)
    return expo * (1.0 / total)


def head_lanes(width, head):
    lane = lax.broadcasted_iota(jnp.int32, (1, width), 1)
    return (lane // HEAD_DIM == head).astype(F32)


def attend_kernel(late, t0, t1, t2, t3, wq, wk, wv, bias, seg_key, seg_query, *refs):
    m0, m1, m2, m3, kept, saved = refs[late:]
    part = t0.shape[1]
    rows = jnp.concatenate([t[0] for t in (t0, t1, t2, t3)], axis=0)
    kept[0] = rows
    width = wq.shape[2]
    queries, keys, values = [
        dot(rows, flat(w[...])) + bias[:, i * width : (i + 1) * width]
        for i, w in enumerate((wq, wk, wv))
    ]
    for i, part_of in enumerate((queries, keys, values)):
        saved[0, :, i * width : (i + 1) * width] = part_of.astype(BF16)
    queries = (queries.astype(BF16).astype(F32) * HEAD_DIM**-0.5).astype(BF16)
    keys = keys.astype(BF16).astype(F32)
    values_t = jnp.transpose(values).astype(BF16)
    allowed = seg_key[0] == seg_query[0]
    mixed = []
    for head in range(width // HEAD_DIM):
        own_keys = (keys * head_lanes(width, head)).astype(BF16)
        chances = softmax_down(dot(own_keys, queries, (1, 1)), allowed)
        own_values = values_t[head * HEAD_DIM : (head + 1) * HEAD_DIM]
        mixed.append(dot(own_values, chances.astype(BF16)))
    mixed = jnp.transpose(jnp.concatenate(mixed, axis=0)).astype(BF16)
    for index, out in enumerate((m0, m1, m2, m3)):
        out[0] = mixed[index * part : (index + 1) * part]


def project_specs(weight, depth):
    shape = (weight.shape[0], depth // weight.shape[0], weight.shape[2])
    return [
        pl.BlockSpec(shape, lambda i, j=j: (0, j + 2, 0), pipeline_mode=pl.Buffered(1))
        for j in range(3)
    ]


def attend(tokens, weight, bias, seg_key, seg_query, first, after):
    count, part, depth = tokens[0].shape
    count = count // CHUNKS
    wide = bias.shape[1]
    length = 4 * part
    return pl.pallas_call(
        functools.partial(attend_kernel, len(after)),
        grid=(count,),
        in_specs=[pl.BlockSpec((1, part, depth), lambda i: (i + first, 0, 0))] * 4
        + project_specs(weight, depth)
        + [
            resident((1, wide)),
            by_row((1, length, 1)),
            by_row((1, 1, length)),
        ]
        + [ELSEWHERE] * len(after),
        out_specs=[by_row((1, part, wide // 3))] * 4
        + [by_row((1, length, depth)), by_row((1, length, wide))],
        out_shape=[jax.ShapeDtypeStruct((count, part, wide // 3), BF16)] * 4
        + [
            jax.ShapeDtypeStruct((count, length, depth), BF16),
            jax.ShapeDtypeStruct((count, length, wide), BF16),
        ],
        compiler_params=pltpu.CompilerParams(vmem_limit_bytes=40 * MIB),
        cost_estimate=pl.CostEstimate(
            flops=count * length * wide * (2 * depth + 16 * length // 3),
            bytes_accessed=count * length * (depth + 2 * wide) * 2,
            transcendentals=count * length * length * wide // (3 * HEAD_DIM),
        ),
        name="attend_forward",
    )(*tokens, weight, weight, weight, bias, seg_key, seg_query, *after)


def attend_back_kernel(
    late, earlier, saved, kept, g0, g1, g2, g3, wq, wk, wv, seg_key, seg_query, *refs
):
    grad_weight, r0, r1, r2, r3, sums, total = refs[late + earlier :]

    @pl.when(pl.program_id(0) == 0)
    def _():
        total[...] = refs[0][...] if earlier else jnp.zeros_like(total)

    part = g0.shape[1]
    width = saved.shape[2] // 3
    factor = HEAD_DIM**-0.5
    queries = (saved[0, :, :width].astype(F32) * factor).astype(BF16)
    keys = saved[0, :, width : 2 * width].astype(F32)
    values = saved[0, :, 2 * width :].astype(F32)
    keys_t = jnp.transpose(keys * factor).astype(BF16)
    grad_mixed = jnp.concatenate([g[0] for g in (g0, g1, g2, g3)], axis=0)
    allowed = seg_key[0] == seg_query[0]
    grad_queries = []
    grad_keys = None
    grad_values = None
    for head in range(width // HEAD_DIM):
        lanes = head_lanes(width, head)
        chances = softmax_down(
            dot((keys * lanes).astype(BF16), queries, (1, 1)), allowed
        )
        grad_weights = dot((values * lanes).astype(BF16), grad_mixed, (1, 1))
        inner = jnp.sum(chances * grad_weights, axis=0, keepdims=True)
        grad_scores = (chances * (grad_weights - inner)).astype(BF16)
        grad_queries.append(dot(keys_t[head * HEAD_DIM : (head + 1) * HEAD_DIM], grad_scores))
        keys_term = dot(grad_scores, queries)
        values_term = dot(chances.astype(BF16), grad_mixed)
        if head == 0:
            grad_keys, grad_values = keys_term, values_term
        else:
            here = lanes > 0.5
            grad_keys = jnp.where(here, keys_term, grad_keys)
            grad_values = jnp.where(here, values_term, grad_values)
    grad_queries = jnp.concatenate(grad_queries, axis=0)
    terms = [
        jnp.transpose(grad_queries).astype(BF16),
        grad_keys.astype(BF16),
        grad_values.astype(BF16),
    ]
    total[:width] += dot(grad_queries.astype(BF16), kept[0])
    for i, term in enumerate(terms):
        sums[0, :, i * width : (i + 1) * width] = jnp.sum(
            term.astype(F32), axis=0, keepdims=True
        )
        if i:
            total[i * width : (i + 1) * width] += dot(term, kept[0], (0, 0))
    rows = sum(dot(term, flat(w[...]), (1, 1)) for term, w in zip(terms, (wq, wk, wv)))
    for index, out in enumerate((r0, r1, r2, r3)):
        out[0] = rows[index * part : (index + 1) * part].astype(out.dtype)

    @pl.when(pl.program_id(0) == pl.num_programs(0) - 1)
    def _():
        if grad_weight.dtype == BF16:
            grad_weight[...] = jnp.transpose(total[...]).astype(BF16)
        else:
            grad_weight[...] = total[...]


def attend_back(saved, kept, grads, weight, seg_key, seg_query, earlier, done, after):
    count, part, width = grads[0].shape
    depth, wide = width * 4, width * 3
    length = 4 * part
    shape, kind = ((depth, wide), BF16) if done else ((wide, depth), F32)
    return pl.pallas_call(
        functools.partial(attend_back_kernel, len(after), len(earlier)),
        grid=(count,),
        in_specs=[by_row((1, length, wide)), by_row((1, length, depth))]
        + [by_row((1, part, width))] * 4
        + project_specs(weight, depth)
        + [
            by_row((1, length, 1)),
            by_row((1, 1, length)),
        ]
        + [resident((wide, depth))] * len(earlier)
        + [ELSEWHERE] * len(after),
        out_specs=[resident(shape)]
        + [by_row((1, part, depth))] * 4
        + [by_row((1, 1, wide))],
        out_shape=[jax.ShapeDtypeStruct(shape, kind)]
        + [jax.ShapeDtypeStruct((count, part, depth), t) for t in (F32, BF16, BF16, BF16)]
        + [jax.ShapeDtypeStruct((count, 1, wide), F32)],
        scratch_shapes=[pltpu.VMEM((wide, depth), F32)],
        compiler_params=pltpu.CompilerParams(vmem_limit_bytes=52 * MIB),
        cost_estimate=pl.CostEstimate(
            flops=count * length * wide * (4 * depth + 40 * length // 3),
            bytes_accessed=count * length * (3 * depth + 3 * wide) * 2,
            transcendentals=count * length * length * wide // (3 * HEAD_DIM),
        ),
        name="attend_backward",
    )(saved, kept, *grads, weight, weight, weight, seg_key, seg_query, *earlier, *after)


def column(shape):
    return pl.BlockSpec(shape, lambda i: (0, i))


def expand_piece(ref):
    return jnp.concatenate([flat(ref[:, i]) for i in range(ref.shape[1])], axis=1)


def reduce_piece(ref):
    columns = ref.shape[1] // 2
    halves = [
        jnp.concatenate([ref[:, half * columns + i] for i in range(columns)], axis=2)
        for half in range(2)
    ]
    return flat(jnp.concatenate(halves, axis=1))


def feed_kernel(*refs):
    sources, (expand, bias, reduce, act, slope, own_out, other_out, far_sum) = (
        refs[: 2 * CHUNKS],
        refs[2 * CHUNKS :],
    )
    step = pl.program_id(0)

    @pl.when(step == 0)
    def _():
        own_out[...] = jnp.zeros_like(own_out)
        far_sum[...] = jnp.zeros_like(far_sum)

    into = expand_piece(expand)
    back = reduce_piece(reduce)
    block = 256
    per = sources[0].shape[0] // block
    half_count = CHUNKS * per

    def inner(index):
        start = index % per * block
        return dot(sources[index // per][start : start + block], into) + bias[...]

    ahead = inner(0)
    for index in range(2 * half_count):
        inside = ahead
        if index + 1 < 2 * half_count:
            ahead = inner(index + 1)
        total = own_out if index < half_count else far_sum
        at = slice(index % half_count * block, (index % half_count + 1) * block)
        to = slice(index * block, (index + 1) * block)
        square = inside * inside
        curve = jnp.tanh(inside * (0.7978845608028654 + 0.7978845608028654 * 0.044715 * square))
        half = 0.5 * curve + 0.5
        active = (inside * half).astype(BF16)
        act[to] = active
        tilt = 0.7978845608028654 * 0.5 + 0.7978845608028654 * 1.5 * 0.044715 * square
        slope[to] = (half + inside * (1.0 - curve * curve) * tilt).astype(BF16)
        total[at] += dot(active, back)

    @pl.when(step == pl.num_programs(0) - 1)
    def _():
        other_out[...] = far_sum[...].astype(BF16)


def feed_weights(weights, pieces, columns):
    chips, _, rows, _ = weights.shape
    return [
        pl.BlockSpec((chips, pieces, rows, PIECE), lambda i: (0, i, 0, 0)),
        pl.BlockSpec(
            (pieces * PIECE // (2 * rows), 2 * columns, rows, PIECE), lambda i: (i, 1, 0, 0)
        ),
    ]


def feed(own, other, weights, bias):
    block, depth = own[0].shape
    rows = CHUNKS * block
    hidden = bias.shape[1]
    pieces = 2
    wide = pieces * PIECE
    expand_spec, reduce_spec = feed_weights(weights, pieces, depth // PIECE)
    return pl.pallas_call(
        feed_kernel,
        grid=(hidden // wide,),
        in_specs=[resident((block, depth))] * (2 * CHUNKS)
        + [expand_spec, column((1, wide)), reduce_spec],
        out_specs=[column((2 * rows, wide))] * 2 + [resident((rows, depth))] * 2,
        out_shape=[jax.ShapeDtypeStruct((2 * rows, hidden), BF16)] * 2
        + [
            jax.ShapeDtypeStruct((rows, depth), F32),
            jax.ShapeDtypeStruct((rows, depth), BF16),
        ],
        scratch_shapes=[pltpu.VMEM((rows, depth), F32)],
        compiler_params=pltpu.CompilerParams(vmem_limit_bytes=56 * MIB),
        cost_estimate=pl.CostEstimate(
            flops=8 * rows * depth * hidden,
            bytes_accessed=4 * rows * (2 * hidden + 3 * depth),
            transcendentals=2 * rows * hidden,
        ),
        name="feed_forward",
    )(*own, *other, weights, bias, weights)


def feed_back_kernel(*refs):
    grads, sources = refs[: 2 * CHUNKS], refs[2 * CHUNKS : 4 * CHUNKS]
    act, slope, expand, reduce, weight_grad, bias_grad, own_out, other_out, far_sum, inside = refs[
        4 * CHUNKS :
    ]
    step = pl.program_id(0)
    block = grads[0].shape[0]

    @pl.when(step == 0)
    def _():
        own_out[...] = jnp.zeros_like(own_out)
        far_sum[...] = jnp.zeros_like(far_sum)

    into = expand_piece(expand)
    back = reduce_piece(reduce)
    bias_sum = jnp.zeros(bias_grad.shape, F32)
    for index in range(2 * CHUNKS):
        total = own_out if index < CHUNKS else far_sum
        at = slice(index % CHUNKS * block, (index % CHUNKS + 1) * block)
        to = slice(index * block, (index + 1) * block)
        grad_act = dot(grads[index][...], back, (1, 1))
        part = (grad_act * slope[to].astype(F32)).astype(BF16)
        inside[to] = part
        bias_sum += jnp.sum(part.astype(F32), axis=0, keepdims=True)
        total[at] += dot(part, into, (1, 1))
    bias_grad[...] = bias_sum
    chips, pieces, height, _ = weight_grad.shape
    columns = pieces // 4
    wide = inside.shape[1]
    reduce_grad = sum(
        dot(act[i * block : (i + 1) * block], grad[...], (0, 0)) for i, grad in enumerate(grads)
    )
    count = wide // (2 * height)
    reduce_grad = reduce_grad.reshape(count, 2 * height, reduce_grad.shape[1]).astype(BF16)
    mine = pl.ds(step * count, count)
    for half in range(2):
        for i in range(columns):
            weight_grad[mine, (2 + half) * columns + i] = reduce_grad[
                :, half * height : (half + 1) * height, i * PIECE : (i + 1) * PIECE
            ]
    flipped = sum(
        dot(inside[i * block : (i + 1) * block], source[...], (0, 0))
        for i, source in enumerate(sources)
    )
    expand_grad = jnp.transpose(flipped).reshape(chips, height, wide).astype(BF16)
    for i in range(wide // PIECE):
        weight_grad[:, step * (wide // PIECE) + i] = expand_grad[
            :, :, i * PIECE : (i + 1) * PIECE
        ]

    @pl.when(step == pl.num_programs(0) - 1)
    def _():
        other_out[...] = far_sum[...].astype(BF16)


def feed_back(grads, sources, act, slope, weights):
    block, depth = grads[0].shape
    rows = CHUNKS * block
    hidden = act.shape[1]
    chips, _, height, _ = weights.shape
    pieces = 2 * hidden // PIECE
    expand_spec, reduce_spec = feed_weights(weights, 2, depth // PIECE)
    wide = 2 * PIECE
    return pl.pallas_call(
        feed_back_kernel,
        grid=(hidden // wide,),
        in_specs=[resident((block, depth))] * (4 * CHUNKS)
        + [column((2 * rows, wide))] * 2
        + [expand_spec, reduce_spec],
        out_specs=[
            resident((chips, pieces, height, PIECE)),
            column((1, wide)),
        ]
        + [resident((rows, depth))] * 2,
        out_shape=[
            jax.ShapeDtypeStruct((chips, pieces, height, PIECE), BF16),
            jax.ShapeDtypeStruct((1, hidden), F32),
            jax.ShapeDtypeStruct((rows, depth), F32),
            jax.ShapeDtypeStruct((rows, depth), BF16),
        ],
        scratch_shapes=[
            pltpu.VMEM((rows, depth), F32),
            pltpu.VMEM((2 * rows, wide), BF16),
        ],
        compiler_params=pltpu.CompilerParams(vmem_limit_bytes=56 * MIB),
        cost_estimate=pl.CostEstimate(
            flops=16 * rows * depth * hidden,
            bytes_accessed=4 * rows * (2 * hidden + 5 * depth) + 8 * depth * hidden,
            transcendentals=0,
        ),
        name="feed_backward",
    )(*grads, *sources, act, slope, weights, weights)


def normalize(values):
    center = values - jnp.mean(values, axis=-1, keepdims=True)
    inverse = lax.rsqrt(jnp.mean(center * center, axis=-1, keepdims=True) + 1e-05)
    return (center * inverse, inverse)


def normalize_back(incoming, scaled, inverse, gain):
    grad_scaled = incoming * gain
    mean_one = jnp.mean(grad_scaled, axis=-1, keepdims=True)
    mean_two = jnp.mean(grad_scaled * scaled, axis=-1, keepdims=True)
    return inverse * (grad_scaled - mean_one - scaled * mean_two)


def add_sums(out, *rows):
    rows = [jnp.sum(row, axis=0, keepdims=True) for row in rows]
    rows.append(jnp.zeros((out.shape[0] - len(rows), out.shape[1]), F32))
    rows = jnp.concatenate(rows, axis=0)

    @pl.when(pl.program_id(0) == 0)
    def _():
        out[...] = rows

    @pl.when(pl.program_id(0) > 0)
    def _():
        out[...] += rows


OUT_BIAS, GAIN_ONE, SHIFT_ONE, RED_BIAS, GAIN_TWO, SHIFT_TWO = (slice(i, i + 1) for i in range(2, 8))
SCALAR = pl.BlockSpec(memory_space=pltpu.SMEM)
ROW_BLOCK = 256


def row_call(kernel, name, ins, outs, arrays, rows, cost):
    return pl.pallas_call(
        kernel,
        grid=(rows // ROW_BLOCK,),
        in_specs=ins,
        out_specs=[spec for spec, _ in outs],
        out_shape=[shape for _, shape in outs],
        compiler_params=pltpu.CompilerParams(vmem_limit_bytes=48 * MIB),
        cost_estimate=pl.CostEstimate(flops=cost, bytes_accessed=rows << 14, transcendentals=rows),
        name=name,
    )(*arrays)


def row_block(width, first=0):
    return pl.BlockSpec((ROW_BLOCK, width), lambda i: (i + first, 0))


def first_norm_kernel(place, m0, m1, m2, m3, tokens, weight, vectors, low, scaled, inverse, mixed):
    total = tokens[...].astype(F32) + vectors[OUT_BIAS]
    parts = [m[...].reshape(ROW_BLOCK, -1) for m in (m0, m1, m2, m3)]
    mixed[...] = jnp.concatenate(parts, axis=1)
    for step, part in enumerate(parts):
        total += dot(part, weight[place[0] ^ step])
    scaled_one, inverse_one = normalize(total)
    scaled[...] = scaled_one
    inverse[...] = inverse_one
    low[...] = (scaled_one * vectors[GAIN_ONE] + vectors[SHIFT_ONE]).astype(BF16)


def first_norm(place, mixed, rows, weight, vectors, chunk):
    width = rows.shape[1]
    count, part, lanes = mixed[0].shape
    size = count * part
    steps = size // ROW_BLOCK
    return row_call(
        first_norm_kernel,
        "first_norm",
        [SCALAR]
        + [by_row((ROW_BLOCK // part, part, lanes))] * 4
        + [row_block(width, chunk * steps), resident(weight.shape), resident(vectors.shape)],
        [
            (row_block(width), jax.ShapeDtypeStruct((size, width), BF16)),
            (row_block(width), jax.ShapeDtypeStruct((size, width), F32)),
            (row_block(1), jax.ShapeDtypeStruct((size, 1), F32)),
            (row_block(width), jax.ShapeDtypeStruct((size, width), BF16)),
        ],
        (place, *mixed, rows, weight, vectors),
        size,
        2 * size * width * width,
    )


def second_norm_kernel(scaled, own, far, grad_out, vectors, layer, grad, low, sums):
    first = scaled[...] * vectors[GAIN_ONE] + vectors[SHIFT_ONE]
    reduced = own[...] + far[...].astype(F32) + vectors[RED_BIAS]
    scaled_two, inverse_two = normalize(first + reduced)
    layer[...] = (scaled_two * vectors[GAIN_TWO] + vectors[SHIFT_TWO]).astype(BF16)
    incoming = grad_out[...].astype(F32)
    grad_second = normalize_back(incoming, scaled_two, inverse_two, vectors[GAIN_TWO])
    grad[...] = grad_second
    low[...] = grad_second.astype(BF16)
    add_sums(sums, incoming * scaled_two, incoming, grad_second.astype(BF16).astype(F32))


def second_norm(scaled, own, far, grad_rows, vectors, chunk):
    size, width = scaled.shape
    steps = size // ROW_BLOCK
    return row_call(
        second_norm_kernel,
        "second_norm",
        [row_block(width)]
        + [row_block(width, chunk * steps)] * 3
        + [resident(vectors.shape)],
        [
            (row_block(width), jax.ShapeDtypeStruct((size, width), BF16)),
            (row_block(width), jax.ShapeDtypeStruct((size, width), F32)),
            (row_block(width), jax.ShapeDtypeStruct((size, width), BF16)),
            (resident((8, width)), jax.ShapeDtypeStruct((8, width), F32)),
        ],
        (scaled, own, far, grad_rows, vectors),
        size,
        size * width * 40,
    )


def first_back_kernel(
    place, grad, own, far, scaled, inverse, weight, vectors, hidden, low, m0, m1, m2, m3, sums
):
    incoming = grad[...] + own[...] + far[...].astype(F32)
    grad_hidden = normalize_back(incoming, scaled[...], inverse[...], vectors[GAIN_ONE])
    hidden[...] = grad_hidden
    attended = grad_hidden.astype(BF16)
    low[...] = attended
    for step, out in enumerate((m0, m1, m2, m3)):
        out[...] = dot(attended, weight[place[0] ^ step], (1, 1)).astype(BF16).reshape(out.shape)
    add_sums(sums, incoming * scaled[...], incoming, attended.astype(F32))


def first_back(place, grad, own, far, scaled, inverse, weight, vectors, chunk, part):
    size, width = grad.shape
    steps = size // ROW_BLOCK
    lanes = weight.shape[1]
    return row_call(
        first_back_kernel,
        "first_back",
        [SCALAR, row_block(width)]
        + [row_block(width, chunk * steps)] * 2
        + [row_block(width), row_block(1), resident(weight.shape), resident(vectors.shape)],
        [
            (row_block(width), jax.ShapeDtypeStruct((size, width), F32)),
            (row_block(width), jax.ShapeDtypeStruct((size, width), BF16)),
        ]
        + [
            (
                by_row((ROW_BLOCK // part, part, lanes)),
                jax.ShapeDtypeStruct((size // part, part, lanes), BF16),
            )
        ]
        * 4
        + [(resident((8, width)), jax.ShapeDtypeStruct((8, width), F32))],
        (place, grad, own, far, scaled, inverse, weight, vectors),
        size,
        2 * size * width * width,
    )


def output_grad_kernel(place, *refs):
    mixed, grads, out = refs[:CHUNKS], refs[CHUNKS:-1], refs[-1]
    lanes = out.shape[1]
    for step in range(out.shape[0]):
        at = slice(step * lanes, (step + 1) * lanes)
        out[place[0] ^ step] = sum(
            dot(m[:, at], g[...], (0, 0)) for m, g in zip(mixed, grads)
        ).astype(BF16)


def output_back(place, mixed, grads, ctx_size):
    size, width = mixed[0].shape
    shape = (ctx_size, width // ctx_size, width)
    return pl.pallas_call(
        output_grad_kernel,
        grid=(1,),
        in_specs=[SCALAR] + [resident((size, width))] * (2 * CHUNKS),
        out_specs=resident(shape),
        out_shape=jax.ShapeDtypeStruct(shape, BF16),
        compiler_params=pltpu.CompilerParams(vmem_limit_bytes=48 * MIB),
        cost_estimate=pl.CostEstimate(
            flops=2 * CHUNKS * size * width * width,
            bytes_accessed=4 * width * (width + CHUNKS * size),
            transcendentals=0,
        ),
        name="output_backward",
    )(place, *mixed, *grads)


def on_device(
    sizes,
    tokens,
    segment_ids,
    project_weight,
    query_bias,
    value_bias,
    output_weight,
    output_bias,
    first_gain,
    first_shift,
    expand_weight,
    expand_bias,
    reduce_weight,
    reduce_bias,
    second_gain,
    second_shift,
    grad_out,
):
    chips = sizes["z"] * sizes["y"] * sizes["x"]
    ctx_size = sizes["x"] * sizes["c"]
    everyone = chips * sizes["c"]
    seq_count, part, width = tokens.shape
    rows_count = seq_count * part
    hidden = expand_weight.shape[1]
    share = width // everyone
    own_hidden = hidden // 2
    lanes = width // ctx_size
    place = lax.axis_index(CTX)
    core = lax.axis_index("c")
    low_core = core == 0

    def hop(array, step):
        return lax.ppermute(array, CTX, [(i, i ^ step) for i in range(ctx_size)])

    def swap(array):
        return lax.ppermute(array, "c", [(0, 1), (1, 0)])

    def chosen(array, index, axis):
        return lax.dynamic_index_in_dim(array, index, axis, keepdims=False)

    def pair(own, other, axis, low):
        return jnp.where(
            low, jnp.stack([own, other], axis=axis), jnp.stack([other, own], axis=axis)
        )

    def by_core(own, other, axis):
        return pair(own, other, axis, low_core)

    def bit_of(name, step):
        return (lax.axis_index(name) // step) % 2

    def trade(array, name, step=1):
        return lax.ppermute(array, name, [(i, i ^ step) for i in range(sizes[name])])

    def widen(array, name, axis=0, step=1):
        return pair(array, trade(array, name, step), axis, bit_of(name, step) == 0)

    def halve(array, axis, name, step=1):
        me = bit_of(name, step)
        return chosen(array, me, axis).astype(F32) + trade(
            chosen(array, 1 - me, axis), name, step
        ).astype(F32)

    z_steps = [1 << i for i in range(sizes["z"].bit_length() - 1)]

    def z_gather(array):
        for index, step in enumerate(z_steps[::-1]):
            array = widen(array, "z", index, step)
        return array

    def z_scatter(blocks, kind=BF16):
        for step in z_steps:
            blocks = blocks.reshape((blocks.shape[0] // 2, 2) + blocks.shape[1:])
            blocks = halve(blocks.astype(kind), 1, "z", step)
        return blocks[0]

    seg_parts = segment_ids.reshape(seq_count, ctx_size, part)
    seg = jnp.concatenate([chosen(seg_parts, place ^ r, 1) for r in range(ctx_size)], axis=1)
    seg_key = seg[:, :, None]
    seg_query = seg[:, None, :]

    vectors = (
        query_bias,
        value_bias,
        output_bias,
        first_gain,
        first_shift,
        reduce_bias,
        second_gain,
        second_shift,
        expand_bias,
    )
    vector_count = 8 * share + expand_bias.shape[0]
    filler = jnp.pad(jnp.stack(vectors[:8]), ((0, 8), (0, 3 * lanes - share))) + jnp.pad(
        expand_bias[None], ((8, 7), (0, 3 * lanes - expand_bias.shape[0]))
    )
    held = jnp.stack(
        [
            jnp.concatenate(
                [
                    jnp.concatenate(
                        [
                            project_weight[:, (ctx_size * j + p) * lanes :][:, :lanes]
                            for j in range(3)
                        ],
                        axis=1,
                    ),
                    filler,
                ]
            )
            for p in range(ctx_size)
        ]
    )
    held = lax.all_to_all(held, CTX, 0, 0, tiled=True)
    sent, held = lax.optimization_barrier((tokens, held))
    across = hop(sent, 2)
    gathered = (tokens, swap(sent), across, swap(across))
    mine = jnp.concatenate(
        [held[:, :share, j * lanes : (j + 1) * lanes].reshape(-1, lanes) for j in range(3)]
    )
    vector_rows = held[:, share:, :lanes].reshape(-1, lanes)
    out_pieces = jnp.concatenate(
        [output_weight[:, i * lanes : (i + 1) * lanes] for i in range(ctx_size)]
    )
    full_project = lax.all_gather(
        jnp.concatenate([widen(out_pieces, "x").reshape(-1, lanes), mine, vector_rows]),
        SEQ,
        axis=0,
    )
    packed = full_project[:, -16 * ctx_size :].reshape(everyone, 16, lanes).astype(F32)
    exp_bias = chosen(
        packed[:, 8, : expand_bias.shape[0]].reshape(chips, 2, -1), core, 1
    ).reshape(1, own_hidden)
    vectors = jnp.swapaxes(packed[:, :8, :share], 0, 1).reshape(8, width)
    full_query, full_value = vectors[0], vectors[1]
    bias_all = jnp.concatenate(
        [
            lax.dynamic_slice_in_dim(full_query, place * lanes, lanes),
            jnp.zeros((lanes,), F32),
            lax.dynamic_slice_in_dim(full_value, place * lanes, lanes),
        ]
    )[None]

    columns = expand_weight.reshape(share, chips, 2, own_hidden // chips)
    own_columns = chosen(columns, core, 2).reshape(share, own_hidden)
    far_columns = chosen(columns, 1 - core, 2).reshape(share, own_hidden)
    both = by_core(own_columns, swap(far_columns), 0)

    def in_pieces(array):
        rows_of, wide = array.shape
        return jnp.swapaxes(array.reshape(rows_of, wide // PIECE, PIECE), 0, 1).reshape(
            -1, 2 * share, PIECE
        )

    own_pieces = jnp.concatenate(
        [
            in_pieces(both.reshape(2 * share, own_hidden)),
            jnp.swapaxes(
                reduce_weight.reshape(2, 2 * share, width // PIECE, PIECE), 1, 2
            ).reshape(-1, 2 * share, PIECE),
        ]
    )
    own_pieces = hold(own_pieces, [across])
    weights = lax.all_gather(widen(own_pieces, "x"), SEQ, axis=0).reshape(
        chips, -1, 2 * share, PIECE
    )

    rows = tokens.reshape(rows_count, width)
    where = place.reshape(1).astype(jnp.int32)
    seqs = seq_count // CHUNKS
    saved, kept_rows, mixed_low, first_low, scaled_one, inverse_one = [], [], [], [], [], []
    for index in range(CHUNKS):
        at = slice(index * seqs, (index + 1) * seqs)
        *mixed, all_rows, kept = attend(
            gathered, full_project, bias_all, seg_key[at], seg_query[at], at.start, []
        )
        kept_rows.append(all_rows)
        saved.append(kept)
        if index == 0:
            out_half = unpack(full_project, share, width, mixed[:1])
            full_output = by_core(out_half, swap(out_half), 1).reshape(ctx_size, lanes, width)
        arrived = [mixed[0]] + [hop(mixed[r], r) for r in (1, 2, 3)]
        low, scaled, inverse, joined = first_norm(
            where, arrived, rows, full_output, vectors, index
        )
        mixed_low.append(joined)
        first_low.append(low)
        scaled_one.append(scaled)
        inverse_one.append(inverse)
    first_far = [swap(low) for low in first_low]
    act, slope, own_sum, far_sum = feed(first_low, first_far, weights, exp_bias)
    far_sum = swap(far_sum)

    grad_rows = grad_out.reshape(rows_count, width)
    layer_parts, grad_second, grad_reduced, second_sums = zip(
        *(
            second_norm(scaled_one[index], own_sum, far_sum, grad_rows, vectors, index)
            for index in range(CHUNKS)
        )
    )
    layer_work = jnp.concatenate(layer_parts, axis=0).reshape(tokens.shape)
    weight_grad, expand_bias_grad, own_back, far_back = feed_back(
        grad_reduced + tuple(swap(grad) for grad in grad_reduced),
        first_low + first_far,
        act,
        slope,
        weights,
    )
    weight_owned = lax.psum_scatter(
        weight_grad.reshape((-1, sizes["x"]) + weight_grad.shape[1:]),
        SEQ,
        scatter_dimension=0,
        tiled=True,
    )[0]
    far_back = swap(far_back)
    grad_hidden, grad_attended, grad_mixed, first_sums = [], [], [], []
    for index in range(CHUNKS):
        grad, low, *mixed, sums = first_back(
            where,
            grad_second[index],
            own_back,
            far_back,
            scaled_one[index],
            inverse_one[index],
            full_output,
            vectors,
            index,
            part,
        )
        grad_hidden.append(grad.reshape(seqs, part, width))
        grad_attended.append(low)
        grad_mixed.append([mixed[0]] + [hop(mixed[r], r) for r in (1, 2, 3)])
        first_sums.append(sums)
    output_grad = output_back(where, mixed_low, grad_attended, ctx_size).reshape(
        sizes["z"], 2, sizes["x"], 2, share, width
    )
    project_grad = []
    work_parts = []
    across_sums = []
    work_hops = []
    sum_parts = []
    for index in range(CHUNKS):
        at = slice(index * seqs, (index + 1) * seqs)
        project_part, r0, r1, r2, r3, sums = attend_back(
            saved[index],
            kept_rows[index],
            grad_mixed[index],
            full_project,
            seg_key[at],
            seg_query[at],
            project_grad,
            index == CHUNKS - 1,
            across_sums[:1] if index else grad_attended[1:],
        )
        project_grad = [project_part]
        across_sums.append((r2.astype(F32) + swap(r3).astype(F32)).astype(BF16))
        work_hops.append(hop(across_sums[index], 2))
        work_parts.append(
            grad_hidden[index] + r0 + swap(r1).astype(F32) + work_hops[index].astype(F32)
        )
        sum_parts.append(sums)
    grad_work = jnp.concatenate(work_parts, axis=0)
    project_grad = [hold(project_grad[0], work_hops[:1])]
    blocks = halve(
        project_grad[0].reshape(sizes["z"], 2, ctx_size * share, 3 * lanes), 1, "y"
    ).astype(BF16)
    later = [blocks, work_hops[1]]
    for step in z_steps:
        blocks = blocks.astype(BF16).reshape((blocks.shape[0] // 2, 2) + blocks.shape[1:])
        blocks = halve(blocks, 1, "z", step)
        if step == 1:
            weight_owned = halve(weight_owned, 0, "x")
            blocks = hold(blocks.astype(BF16), [weight_owned])
    held = lax.all_to_all(
        blocks.astype(F32).reshape(ctx_size, share, 3 * lanes),
        CTX,
        0,
        0,
        tiled=True,
    )
    project_owned = jnp.concatenate(
        [
            held[p, :, j * lanes : (j + 1) * lanes]
            for j in range(3)
            for p in range(ctx_size)
        ],
        axis=1,
    )
    expand_pieces = own_hidden // PIECE
    far_rows = jnp.swapaxes(
        weight_owned[:expand_pieces].reshape(expand_pieces, 2, share, PIECE), 0, 1
    )
    expand_owned = by_core(
        jnp.swapaxes(chosen(far_rows, core, 0), 0, 1).reshape(share, chips, -1),
        jnp.swapaxes(swap(chosen(far_rows, 1 - core, 0)), 0, 1).reshape(share, chips, -1),
        2,
    ).reshape(share, hidden)
    reduce_owned = jnp.swapaxes(
        weight_owned[expand_pieces:].reshape(2, width // PIECE, 2 * share, PIECE), 1, 2
    ).reshape(4 * share, width)

    column_sums = jnp.sum(jnp.concatenate(sum_parts, axis=0), axis=(0, 1))
    zeros = jnp.zeros((width,), F32)
    first_sums, second_sums = sum(first_sums), sum(second_sums)
    grad_vectors = (
        lax.dynamic_update_slice_in_dim(zeros, column_sums[:lanes], place * lanes, 0),
        lax.dynamic_update_slice_in_dim(zeros, column_sums[2 * lanes :], place * lanes, 0),
        first_sums[2],
        first_sums[0],
        first_sums[1],
        second_sums[2],
        second_sums[0],
        second_sums[1],
    )
    hidden_sums = expand_bias_grad.reshape(chips, 1, own_hidden // chips)
    hidden_sums = jnp.where(
        low_core,
        jnp.concatenate([hidden_sums, jnp.zeros_like(hidden_sums)], axis=1),
        jnp.concatenate([jnp.zeros_like(hidden_sums), hidden_sums], axis=1),
    )
    packed_grads = jnp.concatenate(
        [vector.reshape(everyone, share) for vector in grad_vectors]
        + [hidden_sums.reshape(everyone, -1)],
        axis=1,
    )
    packed_grads = jnp.pad(packed_grads, ((0, 0), (0, width - vector_count))).astype(BF16)
    shared = jnp.concatenate(
        [
            output_grad.reshape(everyone, share, width),
            hold(packed_grads, later)[:, None],
        ],
        axis=1,
    ).reshape(sizes["z"], 2, sizes["x"], 2, share + 1, width)
    for axis, name in ((3, "c"), (2, "x"), (1, "y")):
        shared = halve(shared, axis, name).astype(BF16)
    shared = z_scatter(shared)
    output_owned = shared[:share]
    owned = shared[share, :vector_count]
    small = [owned[i * share : (i + 1) * share] for i in range(8)]
    return (
        layer_work,
        grad_work,
        project_owned.astype(F32),
        small[0],
        small[1],
        output_owned.astype(F32),
        small[2],
        small[3],
        small[4],
        expand_owned.astype(F32),
        owned[8 * share :],
        reduce_owned.astype(F32),
        small[5],
        small[6],
        small[7],
    )


def solution(mesh):
    seq_size, ctx_size = mesh.shape["seq"], mesh.shape["ctx"]
    sizes = {"z": seq_size // 2, "y": 2, "x": ctx_size // 2, "c": 2}
    fine = Mesh(mesh.devices.reshape(tuple(sizes.values())), tuple(sizes))
    rows = P(SEQ, CTX, None)
    matrix = P(ALL, None)
    vector = P(ALL)
    return jax.shard_map(
        functools.partial(on_device, sizes),
        mesh=fine,
        in_specs=(
            rows,
            P(SEQ, None),
            matrix,
            vector,
            vector,
            matrix,
            vector,
            vector,
            vector,
            matrix,
            vector,
            matrix,
            vector,
            vector,
            vector,
            rows,
        ),
        out_specs=(
            rows,
            rows,
            matrix,
            vector,
            vector,
            matrix,
            vector,
            vector,
            vector,
            matrix,
            vector,
            matrix,
            vector,
            vector,
            vector,
        ),
        check_vma=False,
    )
```

```python
import functools

import jax
import jax.numpy as jnp
from jax import lax
from jax.experimental import pallas as pl
from jax.experimental.pallas import tpu as pltpu
from jax.sharding import Mesh
from jax.sharding import PartitionSpec as P

HEADS = 16
HEAD_DIM = 64
CHUNKS = 2
PIECE = 256
MIB = 1 << 20
CHIPS = ("z", "y", "x")
SEQ = ("z", "y")
CTX = ("x", "c")
ALL = ("z", "y", "x", "c")
F32 = jnp.float32
BF16 = jnp.bfloat16
ELSEWHERE = pl.BlockSpec(memory_space=pl.ANY)


def dot(left, right, contract=(1, 0)):
    return lax.dot_general(
        left, right, (((contract[0],), (contract[1],)), ((), ())), preferred_element_type=F32
    )


def resident(shape):
    return pl.BlockSpec(shape, lambda i: (0,) * len(shape), pipeline_mode=pl.Buffered(1))


def by_row(shape):
    return pl.BlockSpec(shape, lambda i: (i,) + (0,) * (len(shape) - 1))


def flat(block):
    wide = block.shape[-1]
    if block.shape[-2] % 16:
        return block.astype(F32).reshape(-1, wide).astype(BF16)
    return block.reshape(-1, wide)


def hold_kernel(source, *refs):
    refs[-1][...] = source[...]


def hold(array, after):
    return pl.pallas_call(
        hold_kernel,
        grid=(1,),
        in_specs=[resident(array.shape)] + [ELSEWHERE] * len(after),
        out_specs=resident(array.shape),
        out_shape=jax.ShapeDtypeStruct(array.shape, array.dtype),
        compiler_params=pltpu.CompilerParams(vmem_limit_bytes=16 * MIB),
        name="hold",
    )(array, *after)


def add_kernel(left, right, *refs):
    refs[-1][...] = (left[...].astype(F32) + right[...].astype(F32)).astype(BF16)


def add_low(left, right, after):
    block = (1,) + left.shape[1:]
    return pl.pallas_call(
        add_kernel,
        grid=(left.shape[0],),
        in_specs=[by_row(block)] * 2 + [ELSEWHERE] * len(after),
        out_specs=by_row(block),
        out_shape=jax.ShapeDtypeStruct(left.shape, BF16),
        compiler_params=pltpu.CompilerParams(vmem_limit_bytes=16 * MIB),
        name="add_low",
    )(left, right, *after)


def join_kernel(top, below, *refs):
    out = refs[-1]
    out[:, : top.shape[1]] = top[...]
    out[:, top.shape[1] :] = below[...]


def join(top, below, after):
    shape = (top.shape[0], top.shape[1] + below.shape[1], top.shape[2])
    return pl.pallas_call(
        join_kernel,
        grid=(1,),
        in_specs=[resident(top.shape), resident(below.shape)] + [ELSEWHERE] * len(after),
        out_specs=resident(shape),
        out_shape=jax.ShapeDtypeStruct(shape, BF16),
        compiler_params=pltpu.CompilerParams(vmem_limit_bytes=32 * MIB),
        name="join",
    )(top, below, *after)


def unpack_kernel(pieces, *refs):
    out = refs[-1]
    height, lanes = out.shape[2], pieces.shape[2]
    for half in range(2):
        for i in range(out.shape[3] // lanes):
            start = (half * (out.shape[3] // lanes) + i) * height
            out[:, half, :, i * lanes : (i + 1) * lanes] = pieces[:, start : start + height]


def unpack(gathered, share, width, after):
    count, _, lanes = gathered.shape
    columns = width // lanes
    if share % 16:
        pieces = gathered[:, : 2 * columns * share].reshape(count, 2, columns, share, lanes)
        return jnp.swapaxes(pieces, 2, 3).reshape(2 * count, share, width)
    return pl.pallas_call(
        unpack_kernel,
        grid=(1,),
        in_specs=[pl.BlockSpec((count, 2 * columns * share, lanes), lambda i: (0, 0, 0))]
        + [ELSEWHERE] * len(after),
        out_specs=pl.BlockSpec((count, 2, share, width), lambda i: (0, 0, 0, 0)),
        out_shape=jax.ShapeDtypeStruct((count, 2, share, width), BF16),
        compiler_params=pltpu.CompilerParams(vmem_limit_bytes=16 * MIB),
        name="unpack",
    )(gathered, *after).reshape(2 * count, share, width)


def softmax_down(scores, allowed):
    scores = jnp.where(allowed, scores, -1e30)
    top = jnp.max(scores, axis=0, keepdims=True)
    expo = jnp.exp(scores - top)
    total = jnp.sum(expo, axis=0, keepdims=True)
    return expo * (1.0 / total)


def head_lanes(width, head):
    lane = lax.broadcasted_iota(jnp.int32, (1, width), 1)
    return (lane // HEAD_DIM == head).astype(F32)


def attend_kernel(late, t0, t1, t2, t3, wq, wk, wv, bias, seg_key, seg_query, *refs):
    m0, m1, m2, m3, kept, saved = refs[late:]
    part = t0.shape[1]
    rows = jnp.concatenate([t[0] for t in (t0, t1, t2, t3)], axis=0)
    kept[0] = rows
    width = wq.shape[2]
    queries, keys, values = [
        dot(rows, flat(w[...])) + bias[:, i * width : (i + 1) * width]
        for i, w in enumerate((wq, wk, wv))
    ]
    for i, part_of in enumerate((queries, keys, values)):
        saved[0, :, i * width : (i + 1) * width] = part_of.astype(BF16)
    queries = (queries.astype(BF16).astype(F32) * HEAD_DIM**-0.5).astype(BF16)
    keys = keys.astype(BF16).astype(F32)
    values_t = jnp.transpose(values).astype(BF16)
    allowed = seg_key[0] == seg_query[0]
    mixed = []
    for head in range(width // HEAD_DIM):
        own_keys = (keys * head_lanes(width, head)).astype(BF16)
        chances = softmax_down(dot(own_keys, queries, (1, 1)), allowed)
        own_values = values_t[head * HEAD_DIM : (head + 1) * HEAD_DIM]
        mixed.append(dot(own_values, chances.astype(BF16)))
    mixed = jnp.transpose(jnp.concatenate(mixed, axis=0)).astype(BF16)
    for index, out in enumerate((m0, m1, m2, m3)):
        out[0] = mixed[index * part : (index + 1) * part]


def project_specs(weight, depth):
    shape = (weight.shape[0], depth // weight.shape[0], weight.shape[2])
    return [
        pl.BlockSpec(shape, lambda i, j=j: (0, j + 2, 0), pipeline_mode=pl.Buffered(1))
        for j in range(3)
    ]


def attend(tokens, weight, bias, seg_key, seg_query, first, after):
    count, part, depth = tokens[0].shape
    count = count // CHUNKS
    wide = bias.shape[1]
    length = 4 * part
    return pl.pallas_call(
        functools.partial(attend_kernel, len(after)),
        grid=(count,),
        in_specs=[pl.BlockSpec((1, part, depth), lambda i: (i + first, 0, 0))] * 4
        + project_specs(weight, depth)
        + [
            resident((1, wide)),
            by_row((1, length, 1)),
            by_row((1, 1, length)),
        ]
        + [ELSEWHERE] * len(after),
        out_specs=[by_row((1, part, wide // 3))] * 4
        + [by_row((1, length, depth)), by_row((1, length, wide))],
        out_shape=[jax.ShapeDtypeStruct((count, part, wide // 3), BF16)] * 4
        + [
            jax.ShapeDtypeStruct((count, length, depth), BF16),
            jax.ShapeDtypeStruct((count, length, wide), BF16),
        ],
        compiler_params=pltpu.CompilerParams(vmem_limit_bytes=40 * MIB),
        cost_estimate=pl.CostEstimate(
            flops=count * length * wide * (2 * depth + 16 * length // 3),
            bytes_accessed=count * length * (depth + 2 * wide) * 2,
            transcendentals=count * length * length * wide // (3 * HEAD_DIM),
        ),
        name="attend_forward",
    )(*tokens, weight, weight, weight, bias, seg_key, seg_query, *after)


def attend_back_kernel(
    late, earlier, saved, kept, g0, g1, g2, g3, wq, wk, wv, seg_key, seg_query, *refs
):
    grad_weight, r0, r1, r2, r3, sums, total = refs[late + earlier :]

    @pl.when(pl.program_id(0) == 0)
    def _():
        total[...] = refs[0][...] if earlier else jnp.zeros_like(total)

    part = g0.shape[1]
    width = saved.shape[2] // 3
    factor = HEAD_DIM**-0.5
    queries = (saved[0, :, :width].astype(F32) * factor).astype(BF16)
    keys = saved[0, :, width : 2 * width].astype(F32)
    values = saved[0, :, 2 * width :].astype(F32)
    keys_t = jnp.transpose(keys * factor).astype(BF16)
    grad_mixed = jnp.concatenate([g[0] for g in (g0, g1, g2, g3)], axis=0)
    allowed = seg_key[0] == seg_query[0]
    grad_queries = []
    grad_keys = None
    grad_values = None
    for head in range(width // HEAD_DIM):
        lanes = head_lanes(width, head)
        chances = softmax_down(
            dot((keys * lanes).astype(BF16), queries, (1, 1)), allowed
        )
        grad_weights = dot((values * lanes).astype(BF16), grad_mixed, (1, 1))
        inner = jnp.sum(chances * grad_weights, axis=0, keepdims=True)
        grad_scores = (chances * (grad_weights - inner)).astype(BF16)
        grad_queries.append(dot(keys_t[head * HEAD_DIM : (head + 1) * HEAD_DIM], grad_scores))
        keys_term = dot(grad_scores, queries)
        values_term = dot(chances.astype(BF16), grad_mixed)
        if head == 0:
            grad_keys, grad_values = keys_term, values_term
        else:
            here = lanes > 0.5
            grad_keys = jnp.where(here, keys_term, grad_keys)
            grad_values = jnp.where(here, values_term, grad_values)
    grad_queries = jnp.concatenate(grad_queries, axis=0)
    terms = [
        jnp.transpose(grad_queries).astype(BF16),
        grad_keys.astype(BF16),
        grad_values.astype(BF16),
    ]
    total[:width] += dot(grad_queries.astype(BF16), kept[0])
    for i, term in enumerate(terms):
        sums[0, :, i * width : (i + 1) * width] = jnp.sum(
            term.astype(F32), axis=0, keepdims=True
        )
        if i:
            total[i * width : (i + 1) * width] += dot(term, kept[0], (0, 0))
    rows = sum(dot(term, flat(w[...]), (1, 1)) for term, w in zip(terms, (wq, wk, wv)))
    for index, out in enumerate((r0, r1, r2, r3)):
        out[0] = rows[index * part : (index + 1) * part].astype(out.dtype)

    @pl.when(pl.program_id(0) == pl.num_programs(0) - 1)
    def _():
        if grad_weight.dtype == BF16:
            grad_weight[...] = jnp.transpose(total[...]).astype(BF16)
        else:
            grad_weight[...] = total[...]


def attend_back(saved, kept, grads, weight, seg_key, seg_query, earlier, done, after):
    count, part, width = grads[0].shape
    depth, wide = width * 4, width * 3
    length = 4 * part
    shape, kind = ((depth, wide), BF16) if done else ((wide, depth), F32)
    return pl.pallas_call(
        functools.partial(attend_back_kernel, len(after), len(earlier)),
        grid=(count,),
        in_specs=[by_row((1, length, wide)), by_row((1, length, depth))]
        + [by_row((1, part, width))] * 4
        + project_specs(weight, depth)
        + [
            by_row((1, length, 1)),
            by_row((1, 1, length)),
        ]
        + [resident((wide, depth))] * len(earlier)
        + [ELSEWHERE] * len(after),
        out_specs=[resident(shape)]
        + [by_row((1, part, depth))] * 4
        + [by_row((1, 1, wide))],
        out_shape=[jax.ShapeDtypeStruct(shape, kind)]
        + [jax.ShapeDtypeStruct((count, part, depth), t) for t in (F32, BF16, BF16, BF16)]
        + [jax.ShapeDtypeStruct((count, 1, wide), F32)],
        scratch_shapes=[pltpu.VMEM((wide, depth), F32)],
        compiler_params=pltpu.CompilerParams(vmem_limit_bytes=52 * MIB),
        cost_estimate=pl.CostEstimate(
            flops=count * length * wide * (4 * depth + 40 * length // 3),
            bytes_accessed=count * length * (3 * depth + 3 * wide) * 2,
            transcendentals=count * length * length * wide // (3 * HEAD_DIM),
        ),
        name="attend_backward",
    )(saved, kept, *grads, weight, weight, weight, seg_key, seg_query, *earlier, *after)


def column(shape):
    return pl.BlockSpec(shape, lambda i: (0, i))


def expand_piece(ref):
    return jnp.concatenate([flat(ref[:, i]) for i in range(ref.shape[1])], axis=1)


def reduce_piece(ref):
    columns = ref.shape[1] // 2
    halves = [
        jnp.concatenate([ref[:, half * columns + i] for i in range(columns)], axis=2)
        for half in range(2)
    ]
    return flat(jnp.concatenate(halves, axis=1))


def feed_kernel(*refs):
    sources, (expand, bias, reduce, act, slope, own_out, other_out, far_sum) = (
        refs[: 2 * CHUNKS],
        refs[2 * CHUNKS :],
    )
    step = pl.program_id(0)

    @pl.when(step == 0)
    def _():
        own_out[...] = jnp.zeros_like(own_out)
        far_sum[...] = jnp.zeros_like(far_sum)

    into = expand_piece(expand)
    back = reduce_piece(reduce)
    block = 256
    per = sources[0].shape[0] // block
    half_count = CHUNKS * per

    def inner(index):
        start = index % per * block
        return dot(sources[index // per][start : start + block], into) + bias[...]

    ahead = inner(0)
    for index in range(2 * half_count):
        inside = ahead
        if index + 1 < 2 * half_count:
            ahead = inner(index + 1)
        total = own_out if index < half_count else far_sum
        at = slice(index % half_count * block, (index % half_count + 1) * block)
        to = slice(index * block, (index + 1) * block)
        square = inside * inside
        curve = jnp.tanh(inside * (0.7978845608028654 + 0.7978845608028654 * 0.044715 * square))
        half = 0.5 * curve + 0.5
        active = (inside * half).astype(BF16)
        act[to] = active
        tilt = 0.7978845608028654 * 0.5 + 0.7978845608028654 * 1.5 * 0.044715 * square
        slope[to] = (half + inside * (1.0 - curve * curve) * tilt).astype(BF16)
        total[at] += dot(active, back)

    @pl.when(step == pl.num_programs(0) - 1)
    def _():
        other_out[...] = far_sum[...].astype(BF16)


def feed_weights(weights, pieces, columns):
    chips, _, rows, _ = weights.shape
    return [
        pl.BlockSpec((chips, pieces, rows, PIECE), lambda i: (0, i, 0, 0)),
        pl.BlockSpec(
            (pieces * PIECE // (2 * rows), 2 * columns, rows, PIECE), lambda i: (i, 1, 0, 0)
        ),
    ]


def feed(own, other, weights, bias):
    block, depth = own[0].shape
    rows = CHUNKS * block
    hidden = bias.shape[1]
    pieces = 2
    wide = pieces * PIECE
    expand_spec, reduce_spec = feed_weights(weights, pieces, depth // PIECE)
    return pl.pallas_call(
        feed_kernel,
        grid=(hidden // wide,),
        in_specs=[resident((block, depth))] * (2 * CHUNKS)
        + [expand_spec, column((1, wide)), reduce_spec],
        out_specs=[column((2 * rows, wide))] * 2 + [resident((rows, depth))] * 2,
        out_shape=[jax.ShapeDtypeStruct((2 * rows, hidden), BF16)] * 2
        + [
            jax.ShapeDtypeStruct((rows, depth), F32),
            jax.ShapeDtypeStruct((rows, depth), BF16),
        ],
        scratch_shapes=[pltpu.VMEM((rows, depth), F32)],
        compiler_params=pltpu.CompilerParams(vmem_limit_bytes=56 * MIB),
        cost_estimate=pl.CostEstimate(
            flops=8 * rows * depth * hidden,
            bytes_accessed=4 * rows * (2 * hidden + 3 * depth),
            transcendentals=2 * rows * hidden,
        ),
        name="feed_forward",
    )(*own, *other, weights, bias, weights)


def feed_back_kernel(*refs):
    grads, sources = refs[: 2 * CHUNKS], refs[2 * CHUNKS : 4 * CHUNKS]
    act, slope, expand, reduce, weight_grad, bias_grad, own_out, other_out, far_sum, inside = refs[
        4 * CHUNKS :
    ]
    step = pl.program_id(0)
    block = grads[0].shape[0]

    @pl.when(step == 0)
    def _():
        own_out[...] = jnp.zeros_like(own_out)
        far_sum[...] = jnp.zeros_like(far_sum)

    into = expand_piece(expand)
    back = reduce_piece(reduce)
    bias_sum = jnp.zeros(bias_grad.shape, F32)
    for index in range(2 * CHUNKS):
        total = own_out if index < CHUNKS else far_sum
        at = slice(index % CHUNKS * block, (index % CHUNKS + 1) * block)
        to = slice(index * block, (index + 1) * block)
        grad_act = dot(grads[index][...], back, (1, 1))
        part = (grad_act * slope[to].astype(F32)).astype(BF16)
        inside[to] = part
        bias_sum += jnp.sum(part.astype(F32), axis=0, keepdims=True)
        total[at] += dot(part, into, (1, 1))
    bias_grad[...] = bias_sum
    chips, pieces, height, _ = weight_grad.shape
    columns = pieces // 4
    wide = inside.shape[1]
    reduce_grad = sum(
        dot(act[i * block : (i + 1) * block], grad[...], (0, 0)) for i, grad in enumerate(grads)
    )
    count = wide // (2 * height)
    reduce_grad = reduce_grad.reshape(count, 2 * height, reduce_grad.shape[1]).astype(BF16)
    mine = pl.ds(step * count, count)
    for half in range(2):
        for i in range(columns):
            weight_grad[mine, (2 + half) * columns + i] = reduce_grad[
                :, half * height : (half + 1) * height, i * PIECE : (i + 1) * PIECE
            ]
    flipped = sum(
        dot(inside[i * block : (i + 1) * block], source[...], (0, 0))
        for i, source in enumerate(sources)
    )
    expand_grad = jnp.transpose(flipped).reshape(chips, height, wide).astype(BF16)
    for i in range(wide // PIECE):
        weight_grad[:, step * (wide // PIECE) + i] = expand_grad[
            :, :, i * PIECE : (i + 1) * PIECE
        ]

    @pl.when(step == pl.num_programs(0) - 1)
    def _():
        other_out[...] = far_sum[...].astype(BF16)


def feed_back(grads, sources, act, slope, weights):
    block, depth = grads[0].shape
    rows = CHUNKS * block
    hidden = act.shape[1]
    chips, _, height, _ = weights.shape
    pieces = 2 * hidden // PIECE
    expand_spec, reduce_spec = feed_weights(weights, 2, depth // PIECE)
    wide = 2 * PIECE
    return pl.pallas_call(
        feed_back_kernel,
        grid=(hidden // wide,),
        in_specs=[resident((block, depth))] * (4 * CHUNKS)
        + [column((2 * rows, wide))] * 2
        + [expand_spec, reduce_spec],
        out_specs=[
            resident((chips, pieces, height, PIECE)),
            column((1, wide)),
        ]
        + [resident((rows, depth))] * 2,
        out_shape=[
            jax.ShapeDtypeStruct((chips, pieces, height, PIECE), BF16),
            jax.ShapeDtypeStruct((1, hidden), F32),
            jax.ShapeDtypeStruct((rows, depth), F32),
            jax.ShapeDtypeStruct((rows, depth), BF16),
        ],
        scratch_shapes=[
            pltpu.VMEM((rows, depth), F32),
            pltpu.VMEM((2 * rows, wide), BF16),
        ],
        compiler_params=pltpu.CompilerParams(vmem_limit_bytes=56 * MIB),
        cost_estimate=pl.CostEstimate(
            flops=16 * rows * depth * hidden,
            bytes_accessed=4 * rows * (2 * hidden + 5 * depth) + 8 * depth * hidden,
            transcendentals=0,
        ),
        name="feed_backward",
    )(*grads, *sources, act, slope, weights, weights)


def normalize(values):
    center = values - jnp.mean(values, axis=-1, keepdims=True)
    inverse = lax.rsqrt(jnp.mean(center * center, axis=-1, keepdims=True) + 1e-05)
    return (center * inverse, inverse)


def normalize_back(incoming, scaled, inverse, gain):
    grad_scaled = incoming * gain
    mean_one = jnp.mean(grad_scaled, axis=-1, keepdims=True)
    mean_two = jnp.mean(grad_scaled * scaled, axis=-1, keepdims=True)
    return inverse * (grad_scaled - mean_one - scaled * mean_two)


def add_sums(out, *rows):
    rows = [jnp.sum(row, axis=0, keepdims=True) for row in rows]
    rows.append(jnp.zeros((out.shape[0] - len(rows), out.shape[1]), F32))
    rows = jnp.concatenate(rows, axis=0)

    @pl.when(pl.program_id(0) == 0)
    def _():
        out[...] = rows

    @pl.when(pl.program_id(0) > 0)
    def _():
        out[...] += rows


OUT_BIAS, GAIN_ONE, SHIFT_ONE, RED_BIAS, GAIN_TWO, SHIFT_TWO = (slice(i, i + 1) for i in range(2, 8))
SCALAR = pl.BlockSpec(memory_space=pltpu.SMEM)
ROW_BLOCK = 256


def row_call(kernel, name, ins, outs, arrays, rows, cost):
    return pl.pallas_call(
        kernel,
        grid=(rows // ROW_BLOCK,),
        in_specs=ins,
        out_specs=[spec for spec, _ in outs],
        out_shape=[shape for _, shape in outs],
        compiler_params=pltpu.CompilerParams(vmem_limit_bytes=48 * MIB),
        cost_estimate=pl.CostEstimate(flops=cost, bytes_accessed=rows << 14, transcendentals=rows),
        name=name,
    )(*arrays)


def row_block(width, first=0):
    return pl.BlockSpec((ROW_BLOCK, width), lambda i: (i + first, 0))


def first_norm_kernel(place, m0, m1, m2, m3, tokens, weight, vectors, low, scaled, inverse, mixed):
    total = tokens[...].astype(F32) + vectors[OUT_BIAS]
    parts = [m[...].reshape(ROW_BLOCK, -1) for m in (m0, m1, m2, m3)]
    mixed[...] = jnp.concatenate(parts, axis=1)
    for step, part in enumerate(parts):
        total += dot(part, weight[place[0] ^ step])
    scaled_one, inverse_one = normalize(total)
    scaled[...] = scaled_one
    inverse[...] = inverse_one
    low[...] = (scaled_one * vectors[GAIN_ONE] + vectors[SHIFT_ONE]).astype(BF16)


def first_norm(place, mixed, rows, weight, vectors, chunk):
    width = rows.shape[1]
    count, part, lanes = mixed[0].shape
    size = count * part
    steps = size // ROW_BLOCK
    return row_call(
        first_norm_kernel,
        "first_norm",
        [SCALAR]
        + [by_row((ROW_BLOCK // part, part, lanes))] * 4
        + [row_block(width, chunk * steps), resident(weight.shape), resident(vectors.shape)],
        [
            (row_block(width), jax.ShapeDtypeStruct((size, width), BF16)),
            (row_block(width), jax.ShapeDtypeStruct((size, width), F32)),
            (row_block(1), jax.ShapeDtypeStruct((size, 1), F32)),
            (row_block(width), jax.ShapeDtypeStruct((size, width), BF16)),
        ],
        (place, *mixed, rows, weight, vectors),
        size,
        2 * size * width * width,
    )


def second_norm_kernel(scaled, own, far, grad_out, vectors, layer, grad, low, sums):
    first = scaled[...] * vectors[GAIN_ONE] + vectors[SHIFT_ONE]
    reduced = own[...] + far[...].astype(F32) + vectors[RED_BIAS]
    scaled_two, inverse_two = normalize(first + reduced)
    layer[...] = (scaled_two * vectors[GAIN_TWO] + vectors[SHIFT_TWO]).astype(BF16)
    incoming = grad_out[...].astype(F32)
    grad_second = normalize_back(incoming, scaled_two, inverse_two, vectors[GAIN_TWO])
    grad[...] = grad_second
    low[...] = grad_second.astype(BF16)
    add_sums(sums, incoming * scaled_two, incoming, grad_second.astype(BF16).astype(F32))


def second_norm(scaled, own, far, grad_rows, vectors, chunk):
    size, width = scaled.shape
    steps = size // ROW_BLOCK
    return row_call(
        second_norm_kernel,
        "second_norm",
        [row_block(width)]
        + [row_block(width, chunk * steps)] * 3
        + [resident(vectors.shape)],
        [
            (row_block(width), jax.ShapeDtypeStruct((size, width), BF16)),
            (row_block(width), jax.ShapeDtypeStruct((size, width), F32)),
            (row_block(width), jax.ShapeDtypeStruct((size, width), BF16)),
            (resident((8, width)), jax.ShapeDtypeStruct((8, width), F32)),
        ],
        (scaled, own, far, grad_rows, vectors),
        size,
        size * width * 40,
    )


def first_back_kernel(
    late, place, grad, own, far, scaled, inverse, weight, vectors, *refs
):
    hidden, low, m0, m1, m2, m3, sums = refs[late:]
    incoming = grad[...] + own[...] + far[...].astype(F32)
    grad_hidden = normalize_back(incoming, scaled[...], inverse[...], vectors[GAIN_ONE])
    hidden[...] = grad_hidden
    attended = grad_hidden.astype(BF16)
    low[...] = attended
    for step, out in enumerate((m0, m1, m2, m3)):
        out[...] = dot(attended, weight[place[0] ^ step], (1, 1)).astype(BF16).reshape(out.shape)
    add_sums(sums, incoming * scaled[...], incoming, attended.astype(F32))


def first_back(place, grad, own, far, scaled, inverse, weight, vectors, chunk, part, after):
    size, width = grad.shape
    steps = size // ROW_BLOCK
    lanes = weight.shape[1]
    return row_call(
        functools.partial(first_back_kernel, len(after)),
        "first_back",
        [SCALAR, row_block(width)]
        + [row_block(width, chunk * steps)] * 2
        + [row_block(width), row_block(1), resident(weight.shape), resident(vectors.shape)]
        + [ELSEWHERE] * len(after),
        [
            (row_block(width), jax.ShapeDtypeStruct((size, width), F32)),
            (row_block(width), jax.ShapeDtypeStruct((size, width), BF16)),
        ]
        + [
            (
                by_row((ROW_BLOCK // part, part, lanes)),
                jax.ShapeDtypeStruct((size // part, part, lanes), BF16),
            )
        ]
        * 4
        + [(resident((8, width)), jax.ShapeDtypeStruct((8, width), F32))],
        (place, grad, own, far, scaled, inverse, weight, vectors, *after),
        size,
        2 * size * width * width,
    )


def output_grad_kernel(place, *refs):
    mixed, grads, out = refs[:CHUNKS], refs[CHUNKS : 2 * CHUNKS], refs[-1]
    lanes = out.shape[1]
    for step in range(out.shape[0]):
        at = slice(step * lanes, (step + 1) * lanes)
        out[place[0] ^ step] = sum(
            dot(m[:, at], g[...], (0, 0)) for m, g in zip(mixed, grads)
        ).astype(BF16)


def output_back(place, mixed, grads, ctx_size, after):
    size, width = mixed[0].shape
    shape = (ctx_size, width // ctx_size, width)
    return pl.pallas_call(
        output_grad_kernel,
        grid=(1,),
        in_specs=[SCALAR]
        + [resident((size, width))] * (2 * CHUNKS)
        + [ELSEWHERE] * len(after),
        out_specs=resident(shape),
        out_shape=jax.ShapeDtypeStruct(shape, BF16),
        compiler_params=pltpu.CompilerParams(vmem_limit_bytes=48 * MIB),
        cost_estimate=pl.CostEstimate(
            flops=2 * CHUNKS * size * width * width,
            bytes_accessed=4 * width * (width + CHUNKS * size),
            transcendentals=0,
        ),
        name="output_backward",
    )(place, *mixed, *grads, *after)


def on_device(
    sizes,
    tokens,
    segment_ids,
    project_weight,
    query_bias,
    value_bias,
    output_weight,
    output_bias,
    first_gain,
    first_shift,
    expand_weight,
    expand_bias,
    reduce_weight,
    reduce_bias,
    second_gain,
    second_shift,
    grad_out,
):
    chips = sizes["z"] * sizes["y"] * sizes["x"]
    ctx_size = sizes["x"] * sizes["c"]
    everyone = chips * sizes["c"]
    seq_count, part, width = tokens.shape
    rows_count = seq_count * part
    hidden = expand_weight.shape[1]
    share = width // everyone
    own_hidden = hidden // 2
    lanes = width // ctx_size
    place = lax.axis_index(CTX)
    core = lax.axis_index("c")
    low_core = core == 0

    def hop(array, step):
        return lax.ppermute(array, CTX, [(i, i ^ step) for i in range(ctx_size)])

    def swap(array):
        return lax.ppermute(array, "c", [(0, 1), (1, 0)])

    def chosen(array, index, axis):
        return lax.dynamic_index_in_dim(array, index, axis, keepdims=False)

    def pair(own, other, axis, low):
        return jnp.where(
            low, jnp.stack([own, other], axis=axis), jnp.stack([other, own], axis=axis)
        )

    def by_core(own, other, axis):
        return pair(own, other, axis, low_core)

    def bit_of(name, step):
        return (lax.axis_index(name) // step) % 2

    def trade(array, name, step=1):
        return lax.ppermute(array, name, [(i, i ^ step) for i in range(sizes[name])])

    def widen(array, name, axis=0, step=1):
        return pair(array, trade(array, name, step), axis, bit_of(name, step) == 0)

    def halve(array, axis, name, step=1):
        me = bit_of(name, step)
        return chosen(array, me, axis).astype(F32) + trade(
            chosen(array, 1 - me, axis), name, step
        ).astype(F32)

    z_steps = [1 << i for i in range(sizes["z"].bit_length() - 1)]

    def z_gather(array):
        for index, step in enumerate(z_steps[::-1]):
            array = widen(array, "z", index, step)
        return array

    def z_scatter(blocks, kind=BF16):
        for step in z_steps:
            blocks = blocks.reshape((blocks.shape[0] // 2, 2) + blocks.shape[1:])
            blocks = halve(blocks.astype(kind), 1, "z", step)
        return blocks[0]

    seg_parts = segment_ids.reshape(seq_count, ctx_size, part)
    seg = jnp.concatenate([chosen(seg_parts, place ^ r, 1) for r in range(ctx_size)], axis=1)
    seg_key = seg[:, :, None]
    seg_query = seg[:, None, :]

    vectors = (
        query_bias,
        value_bias,
        output_bias,
        first_gain,
        first_shift,
        reduce_bias,
        second_gain,
        second_shift,
        expand_bias,
    )
    vector_count = 8 * share + expand_bias.shape[0]
    filler = jnp.pad(jnp.stack(vectors[:8]), ((0, 8), (0, 3 * lanes - share))) + jnp.pad(
        expand_bias[None], ((8, 7), (0, 3 * lanes - expand_bias.shape[0]))
    )
    held = jnp.stack(
        [
            jnp.concatenate(
                [
                    jnp.concatenate(
                        [
                            project_weight[:, (ctx_size * j + p) * lanes :][:, :lanes]
                            for j in range(3)
                        ],
                        axis=1,
                    ),
                    filler,
                ]
            )
            for p in range(ctx_size)
        ]
    )
    held = lax.all_to_all(held, CTX, 0, 0, tiled=True)
    sent, held = lax.optimization_barrier((tokens, held))
    across = hop(sent, 2)
    gathered = (tokens, swap(sent), across, swap(across))
    mine = jnp.concatenate(
        [held[:, :share, j * lanes : (j + 1) * lanes].reshape(-1, lanes) for j in range(3)]
    )
    vector_rows = held[:, share:, :lanes].reshape(-1, lanes)
    out_pieces = jnp.concatenate(
        [output_weight[:, i * lanes : (i + 1) * lanes] for i in range(ctx_size)]
    )
    full_project = lax.all_gather(
        jnp.concatenate([widen(out_pieces, "x").reshape(-1, lanes), mine, vector_rows]),
        SEQ,
        axis=0,
    )
    packed = full_project[:, -16 * ctx_size :].reshape(everyone, 16, lanes).astype(F32)
    exp_bias = chosen(
        packed[:, 8, : expand_bias.shape[0]].reshape(chips, 2, -1), core, 1
    ).reshape(1, own_hidden)
    vectors = jnp.swapaxes(packed[:, :8, :share], 0, 1).reshape(8, width)
    full_query, full_value = vectors[0], vectors[1]
    bias_all = jnp.concatenate(
        [
            lax.dynamic_slice_in_dim(full_query, place * lanes, lanes),
            jnp.zeros((lanes,), F32),
            lax.dynamic_slice_in_dim(full_value, place * lanes, lanes),
        ]
    )[None]

    columns = expand_weight.reshape(share, chips, 2, own_hidden // chips)
    own_columns = chosen(columns, core, 2).reshape(share, own_hidden)
    far_columns = chosen(columns, 1 - core, 2).reshape(share, own_hidden)
    both = by_core(own_columns, swap(far_columns), 0)

    def in_pieces(array):
        rows_of, wide = array.shape
        return jnp.swapaxes(array.reshape(rows_of, wide // PIECE, PIECE), 0, 1).reshape(
            -1, 2 * share, PIECE
        )

    own_pieces = jnp.concatenate(
        [
            in_pieces(both.reshape(2 * share, own_hidden)),
            jnp.swapaxes(
                reduce_weight.reshape(2, 2 * share, width // PIECE, PIECE), 1, 2
            ).reshape(-1, 2 * share, PIECE),
        ]
    )
    own_pieces = hold(own_pieces, [across])
    weights = lax.all_gather(widen(own_pieces, "x"), SEQ, axis=0).reshape(
        chips, -1, 2 * share, PIECE
    )

    rows = tokens.reshape(rows_count, width)
    where = place.reshape(1).astype(jnp.int32)
    seqs = seq_count // CHUNKS
    saved, kept_rows, mixed_low, first_low, scaled_one, inverse_one = [], [], [], [], [], []
    for index in range(CHUNKS):
        at = slice(index * seqs, (index + 1) * seqs)
        *mixed, all_rows, kept = attend(
            gathered, full_project, bias_all, seg_key[at], seg_query[at], at.start, []
        )
        kept_rows.append(all_rows)
        saved.append(kept)
        if index == 0:
            out_half = unpack(full_project, share, width, mixed[:1])
            full_output = by_core(out_half, swap(out_half), 1).reshape(ctx_size, lanes, width)
        arrived = [mixed[0]] + [hop(mixed[r], r) for r in (1, 2, 3)]
        low, scaled, inverse, joined = first_norm(
            where, arrived, rows, full_output, vectors, index
        )
        mixed_low.append(joined)
        first_low.append(low)
        scaled_one.append(scaled)
        inverse_one.append(inverse)
    first_far = [swap(low) for low in first_low]
    act, slope, own_sum, far_sum = feed(first_low, first_far, weights, exp_bias)
    far_sum = swap(far_sum)

    grad_rows = grad_out.reshape(rows_count, width)
    layer_parts, grad_second, grad_reduced, second_sums = zip(
        *(
            second_norm(scaled_one[index], own_sum, far_sum, grad_rows, vectors, index)
            for index in range(CHUNKS)
        )
    )
    layer_work = jnp.concatenate(layer_parts, axis=0).reshape(tokens.shape)
    weight_grad, expand_bias_grad, own_back, far_back = feed_back(
        grad_reduced + tuple(swap(grad) for grad in grad_reduced),
        first_low + first_far,
        act,
        slope,
        weights,
    )
    weight_owned = lax.psum_scatter(
        weight_grad.reshape((-1, sizes["x"]) + weight_grad.shape[1:]),
        SEQ,
        scatter_dimension=0,
        tiled=True,
    )[0]
    far_back = swap(far_back)
    grad_hidden, grad_attended, grad_mixed, first_sums = [], [], [], []
    for index in range(CHUNKS):
        grad, low, *mixed, sums = first_back(
            where,
            grad_second[index],
            own_back,
            far_back,
            scaled_one[index],
            inverse_one[index],
            full_output,
            vectors,
            index,
            part,
            grad_mixed[0][1:2] if index else [],
        )
        grad_hidden.append(grad.reshape(seqs, part, width))
        grad_attended.append(low)
        grad_mixed.append([mixed[0]] + [hop(mixed[r], r) for r in (1, 2, 3)])
        first_sums.append(sums)
    def shared_sums(after):
        output_grad = output_back(where, mixed_low, grad_attended, ctx_size, after)
        zeros = jnp.zeros((width,), F32)
        first_total, second_total = sum(first_sums), sum(second_sums)
        grad_vectors = (
            zeros,
            zeros,
            first_total[2],
            first_total[0],
            first_total[1],
            second_total[2],
            second_total[0],
            second_total[1],
        )
        hidden_sums = expand_bias_grad.reshape(chips, 1, own_hidden // chips)
        hidden_sums = jnp.where(
            low_core,
            jnp.concatenate([hidden_sums, jnp.zeros_like(hidden_sums)], axis=1),
            jnp.concatenate([jnp.zeros_like(hidden_sums), hidden_sums], axis=1),
        )
        packed_grads = jnp.concatenate(
            [vector.reshape(everyone, share) for vector in grad_vectors]
            + [hidden_sums.reshape(everyone, -1)],
            axis=1,
        )
        packed_grads = jnp.pad(packed_grads, ((0, 0), (0, width - vector_count))).astype(BF16)
        shared = jnp.concatenate(
            [output_grad.reshape(everyone, share, width), packed_grads[:, None]], axis=1
        ).reshape(sizes["z"], 2, sizes["x"], 2, share + 1, width)
        shared_chip = halve(shared, 3, "c").astype(BF16)
        shared = halve(shared_chip, 2, "x").astype(BF16)
        return shared_chip, shared

    project_grad = []
    work_parts = []
    across_sums = []
    work_hops = []
    sum_parts = []
    for index in range(CHUNKS):
        at = slice(index * seqs, (index + 1) * seqs)
        if index == 1:
            shared_chip, shared = shared_sums(grad_mixed[1][1:] + sum_parts)
        project_part, r0, r1, r2, r3, sums = attend_back(
            saved[index],
            kept_rows[index],
            grad_mixed[index],
            full_project,
            seg_key[at],
            seg_query[at],
            project_grad,
            index == CHUNKS - 1,
            across_sums[:1] + [shared_chip] if index else grad_attended[1:],
        )
        project_grad = [project_part]
        across_sums.append(add_low(r2, swap(r3), work_hops[:1] if index else grad_mixed[1][1:]))
        work_hops.append(hop(across_sums[index], 2))
        work_parts.append(
            grad_hidden[index] + r0 + swap(r1).astype(F32) + work_hops[index].astype(F32)
        )
        sum_parts.append(sums)
    grad_work = jnp.concatenate(work_parts, axis=0)
    column_sums = jnp.sum(jnp.concatenate(sum_parts, axis=0), axis=(0, 1))
    holders = sizes["z"] * 2
    owners = holders // ctx_size
    bias_grads = jnp.concatenate(
        [
            column_sums[at : at + lanes].reshape(owners, ctx_size, share)
            for at in (0, 2 * lanes)
        ],
        axis=2,
    )
    bias_grads = jnp.pad(
        bias_grads, ((0, 0), (0, 16 - ctx_size), (0, 3 * lanes - 2 * share))
    ).astype(BF16)
    bias_grads = lax.dynamic_update_slice_in_dim(
        jnp.zeros((holders, 16, 3 * lanes), BF16), bias_grads, place * owners, 0
    )
    blocks = join(
        project_grad[0].reshape(holders, ctx_size * share, 3 * lanes),
        bias_grads,
        work_hops[:1],
    )
    blocks = halve(blocks.reshape((sizes["z"], 2) + blocks.shape[1:]), 1, "y").astype(BF16)
    blocks = hold(blocks, work_hops[1:])
    shared = halve(hold(shared, [blocks]), 1, "y")
    shared = z_scatter(shared)
    output_owned = shared[:share]
    owned = shared[share, :vector_count]
    blocks = z_scatter(blocks)
    weight_owned = halve(weight_owned, 0, "x")
    blocks = jnp.concatenate(
        [
            blocks[: ctx_size * share].reshape(ctx_size, share, 3 * lanes),
            jnp.pad(
                blocks[ctx_size * share :][:ctx_size, None], ((0, 0), (0, 7), (0, 0))
            ),
        ],
        axis=1,
    )
    held = lax.all_to_all(hold(blocks, [weight_owned]), CTX, 0, 0, tiled=True)
    bias_owned = jnp.sum(held[:, share, : 2 * share], axis=0)
    project_owned = jnp.concatenate(
        [
            held[p, :share, j * lanes : (j + 1) * lanes]
            for j in range(3)
            for p in range(ctx_size)
        ],
        axis=1,
    )
    expand_pieces = own_hidden // PIECE
    far_rows = jnp.swapaxes(
        weight_owned[:expand_pieces].reshape(expand_pieces, 2, share, PIECE), 0, 1
    )
    expand_owned = by_core(
        jnp.swapaxes(chosen(far_rows, core, 0), 0, 1).reshape(share, chips, -1),
        jnp.swapaxes(swap(chosen(far_rows, 1 - core, 0)), 0, 1).reshape(share, chips, -1),
        2,
    ).reshape(share, hidden)
    reduce_owned = jnp.swapaxes(
        weight_owned[expand_pieces:].reshape(2, width // PIECE, 2 * share, PIECE), 1, 2
    ).reshape(4 * share, width)

    small = [owned[i * share : (i + 1) * share] for i in range(8)]
    return (
        layer_work,
        grad_work,
        project_owned.astype(F32),
        bias_owned[:share],
        bias_owned[share:],
        output_owned.astype(F32),
        small[2],
        small[3],
        small[4],
        expand_owned.astype(F32),
        owned[8 * share :],
        reduce_owned.astype(F32),
        small[5],
        small[6],
        small[7],
    )


def solution(mesh):
    seq_size, ctx_size = mesh.shape["seq"], mesh.shape["ctx"]
    sizes = {"z": seq_size // 2, "y": 2, "x": ctx_size // 2, "c": 2}
    fine = Mesh(mesh.devices.reshape(tuple(sizes.values())), tuple(sizes))
    rows = P(SEQ, CTX, None)
    matrix = P(ALL, None)
    vector = P(ALL)
    return jax.shard_map(
        functools.partial(on_device, sizes),
        mesh=fine,
        in_specs=(
            rows,
            P(SEQ, None),
            matrix,
            vector,
            vector,
            matrix,
            vector,
            vector,
            vector,
            matrix,
            vector,
            matrix,
            vector,
            vector,
            vector,
            rows,
        ),
        out_specs=(
            rows,
            rows,
            matrix,
            vector,
            vector,
            matrix,
            vector,
            vector,
            vector,
            matrix,
            vector,
            matrix,
            vector,
            vector,
            vector,
        ),
        check_vma=False,
    )
```

```python
import functools

import jax
import jax.numpy as jnp
from jax import lax
from jax.experimental import pallas as pl
from jax.experimental.pallas import tpu as pltpu
from jax.sharding import Mesh
from jax.sharding import PartitionSpec as P

HEADS = 16
HEAD_DIM = 64
CHUNKS = 2
PIECE = 256
MIB = 1 << 20
CHIPS = ("z", "y", "x")
SEQ = ("z", "y")
CTX = ("x", "c")
ALL = ("z", "y", "x", "c")
F32 = jnp.float32
BF16 = jnp.bfloat16
ELSEWHERE = pl.BlockSpec(memory_space=pl.ANY)


def dot(left, right, contract=(1, 0)):
    return lax.dot_general(
        left, right, (((contract[0],), (contract[1],)), ((), ())), preferred_element_type=F32
    )


def resident(shape):
    return pl.BlockSpec(shape, lambda i: (0,) * len(shape), pipeline_mode=pl.Buffered(1))


def by_row(shape):
    return pl.BlockSpec(shape, lambda i: (i,) + (0,) * (len(shape) - 1))


def flat(block):
    wide = block.shape[-1]
    if block.shape[-2] % 16:
        return block.astype(F32).reshape(-1, wide).astype(BF16)
    return block.reshape(-1, wide)


def hold_kernel(source, *refs):
    refs[-1][...] = source[...]


def hold(array, after):
    return pl.pallas_call(
        hold_kernel,
        grid=(1,),
        in_specs=[resident(array.shape)] + [ELSEWHERE] * len(after),
        out_specs=resident(array.shape),
        out_shape=jax.ShapeDtypeStruct(array.shape, array.dtype),
        compiler_params=pltpu.CompilerParams(vmem_limit_bytes=16 * MIB),
        name="hold",
    )(array, *after)


def add_kernel(left, right, *refs):
    refs[-1][...] = (left[...].astype(F32) + right[...].astype(F32)).astype(BF16)


def add_low(left, right, after):
    block = (1,) + left.shape[1:]
    return pl.pallas_call(
        add_kernel,
        grid=(left.shape[0],),
        in_specs=[by_row(block)] * 2 + [ELSEWHERE] * len(after),
        out_specs=by_row(block),
        out_shape=jax.ShapeDtypeStruct(left.shape, BF16),
        compiler_params=pltpu.CompilerParams(vmem_limit_bytes=16 * MIB),
        name="add_low",
    )(left, right, *after)


def join_kernel(top, below, *refs):
    out = refs[-1]
    out[:, : top.shape[1]] = top[...]
    out[:, top.shape[1] :] = below[...]


def join(top, below, after):
    shape = (top.shape[0], top.shape[1] + below.shape[1], top.shape[2])
    return pl.pallas_call(
        join_kernel,
        grid=(1,),
        in_specs=[resident(top.shape), resident(below.shape)] + [ELSEWHERE] * len(after),
        out_specs=resident(shape),
        out_shape=jax.ShapeDtypeStruct(shape, BF16),
        compiler_params=pltpu.CompilerParams(vmem_limit_bytes=32 * MIB),
        name="join",
    )(top, below, *after)


def unpack_kernel(pieces, *refs):
    out = refs[-1]
    height, lanes = out.shape[2], pieces.shape[2]
    for half in range(2):
        for i in range(out.shape[3] // lanes):
            start = (half * (out.shape[3] // lanes) + i) * height
            out[:, half, :, i * lanes : (i + 1) * lanes] = pieces[:, start : start + height]


def unpack(gathered, share, width, after):
    count, _, lanes = gathered.shape
    columns = width // lanes
    if share % 16:
        pieces = gathered[:, : 2 * columns * share].reshape(count, 2, columns, share, lanes)
        return jnp.swapaxes(pieces, 2, 3).reshape(2 * count, share, width)
    return pl.pallas_call(
        unpack_kernel,
        grid=(1,),
        in_specs=[pl.BlockSpec((count, 2 * columns * share, lanes), lambda i: (0, 0, 0))]
        + [ELSEWHERE] * len(after),
        out_specs=pl.BlockSpec((count, 2, share, width), lambda i: (0, 0, 0, 0)),
        out_shape=jax.ShapeDtypeStruct((count, 2, share, width), BF16),
        compiler_params=pltpu.CompilerParams(vmem_limit_bytes=16 * MIB),
        name="unpack",
    )(gathered, *after).reshape(2 * count, share, width)


def softmax_down(scores, allowed):
    scores = jnp.where(allowed, scores, -1e30)
    top = jnp.max(scores, axis=0, keepdims=True)
    expo = jnp.exp(scores - top)
    total = jnp.sum(expo, axis=0, keepdims=True)
    return expo * (1.0 / total)


def head_lanes(width, head):
    lane = lax.broadcasted_iota(jnp.int32, (1, width), 1)
    return (lane // HEAD_DIM == head).astype(F32)


def attend_kernel(late, t0, t1, t2, t3, wq, wk, wv, bias, seg_key, seg_query, *refs):
    m0, m1, m2, m3, kept, saved = refs[late:]
    part = t0.shape[1]
    rows = jnp.concatenate([t[0] for t in (t0, t1, t2, t3)], axis=0)
    kept[0] = rows
    width = wq.shape[2]
    queries, keys, values = [
        dot(rows, flat(w[...])) + bias[:, i * width : (i + 1) * width]
        for i, w in enumerate((wq, wk, wv))
    ]
    for i, part_of in enumerate((queries, keys, values)):
        saved[0, :, i * width : (i + 1) * width] = part_of.astype(BF16)
    queries = (queries.astype(BF16).astype(F32) * HEAD_DIM**-0.5).astype(BF16)
    keys = keys.astype(BF16).astype(F32)
    values_t = jnp.transpose(values).astype(BF16)
    allowed = seg_key[0] == seg_query[0]
    mixed = []
    for head in range(width // HEAD_DIM):
        own_keys = (keys * head_lanes(width, head)).astype(BF16)
        chances = softmax_down(dot(own_keys, queries, (1, 1)), allowed)
        own_values = values_t[head * HEAD_DIM : (head + 1) * HEAD_DIM]
        mixed.append(dot(own_values, chances.astype(BF16)))
    mixed = jnp.transpose(jnp.concatenate(mixed, axis=0)).astype(BF16)
    for index, out in enumerate((m0, m1, m2, m3)):
        out[0] = mixed[index * part : (index + 1) * part]


def project_specs(weight, depth):
    shape = (weight.shape[0], depth // weight.shape[0], weight.shape[2])
    return [
        pl.BlockSpec(shape, lambda i, j=j: (0, j + 2, 0), pipeline_mode=pl.Buffered(1))
        for j in range(3)
    ]


def attend(tokens, weight, bias, seg_key, seg_query, first, after):
    count, part, depth = tokens[0].shape
    count = count // CHUNKS
    wide = bias.shape[1]
    length = 4 * part
    return pl.pallas_call(
        functools.partial(attend_kernel, len(after)),
        grid=(count,),
        in_specs=[pl.BlockSpec((1, part, depth), lambda i: (i + first, 0, 0))] * 4
        + project_specs(weight, depth)
        + [
            resident((1, wide)),
            by_row((1, length, 1)),
            by_row((1, 1, length)),
        ]
        + [ELSEWHERE] * len(after),
        out_specs=[by_row((1, part, wide // 3))] * 4
        + [by_row((1, length, depth)), by_row((1, length, wide))],
        out_shape=[jax.ShapeDtypeStruct((count, part, wide // 3), BF16)] * 4
        + [
            jax.ShapeDtypeStruct((count, length, depth), BF16),
            jax.ShapeDtypeStruct((count, length, wide), BF16),
        ],
        compiler_params=pltpu.CompilerParams(vmem_limit_bytes=40 * MIB),
        cost_estimate=pl.CostEstimate(
            flops=count * length * wide * (2 * depth + 16 * length // 3),
            bytes_accessed=count * length * (depth + 2 * wide) * 2,
            transcendentals=count * length * length * wide // (3 * HEAD_DIM),
        ),
        name="attend_forward",
    )(*tokens, weight, weight, weight, bias, seg_key, seg_query, *after)


def attend_back_kernel(
    late, earlier, saved, kept, g0, g1, g2, g3, wq, wk, wv, seg_key, seg_query, *refs
):
    grad_weight, r0, r1, r2, r3, sums, total = refs[late + earlier :]

    @pl.when(pl.program_id(0) == 0)
    def _():
        total[...] = refs[0][...] if earlier else jnp.zeros_like(total)

    part = g0.shape[1]
    width = saved.shape[2] // 3
    factor = HEAD_DIM**-0.5
    queries = (saved[0, :, :width].astype(F32) * factor).astype(BF16)
    keys = saved[0, :, width : 2 * width].astype(F32)
    values = saved[0, :, 2 * width :].astype(F32)
    keys_t = jnp.transpose(keys * factor).astype(BF16)
    grad_mixed = jnp.concatenate([g[0] for g in (g0, g1, g2, g3)], axis=0)
    allowed = seg_key[0] == seg_query[0]
    grad_queries = []
    grad_keys = None
    grad_values = None
    for head in range(width // HEAD_DIM):
        lanes = head_lanes(width, head)
        chances = softmax_down(
            dot((keys * lanes).astype(BF16), queries, (1, 1)), allowed
        )
        grad_weights = dot((values * lanes).astype(BF16), grad_mixed, (1, 1))
        inner = jnp.sum(chances * grad_weights, axis=0, keepdims=True)
        grad_scores = (chances * (grad_weights - inner)).astype(BF16)
        grad_queries.append(dot(keys_t[head * HEAD_DIM : (head + 1) * HEAD_DIM], grad_scores))
        keys_term = dot(grad_scores, queries)
        values_term = dot(chances.astype(BF16), grad_mixed)
        if head == 0:
            grad_keys, grad_values = keys_term, values_term
        else:
            here = lanes > 0.5
            grad_keys = jnp.where(here, keys_term, grad_keys)
            grad_values = jnp.where(here, values_term, grad_values)
    grad_queries = jnp.concatenate(grad_queries, axis=0)
    terms = [
        jnp.transpose(grad_queries).astype(BF16),
        grad_keys.astype(BF16),
        grad_values.astype(BF16),
    ]
    total[:width] += dot(grad_queries.astype(BF16), kept[0])
    for i, term in enumerate(terms):
        sums[0, :, i * width : (i + 1) * width] = jnp.sum(
            term.astype(F32), axis=0, keepdims=True
        )
        if i:
            total[i * width : (i + 1) * width] += dot(term, kept[0], (0, 0))
    rows = sum(dot(term, flat(w[...]), (1, 1)) for term, w in zip(terms, (wq, wk, wv)))
    for index, out in enumerate((r0, r1, r2, r3)):
        out[0] = rows[index * part : (index + 1) * part].astype(out.dtype)

    @pl.when(pl.program_id(0) == pl.num_programs(0) - 1)
    def _():
        if grad_weight.dtype == BF16:
            grad_weight[...] = jnp.transpose(total[...]).astype(BF16)
        else:
            grad_weight[...] = total[...]


def attend_back(saved, kept, grads, weight, seg_key, seg_query, earlier, done, after):
    count, part, width = grads[0].shape
    depth, wide = width * 4, width * 3
    length = 4 * part
    shape, kind = ((depth, wide), BF16) if done else ((wide, depth), F32)
    return pl.pallas_call(
        functools.partial(attend_back_kernel, len(after), len(earlier)),
        grid=(count,),
        in_specs=[by_row((1, length, wide)), by_row((1, length, depth))]
        + [by_row((1, part, width))] * 4
        + project_specs(weight, depth)
        + [
            by_row((1, length, 1)),
            by_row((1, 1, length)),
        ]
        + [resident((wide, depth))] * len(earlier)
        + [ELSEWHERE] * len(after),
        out_specs=[resident(shape)]
        + [by_row((1, part, depth))] * 4
        + [by_row((1, 1, wide))],
        out_shape=[jax.ShapeDtypeStruct(shape, kind)]
        + [jax.ShapeDtypeStruct((count, part, depth), t) for t in (F32, BF16, BF16, BF16)]
        + [jax.ShapeDtypeStruct((count, 1, wide), F32)],
        scratch_shapes=[pltpu.VMEM((wide, depth), F32)],
        compiler_params=pltpu.CompilerParams(vmem_limit_bytes=52 * MIB),
        cost_estimate=pl.CostEstimate(
            flops=count * length * wide * (4 * depth + 40 * length // 3),
            bytes_accessed=count * length * (3 * depth + 3 * wide) * 2,
            transcendentals=count * length * length * wide // (3 * HEAD_DIM),
        ),
        name="attend_backward",
    )(saved, kept, *grads, weight, weight, weight, seg_key, seg_query, *earlier, *after)


def column(shape):
    return pl.BlockSpec(shape, lambda i: (0, i))


def expand_piece(ref):
    return jnp.concatenate([flat(ref[:, i]) for i in range(ref.shape[1])], axis=1)


def reduce_piece(ref):
    columns = ref.shape[1] // 2
    halves = [
        jnp.concatenate([ref[:, half * columns + i] for i in range(columns)], axis=2)
        for half in range(2)
    ]
    return flat(jnp.concatenate(halves, axis=1))


def feed_kernel(*refs):
    sources, (expand, bias, reduce, act, slope, own_out, other_out, far_sum) = (
        refs[: 2 * CHUNKS],
        refs[2 * CHUNKS :],
    )
    step = pl.program_id(0)

    @pl.when(step == 0)
    def _():
        own_out[...] = jnp.zeros_like(own_out)
        far_sum[...] = jnp.zeros_like(far_sum)

    into = expand_piece(expand)
    back = reduce_piece(reduce)
    block = 256
    per = sources[0].shape[0] // block
    half_count = CHUNKS * per

    def inner(index):
        start = index % per * block
        return dot(sources[index // per][start : start + block], into) + bias[...]

    ahead = inner(0)
    for index in range(2 * half_count):
        inside = ahead
        if index + 1 < 2 * half_count:
            ahead = inner(index + 1)
        total = own_out if index < half_count else far_sum
        at = slice(index % half_count * block, (index % half_count + 1) * block)
        to = slice(index * block, (index + 1) * block)
        square = inside * inside
        curve = jnp.tanh(inside * (0.7978845608028654 + 0.7978845608028654 * 0.044715 * square))
        half = 0.5 * curve + 0.5
        active = (inside * half).astype(BF16)
        act[to] = active
        tilt = 0.7978845608028654 * 0.5 + 0.7978845608028654 * 1.5 * 0.044715 * square
        slope[to] = (half + inside * (1.0 - curve * curve) * tilt).astype(BF16)
        total[at] += dot(active, back)

    @pl.when(step == pl.num_programs(0) - 1)
    def _():
        other_out[...] = far_sum[...].astype(BF16)


def feed_weights(weights, pieces, columns):
    chips, _, rows, _ = weights.shape
    return [
        pl.BlockSpec((chips, pieces, rows, PIECE), lambda i: (0, i, 0, 0)),
        pl.BlockSpec(
            (pieces * PIECE // (2 * rows), 2 * columns, rows, PIECE), lambda i: (i, 1, 0, 0)
        ),
    ]


def feed(own, other, weights, bias):
    block, depth = own[0].shape
    rows = CHUNKS * block
    hidden = bias.shape[1]
    pieces = 2
    wide = pieces * PIECE
    expand_spec, reduce_spec = feed_weights(weights, pieces, depth // PIECE)
    return pl.pallas_call(
        feed_kernel,
        grid=(hidden // wide,),
        in_specs=[resident((block, depth))] * (2 * CHUNKS)
        + [expand_spec, column((1, wide)), reduce_spec],
        out_specs=[column((2 * rows, wide))] * 2 + [resident((rows, depth))] * 2,
        out_shape=[jax.ShapeDtypeStruct((2 * rows, hidden), BF16)] * 2
        + [
            jax.ShapeDtypeStruct((rows, depth), F32),
            jax.ShapeDtypeStruct((rows, depth), BF16),
        ],
        scratch_shapes=[pltpu.VMEM((rows, depth), F32)],
        compiler_params=pltpu.CompilerParams(vmem_limit_bytes=56 * MIB),
        cost_estimate=pl.CostEstimate(
            flops=8 * rows * depth * hidden,
            bytes_accessed=4 * rows * (2 * hidden + 3 * depth),
            transcendentals=2 * rows * hidden,
        ),
        name="feed_forward",
    )(*own, *other, weights, bias, weights)


def feed_back_kernel(*refs):
    grads, sources = refs[: 2 * CHUNKS], refs[2 * CHUNKS : 4 * CHUNKS]
    act, slope, expand, reduce, weight_grad, bias_grad, own_out, other_out, far_sum, inside = refs[
        4 * CHUNKS :
    ]
    step = pl.program_id(0)
    block = grads[0].shape[0]

    @pl.when(step == 0)
    def _():
        own_out[...] = jnp.zeros_like(own_out)
        far_sum[...] = jnp.zeros_like(far_sum)

    into = expand_piece(expand)
    back = reduce_piece(reduce)
    bias_sum = jnp.zeros(bias_grad.shape, F32)
    for index in range(2 * CHUNKS):
        total = own_out if index < CHUNKS else far_sum
        at = slice(index % CHUNKS * block, (index % CHUNKS + 1) * block)
        to = slice(index * block, (index + 1) * block)
        grad_act = dot(grads[index][...], back, (1, 1))
        part = (grad_act * slope[to].astype(F32)).astype(BF16)
        inside[to] = part
        bias_sum += jnp.sum(part.astype(F32), axis=0, keepdims=True)
        total[at] += dot(part, into, (1, 1))
    bias_grad[...] = bias_sum
    chips, pieces, height, _ = weight_grad.shape
    columns = pieces // 4
    wide = inside.shape[1]
    reduce_grad = sum(
        dot(act[i * block : (i + 1) * block], grad[...], (0, 0)) for i, grad in enumerate(grads)
    )
    count = wide // (2 * height)
    reduce_grad = reduce_grad.reshape(count, 2 * height, reduce_grad.shape[1]).astype(BF16)
    mine = pl.ds(step * count, count)
    for half in range(2):
        for i in range(columns):
            weight_grad[mine, (2 + half) * columns + i] = reduce_grad[
                :, half * height : (half + 1) * height, i * PIECE : (i + 1) * PIECE
            ]
    flipped = sum(
        dot(inside[i * block : (i + 1) * block], source[...], (0, 0))
        for i, source in enumerate(sources)
    )
    expand_grad = jnp.transpose(flipped).reshape(chips, height, wide).astype(BF16)
    for i in range(wide // PIECE):
        weight_grad[:, step * (wide // PIECE) + i] = expand_grad[
            :, :, i * PIECE : (i + 1) * PIECE
        ]

    @pl.when(step == pl.num_programs(0) - 1)
    def _():
        other_out[...] = far_sum[...].astype(BF16)


def feed_back(grads, sources, act, slope, weights):
    block, depth = grads[0].shape
    rows = CHUNKS * block
    hidden = act.shape[1]
    chips, _, height, _ = weights.shape
    pieces = 2 * hidden // PIECE
    expand_spec, reduce_spec = feed_weights(weights, 2, depth // PIECE)
    wide = 2 * PIECE
    return pl.pallas_call(
        feed_back_kernel,
        grid=(hidden // wide,),
        in_specs=[resident((block, depth))] * (4 * CHUNKS)
        + [column((2 * rows, wide))] * 2
        + [expand_spec, reduce_spec],
        out_specs=[
            resident((chips, pieces, height, PIECE)),
            column((1, wide)),
        ]
        + [resident((rows, depth))] * 2,
        out_shape=[
            jax.ShapeDtypeStruct((chips, pieces, height, PIECE), BF16),
            jax.ShapeDtypeStruct((1, hidden), F32),
            jax.ShapeDtypeStruct((rows, depth), F32),
            jax.ShapeDtypeStruct((rows, depth), BF16),
        ],
        scratch_shapes=[
            pltpu.VMEM((rows, depth), F32),
            pltpu.VMEM((2 * rows, wide), BF16),
        ],
        compiler_params=pltpu.CompilerParams(vmem_limit_bytes=56 * MIB),
        cost_estimate=pl.CostEstimate(
            flops=16 * rows * depth * hidden,
            bytes_accessed=4 * rows * (2 * hidden + 5 * depth) + 8 * depth * hidden,
            transcendentals=0,
        ),
        name="feed_backward",
    )(*grads, *sources, act, slope, weights, weights)


def normalize(values):
    center = values - jnp.mean(values, axis=-1, keepdims=True)
    inverse = lax.rsqrt(jnp.mean(center * center, axis=-1, keepdims=True) + 1e-05)
    return (center * inverse, inverse)


def normalize_back(incoming, scaled, inverse, gain):
    grad_scaled = incoming * gain
    mean_one = jnp.mean(grad_scaled, axis=-1, keepdims=True)
    mean_two = jnp.mean(grad_scaled * scaled, axis=-1, keepdims=True)
    return inverse * (grad_scaled - mean_one - scaled * mean_two)


def add_sums(out, *rows):
    rows = [jnp.sum(row, axis=0, keepdims=True) for row in rows]
    rows.append(jnp.zeros((out.shape[0] - len(rows), out.shape[1]), F32))
    rows = jnp.concatenate(rows, axis=0)

    @pl.when(pl.program_id(0) == 0)
    def _():
        out[...] = rows

    @pl.when(pl.program_id(0) > 0)
    def _():
        out[...] += rows


OUT_BIAS, GAIN_ONE, SHIFT_ONE, RED_BIAS, GAIN_TWO, SHIFT_TWO = (slice(i, i + 1) for i in range(2, 8))
SCALAR = pl.BlockSpec(memory_space=pltpu.SMEM)
ROW_BLOCK = 256


def row_call(kernel, name, ins, outs, arrays, rows, cost):
    return pl.pallas_call(
        kernel,
        grid=(rows // ROW_BLOCK,),
        in_specs=ins,
        out_specs=[spec for spec, _ in outs],
        out_shape=[shape for _, shape in outs],
        compiler_params=pltpu.CompilerParams(vmem_limit_bytes=48 * MIB),
        cost_estimate=pl.CostEstimate(flops=cost, bytes_accessed=rows << 14, transcendentals=rows),
        name=name,
    )(*arrays)


def row_block(width, first=0):
    return pl.BlockSpec((ROW_BLOCK, width), lambda i: (i + first, 0))


def first_norm_kernel(place, m0, m1, m2, m3, tokens, weight, vectors, low, scaled, inverse, mixed):
    total = tokens[...].astype(F32) + vectors[OUT_BIAS]
    parts = [m[...].reshape(ROW_BLOCK, -1) for m in (m0, m1, m2, m3)]
    mixed[...] = jnp.concatenate(parts, axis=1)
    for step, part in enumerate(parts):
        total += dot(part, weight[place[0] ^ step])
    scaled_one, inverse_one = normalize(total)
    scaled[...] = scaled_one
    inverse[...] = inverse_one
    low[...] = (scaled_one * vectors[GAIN_ONE] + vectors[SHIFT_ONE]).astype(BF16)


def first_norm(place, mixed, rows, weight, vectors, chunk):
    width = rows.shape[1]
    count, part, lanes = mixed[0].shape
    size = count * part
    steps = size // ROW_BLOCK
    return row_call(
        first_norm_kernel,
        "first_norm",
        [SCALAR]
        + [by_row((ROW_BLOCK // part, part, lanes))] * 4
        + [row_block(width, chunk * steps), resident(weight.shape), resident(vectors.shape)],
        [
            (row_block(width), jax.ShapeDtypeStruct((size, width), BF16)),
            (row_block(width), jax.ShapeDtypeStruct((size, width), F32)),
            (row_block(1), jax.ShapeDtypeStruct((size, 1), F32)),
            (row_block(width), jax.ShapeDtypeStruct((size, width), BF16)),
        ],
        (place, *mixed, rows, weight, vectors),
        size,
        2 * size * width * width,
    )


def second_norm_kernel(scaled, own, far, grad_out, vectors, layer, grad, low, sums):
    first = scaled[...] * vectors[GAIN_ONE] + vectors[SHIFT_ONE]
    reduced = own[...] + far[...].astype(F32) + vectors[RED_BIAS]
    scaled_two, inverse_two = normalize(first + reduced)
    layer[...] = (scaled_two * vectors[GAIN_TWO] + vectors[SHIFT_TWO]).astype(BF16)
    incoming = grad_out[...].astype(F32)
    grad_second = normalize_back(incoming, scaled_two, inverse_two, vectors[GAIN_TWO])
    grad[...] = grad_second
    low[...] = grad_second.astype(BF16)
    add_sums(sums, incoming * scaled_two, incoming, grad_second.astype(BF16).astype(F32))


def second_norm(scaled, own, far, grad_rows, vectors, chunk):
    size, width = scaled.shape
    steps = size // ROW_BLOCK
    return row_call(
        second_norm_kernel,
        "second_norm",
        [row_block(width)]
        + [row_block(width, chunk * steps)] * 3
        + [resident(vectors.shape)],
        [
            (row_block(width), jax.ShapeDtypeStruct((size, width), BF16)),
            (row_block(width), jax.ShapeDtypeStruct((size, width), F32)),
            (row_block(width), jax.ShapeDtypeStruct((size, width), BF16)),
            (resident((8, width)), jax.ShapeDtypeStruct((8, width), F32)),
        ],
        (scaled, own, far, grad_rows, vectors),
        size,
        size * width * 40,
    )


def first_back_kernel(
    late, place, grad, own, far, scaled, inverse, weight, vectors, *refs
):
    hidden, low, m0, m1, m2, m3, sums = refs[late:]
    incoming = grad[...] + own[...] + far[...].astype(F32)
    grad_hidden = normalize_back(incoming, scaled[...], inverse[...], vectors[GAIN_ONE])
    hidden[...] = grad_hidden
    attended = grad_hidden.astype(BF16)
    low[...] = attended
    for step, out in enumerate((m0, m1, m2, m3)):
        out[...] = dot(attended, weight[place[0] ^ step], (1, 1)).astype(BF16).reshape(out.shape)
    add_sums(sums, incoming * scaled[...], incoming, attended.astype(F32))


def first_back(place, grad, own, far, scaled, inverse, weight, vectors, chunk, part, after):
    size, width = grad.shape
    steps = size // ROW_BLOCK
    lanes = weight.shape[1]
    return row_call(
        functools.partial(first_back_kernel, len(after)),
        "first_back",
        [SCALAR, row_block(width)]
        + [row_block(width, chunk * steps)] * 2
        + [row_block(width), row_block(1), resident(weight.shape), resident(vectors.shape)]
        + [ELSEWHERE] * len(after),
        [
            (row_block(width), jax.ShapeDtypeStruct((size, width), F32)),
            (row_block(width), jax.ShapeDtypeStruct((size, width), BF16)),
        ]
        + [
            (
                by_row((ROW_BLOCK // part, part, lanes)),
                jax.ShapeDtypeStruct((size // part, part, lanes), BF16),
            )
        ]
        * 4
        + [(resident((8, width)), jax.ShapeDtypeStruct((8, width), F32))],
        (place, grad, own, far, scaled, inverse, weight, vectors, *after),
        size,
        2 * size * width * width,
    )


def output_grad_kernel(place, *refs):
    mixed, grads, out = refs[:CHUNKS], refs[CHUNKS : 2 * CHUNKS], refs[-1]
    lanes = out.shape[1]
    for step in range(out.shape[0]):
        at = slice(step * lanes, (step + 1) * lanes)
        out[place[0] ^ step] = sum(
            dot(m[:, at], g[...], (0, 0)) for m, g in zip(mixed, grads)
        ).astype(BF16)


def output_back(place, mixed, grads, ctx_size, after):
    size, width = mixed[0].shape
    shape = (ctx_size, width // ctx_size, width)
    return pl.pallas_call(
        output_grad_kernel,
        grid=(1,),
        in_specs=[SCALAR]
        + [resident((size, width))] * (2 * CHUNKS)
        + [ELSEWHERE] * len(after),
        out_specs=resident(shape),
        out_shape=jax.ShapeDtypeStruct(shape, BF16),
        compiler_params=pltpu.CompilerParams(vmem_limit_bytes=48 * MIB),
        cost_estimate=pl.CostEstimate(
            flops=2 * CHUNKS * size * width * width,
            bytes_accessed=4 * width * (width + CHUNKS * size),
            transcendentals=0,
        ),
        name="output_backward",
    )(place, *mixed, *grads, *after)


def on_device(
    sizes,
    tokens,
    segment_ids,
    project_weight,
    query_bias,
    value_bias,
    output_weight,
    output_bias,
    first_gain,
    first_shift,
    expand_weight,
    expand_bias,
    reduce_weight,
    reduce_bias,
    second_gain,
    second_shift,
    grad_out,
):
    chips = sizes["z"] * sizes["y"] * sizes["x"]
    ctx_size = sizes["x"] * sizes["c"]
    everyone = chips * sizes["c"]
    seq_count, part, width = tokens.shape
    rows_count = seq_count * part
    hidden = expand_weight.shape[1]
    share = width // everyone
    own_hidden = hidden // 2
    lanes = width // ctx_size
    place = lax.axis_index(CTX)
    core = lax.axis_index("c")
    low_core = core == 0

    def hop(array, step):
        return lax.ppermute(array, CTX, [(i, i ^ step) for i in range(ctx_size)])

    def swap(array):
        return lax.ppermute(array, "c", [(0, 1), (1, 0)])

    def chosen(array, index, axis):
        return lax.dynamic_index_in_dim(array, index, axis, keepdims=False)

    def pair(own, other, axis, low):
        return jnp.where(
            low, jnp.stack([own, other], axis=axis), jnp.stack([other, own], axis=axis)
        )

    def by_core(own, other, axis):
        return pair(own, other, axis, low_core)

    def bit_of(name, step):
        return (lax.axis_index(name) // step) % 2

    def trade(array, name, step=1):
        return lax.ppermute(array, name, [(i, i ^ step) for i in range(sizes[name])])

    def widen(array, name, axis=0, step=1):
        return pair(array, trade(array, name, step), axis, bit_of(name, step) == 0)

    def halve(array, axis, name, step=1):
        me = bit_of(name, step)
        return chosen(array, me, axis).astype(F32) + trade(
            chosen(array, 1 - me, axis), name, step
        ).astype(F32)

    z_steps = [1 << i for i in range(sizes["z"].bit_length() - 1)]

    def z_gather(array):
        for index, step in enumerate(z_steps[::-1]):
            array = widen(array, "z", index, step)
        return array

    def z_scatter(blocks, kind=BF16):
        for step in z_steps:
            blocks = blocks.reshape((blocks.shape[0] // 2, 2) + blocks.shape[1:])
            blocks = halve(blocks.astype(kind), 1, "z", step)
        return blocks[0]

    seg_parts = segment_ids.reshape(seq_count, ctx_size, part)
    seg = jnp.concatenate([chosen(seg_parts, place ^ r, 1) for r in range(ctx_size)], axis=1)
    seg_key = seg[:, :, None]
    seg_query = seg[:, None, :]

    vectors = (
        query_bias,
        value_bias,
        output_bias,
        first_gain,
        first_shift,
        reduce_bias,
        second_gain,
        second_shift,
        expand_bias,
    )
    vector_count = 8 * share + expand_bias.shape[0]
    filler = jnp.pad(jnp.stack(vectors[:8]), ((0, 8), (0, 3 * lanes - share))) + jnp.pad(
        expand_bias[None], ((8, 7), (0, 3 * lanes - expand_bias.shape[0]))
    )
    held = jnp.stack(
        [
            jnp.concatenate(
                [
                    jnp.concatenate(
                        [
                            project_weight[:, (ctx_size * j + p) * lanes :][:, :lanes]
                            for j in range(3)
                        ],
                        axis=1,
                    ),
                    filler,
                ]
            )
            for p in range(ctx_size)
        ]
    )
    held = lax.all_to_all(held, CTX, 0, 0, tiled=True)
    sent, held = lax.optimization_barrier((tokens, held))
    across = hop(sent, 2)
    gathered = (tokens, swap(sent), across, swap(across))
    mine = jnp.concatenate(
        [held[:, :share, j * lanes : (j + 1) * lanes].reshape(-1, lanes) for j in range(3)]
    )
    vector_rows = held[:, share:, :lanes].reshape(-1, lanes)
    out_pieces = jnp.concatenate(
        [output_weight[:, i * lanes : (i + 1) * lanes] for i in range(ctx_size)]
    )
    full_project = lax.all_gather(
        jnp.concatenate([widen(out_pieces, "x").reshape(-1, lanes), mine, vector_rows]),
        SEQ,
        axis=0,
    )
    packed = full_project[:, -16 * ctx_size :].reshape(everyone, 16, lanes).astype(F32)
    exp_bias = chosen(
        packed[:, 8, : expand_bias.shape[0]].reshape(chips, 2, -1), core, 1
    ).reshape(1, own_hidden)
    vectors = jnp.swapaxes(packed[:, :8, :share], 0, 1).reshape(8, width)
    full_query, full_value = vectors[0], vectors[1]
    bias_all = jnp.concatenate(
        [
            lax.dynamic_slice_in_dim(full_query, place * lanes, lanes),
            jnp.zeros((lanes,), F32),
            lax.dynamic_slice_in_dim(full_value, place * lanes, lanes),
        ]
    )[None]

    columns = expand_weight.reshape(share, chips, 2, own_hidden // chips)
    own_columns = chosen(columns, core, 2).reshape(share, own_hidden)
    far_columns = chosen(columns, 1 - core, 2).reshape(share, own_hidden)
    both = by_core(own_columns, swap(far_columns), 0)

    def in_pieces(array):
        rows_of, wide = array.shape
        return jnp.swapaxes(array.reshape(rows_of, wide // PIECE, PIECE), 0, 1).reshape(
            -1, 2 * share, PIECE
        )

    own_pieces = jnp.concatenate(
        [
            in_pieces(both.reshape(2 * share, own_hidden)),
            jnp.swapaxes(
                reduce_weight.reshape(2, 2 * share, width // PIECE, PIECE), 1, 2
            ).reshape(-1, 2 * share, PIECE),
        ]
    )
    own_pieces = hold(own_pieces, [across])
    weights = lax.all_gather(widen(own_pieces, "x"), SEQ, axis=0).reshape(
        chips, -1, 2 * share, PIECE
    )

    rows = tokens.reshape(rows_count, width)
    where = place.reshape(1).astype(jnp.int32)
    seqs = seq_count // CHUNKS
    saved, kept_rows, mixed_low, first_low, scaled_one, inverse_one = [], [], [], [], [], []
    for index in range(CHUNKS):
        at = slice(index * seqs, (index + 1) * seqs)
        *mixed, all_rows, kept = attend(
            gathered, full_project, bias_all, seg_key[at], seg_query[at], at.start, []
        )
        kept_rows.append(all_rows)
        saved.append(kept)
        if index == 0:
            out_half = unpack(full_project, share, width, mixed[:1])
            full_output = by_core(out_half, swap(out_half), 1).reshape(ctx_size, lanes, width)
        arrived = [mixed[0]] + [hop(mixed[r], r) for r in (1, 2, 3)]
        low, scaled, inverse, joined = first_norm(
            where, arrived, rows, full_output, vectors, index
        )
        mixed_low.append(joined)
        first_low.append(low)
        scaled_one.append(scaled)
        inverse_one.append(inverse)
    first_far = [swap(low) for low in first_low]
    act, slope, own_sum, far_sum = feed(first_low, first_far, weights, exp_bias)
    far_sum = swap(far_sum)

    grad_rows = grad_out.reshape(rows_count, width)
    layer_parts, grad_second, grad_reduced, second_sums = zip(
        *(
            second_norm(scaled_one[index], own_sum, far_sum, grad_rows, vectors, index)
            for index in range(CHUNKS)
        )
    )
    layer_work = jnp.concatenate(layer_parts, axis=0).reshape(tokens.shape)
    weight_grad, expand_bias_grad, own_back, far_back = feed_back(
        grad_reduced + tuple(swap(grad) for grad in grad_reduced),
        first_low + first_far,
        act,
        slope,
        weights,
    )
    weight_owned = lax.psum_scatter(
        weight_grad.reshape((-1, sizes["x"]) + weight_grad.shape[1:]),
        SEQ,
        scatter_dimension=0,
        tiled=True,
    )[0]
    far_back = swap(far_back)
    grad_hidden, grad_attended, grad_mixed, first_sums = [], [], [], []
    for index in range(CHUNKS):
        grad, low, *mixed, sums = first_back(
            where,
            grad_second[index],
            own_back,
            far_back,
            scaled_one[index],
            inverse_one[index],
            full_output,
            vectors,
            index,
            part,
            grad_mixed[0][1:2] if index else [],
        )
        grad_hidden.append(grad.reshape(seqs, part, width))
        grad_attended.append(low)
        grad_mixed.append([mixed[0]] + [hop(mixed[r], r) for r in (1, 2, 3)])
        first_sums.append(sums)
    def shared_sums(after):
        output_grad = output_back(where, mixed_low, grad_attended, ctx_size, after)
        zeros = jnp.zeros((width,), F32)
        first_total, second_total = sum(first_sums), sum(second_sums)
        grad_vectors = (
            zeros,
            zeros,
            first_total[2],
            first_total[0],
            first_total[1],
            second_total[2],
            second_total[0],
            second_total[1],
        )
        hidden_sums = expand_bias_grad.reshape(chips, 1, own_hidden // chips)
        hidden_sums = jnp.where(
            low_core,
            jnp.concatenate([hidden_sums, jnp.zeros_like(hidden_sums)], axis=1),
            jnp.concatenate([jnp.zeros_like(hidden_sums), hidden_sums], axis=1),
        )
        packed_grads = jnp.concatenate(
            [vector.reshape(everyone, share) for vector in grad_vectors]
            + [hidden_sums.reshape(everyone, -1)],
            axis=1,
        )
        packed_grads = jnp.pad(packed_grads, ((0, 0), (0, width - vector_count))).astype(BF16)
        shared = jnp.concatenate(
            [output_grad.reshape(everyone, share, width), packed_grads[:, None]], axis=1
        ).reshape(sizes["z"], 2, sizes["x"], 2, share + 1, width)
        shared_chip = halve(shared, 3, "c").astype(BF16)
        shared = halve(shared_chip, 2, "x").astype(BF16)
        return shared_chip, shared

    project_grad = []
    work_parts = []
    across_sums = []
    work_hops = []
    sum_parts = []
    for index in range(CHUNKS):
        at = slice(index * seqs, (index + 1) * seqs)
        if index == 1:
            shared_chip, shared = shared_sums(grad_mixed[1][1:] + sum_parts)
        project_part, r0, r1, r2, r3, sums = attend_back(
            saved[index],
            kept_rows[index],
            grad_mixed[index],
            full_project,
            seg_key[at],
            seg_query[at],
            project_grad,
            index == CHUNKS - 1,
            across_sums[:1] + [shared_chip] if index else grad_attended[1:],
        )
        project_grad = [project_part]
        across_sums.append(add_low(r2, swap(r3), work_hops[:1] if index else grad_mixed[1][1:]))
        work_hops.append(hop(across_sums[index], 2))
        work_parts.append(
            grad_hidden[index] + r0 + swap(r1).astype(F32) + work_hops[index].astype(F32)
        )
        sum_parts.append(sums)
    grad_work = jnp.concatenate(work_parts, axis=0)
    column_sums = jnp.sum(jnp.concatenate(sum_parts, axis=0), axis=(0, 1))
    holders = sizes["z"] * 2
    owners = holders // ctx_size
    bias_grads = jnp.concatenate(
        [
            column_sums[at : at + lanes].reshape(owners, ctx_size, share)
            for at in (0, 2 * lanes)
        ],
        axis=2,
    )
    bias_grads = jnp.pad(
        bias_grads, ((0, 0), (0, 16 - ctx_size), (0, 3 * lanes - 2 * share))
    ).astype(BF16)
    bias_grads = lax.dynamic_update_slice_in_dim(
        jnp.zeros((holders, 16, 3 * lanes), BF16), bias_grads, place * owners, 0
    )
    blocks = join(
        project_grad[0].reshape(holders, ctx_size * share, 3 * lanes),
        bias_grads,
        work_hops[:1],
    )
    blocks = halve(blocks.reshape((sizes["z"], 2) + blocks.shape[1:]), 1, "y").astype(BF16)
    blocks = hold(blocks, work_hops[1:])
    weight_owned = halve(weight_owned, 0, "x")
    shared = halve(hold(shared, [blocks, weight_owned]), 1, "y")
    shared = z_scatter(shared)
    output_owned = shared[:share]
    owned = shared[share, :vector_count]
    blocks = z_scatter(blocks)
    blocks = jnp.concatenate(
        [
            blocks[: ctx_size * share].reshape(ctx_size, share, 3 * lanes),
            jnp.pad(
                blocks[ctx_size * share :][:ctx_size, None], ((0, 0), (0, 7), (0, 0))
            ),
        ],
        axis=1,
    )
    held = lax.all_to_all(blocks, CTX, 0, 0, tiled=True)
    bias_owned = jnp.sum(held[:, share, : 2 * share], axis=0)
    project_owned = jnp.concatenate(
        [
            held[p, :share, j * lanes : (j + 1) * lanes]
            for j in range(3)
            for p in range(ctx_size)
        ],
        axis=1,
    )
    expand_pieces = own_hidden // PIECE
    far_rows = jnp.swapaxes(
        weight_owned[:expand_pieces].reshape(expand_pieces, 2, share, PIECE), 0, 1
    )
    expand_owned = by_core(
        jnp.swapaxes(chosen(far_rows, core, 0), 0, 1).reshape(share, chips, -1),
        jnp.swapaxes(swap(chosen(far_rows, 1 - core, 0)), 0, 1).reshape(share, chips, -1),
        2,
    ).reshape(share, hidden)
    reduce_owned = jnp.swapaxes(
        weight_owned[expand_pieces:].reshape(2, width // PIECE, 2 * share, PIECE), 1, 2
    ).reshape(4 * share, width)

    small = [owned[i * share : (i + 1) * share] for i in range(8)]
    return (
        layer_work,
        grad_work,
        project_owned.astype(F32),
        bias_owned[:share],
        bias_owned[share:],
        output_owned.astype(F32),
        small[2],
        small[3],
        small[4],
        expand_owned.astype(F32),
        owned[8 * share :],
        reduce_owned.astype(F32),
        small[5],
        small[6],
        small[7],
    )


def solution(mesh):
    seq_size, ctx_size = mesh.shape["seq"], mesh.shape["ctx"]
    sizes = {"z": seq_size // 2, "y": 2, "x": ctx_size // 2, "c": 2}
    fine = Mesh(mesh.devices.reshape(tuple(sizes.values())), tuple(sizes))
    rows = P(SEQ, CTX, None)
    matrix = P(ALL, None)
    vector = P(ALL)
    return jax.shard_map(
        functools.partial(on_device, sizes),
        mesh=fine,
        in_specs=(
            rows,
            P(SEQ, None),
            matrix,
            vector,
            vector,
            matrix,
            vector,
            vector,
            vector,
            matrix,
            vector,
            matrix,
            vector,
            vector,
            vector,
            rows,
        ),
        out_specs=(
            rows,
            rows,
            matrix,
            vector,
            vector,
            matrix,
            vector,
            vector,
            vector,
            matrix,
            vector,
            matrix,
            vector,
            vector,
            vector,
        ),
        check_vma=False,
    )
```
